128 devices in a mesh: dp: 2 (over core), row: 8 (over z, y_lo), col: 8 (over x, y_hi).
Axes of the slice: x: 4, y: 4 (y_hi: 2, y_lo: 2; y = y_hi * 2 + y_lo), z: 4, core: 2. Of those that a mesh axis runs over, the one named last changes fastest.
Arguments:
- images: bfloat16 [5120, 1024], P(('dp', 'col'), 'row'), may hold values from -6 to 6
- norm_gain1: float32 [2, 1024], P(None, 'row'), may hold values from 0.25 to 1.75
- norm_bias1: float32 [2, 1024], P(None, 'row'), may hold values from -4 to 4
- w_qkv: bfloat16 [2, 1024, 3, 1024], P(None, 'row', None, 'col'), may hold values from -0.1875 to 0.1875
- qv_bias: float32 [2, 2, 1024], P(None, None, 'col'), may hold values from -4 to 4
- w_out: bfloat16 [2, 1024, 1024], P(None, 'col', 'row'), may hold values from -1.5 to 1.5
- out_bias: float32 [2, 1024], P(None, 'row'), may hold values from -4 to 4
- norm_gain2: float32 [2, 1024], P(None, 'row'), may hold values from 0.25 to 1.75
- norm_bias2: float32 [2, 1024], P(None, 'row'), may hold values from -4 to 4
- w_up: bfloat16 [2, 1024, 4096], P(None, 'row', 'col'), may hold values from -0.1875 to 0.1875
- up_bias: float32 [2, 4096], P(None, 'col'), may hold values from -4 to 4
- w_down: bfloat16 [2, 4096, 1024], P(None, 'col', 'row'), may hold values from -0.09375 to 0.09375
- down_bias: float32 [2, 1024], P(None, 'row'), may hold values from -4 to 4
- cotangent: bfloat16 [5120, 1024], P(('dp', 'col'), 'row'), may hold values from -6 to 6
Outputs:
- encoded: bfloat16 [5120, 1024], P(('dp', 'col'), 'row')
- grad_input: float32 [5120, 1024], P(('dp', 'col'), 'row')
- grad_qkv: float32 [2, 1024, 3, 1024], P(None, 'row', None, 'col')
- grad_out_proj: float32 [2, 1024, 1024], P(None, 'col', 'row')
- grad_up: float32 [2, 1024, 4096], P(None, 'row', 'col')
- grad_down: float32 [2, 4096, 1024], P(None, 'col', 'row')
- grad_gain1: float32 [2, 1024], P(None, 'row')
- grad_bias1: float32 [2, 1024], P(None, 'row')
- grad_qv_bias: float32 [2, 2, 1024], P(None, None, 'col')
- grad_out_bias: float32 [2, 1024], P(None, 'row')
- grad_gain2: float32 [2, 1024], P(None, 'row')
- grad_bias2: float32 [2, 1024], P(None, 'row')
- grad_up_bias: float32 [2, 4096], P(None, 'col')
- grad_down_bias: float32 [2, 1024], P(None, 'row')
The draws below stay inside these ranges and needn't reach their ends.
All inputs are finite; a program needn't handle non-finite values.
Results may differ from the reference program's by a relative error of at most 0.038.
Values may be sent and summed in bfloat16 or wider, within the bound.
A program may use at most 128 MiB of HBM per device.

```python
import jax
import jax.numpy as jnp
from jax import lax

D = 1024
HEADS = 16
F = 4096
SEQ = 320
LAYERS = 2
HEAD_DIM = 64
TOKENS = 5120


def block_levels(key, dims, cuts, smallest, high):
    loudness = 1.0
    for axis_at, blocks in cuts:
        steps = jax.random.uniform(jax.random.fold_in(jax.random.fold_in(key, 6), axis_at), (blocks,), jnp.float32, smallest / len(cuts), high / len(cuts))
        loudness = loudness * jnp.repeat(jnp.exp(steps), dims[axis_at] // blocks).reshape((-1,) + (1,) * (len(dims) - 1 - axis_at))
    return loudness


def centred(stream_key, shape, scale, bound, split=(), held_as=jnp.bfloat16):
    drawn = scale * jax.random.normal(stream_key, shape, jnp.float32)
    if split:
        drawn = drawn * block_levels(stream_key, shape, split, -0.22, 0.18)
    return jnp.clip(drawn, -bound, bound).astype(held_as)


def setup_inputs(seed: int = 0) -> dict:
    splits = jax.random.split(jax.random.key(seed), 15)
    return {
        "images": centred(splits[0], (TOKENS, D), 1.0, 6.0, ((0, 16), (1, 8))),
        "norm_gain1": jnp.clip(1.0 + 0.15 * jax.random.normal(splits[1], (LAYERS, D), jnp.float32), 0.25, 1.75),
        "norm_bias1": centred(splits[2], (LAYERS, D), 0.3, 4.0, ((1, 8),), jnp.float32),
        "w_qkv": centred(splits[3], (LAYERS, D, 3, D), D ** -0.5, 0.1875, ((1, 8), (3, 8))),
        "qv_bias": centred(splits[4], (LAYERS, 2, D), 0.3, 4.0, ((2, 8),), jnp.float32),
        "w_out": centred(splits[5], (LAYERS, D, D), (D // 64) ** -0.5, 1.5, ((1, 8), (2, 8))),
        "out_bias": centred(splits[6], (LAYERS, D), 0.3, 4.0, ((1, 8),), jnp.float32),
        "norm_gain2": jnp.clip(1.0 + 0.15 * jax.random.normal(splits[7], (LAYERS, D), jnp.float32), 0.25, 1.75),
        "norm_bias2": centred(splits[8], (LAYERS, D), 0.3, 4.0, ((1, 8),), jnp.float32),
        "w_up": centred(splits[9], (LAYERS, D, F), D ** -0.5, 0.1875, ((1, 8), (2, 8))),
        "up_bias": centred(splits[10], (LAYERS, F), 0.3, 4.0, ((1, 8),), jnp.float32),
        "w_down": centred(splits[11], (LAYERS, F, D), F ** -0.5, 0.09375, ((1, 8), (2, 8))),
        "down_bias": centred(splits[12], (LAYERS, D), 0.3, 4.0, ((1, 8),), jnp.float32),
        "cotangent": centred(splits[13], (TOKENS, D), 1.0, 6.0, ((0, 16), (1, 8))),
    }


@jax.custom_vjp
def low(v):
    return lax.optimization_barrier(v.astype(jnp.bfloat16)).astype(jnp.float32)

@jax.custom_vjp
def low_back(v):
    return v

def low_keep(v):
    return (low(v), None)

def low_pass(kept, grad):
    return (grad,)

def back_keep(v):
    return (v, None)

def back_low(kept, grad):
    return (low(grad),)
low.defvjp(low_keep, low_pass)
low_back.defvjp(back_keep, back_low)
norm_eps = 1e-06

def matmul(left, right):
    return jnp.dot(left, right, precision=lax.Precision.HIGHEST)

def layer_norm(resid, norm_gain, norm_shift):
    center = lax.optimization_barrier(jnp.mean(resid, axis=-1, keepdims=True))
    spread = lax.optimization_barrier(jnp.mean(jnp.square(resid - center), axis=-1, keepdims=True))
    return (resid - center) * lax.rsqrt(spread + norm_eps) * norm_gain + norm_shift

def attend(triple):
    query, keys, values = triple
    scores = low_back(jnp.einsum('qhd,khd->hqk', query, keys, precision=lax.Precision.HIGHEST) * HEAD_DIM ** (-0.5))
    largest = lax.optimization_barrier(jnp.max(scores, axis=-1, keepdims=True))
    raised = jnp.exp(scores - largest)
    shares = raised / lax.optimization_barrier(jnp.sum(raised, axis=-1, keepdims=True))
    return jnp.einsum('hqk,khd->qhd', low(shares), values, precision=lax.Precision.HIGHEST)

def layer(resid, weights):
    gain_one, shift_one, qkv_weight, qv_shift, out_weight, out_shift, gain_two, shift_two, up_weight, up_shift, down_weight, down_shift = weights
    normed = low(layer_norm(resid, gain_one, shift_one))
    query = low(low_back(matmul(normed, qkv_weight[:, 0]) + qv_shift[0]))
    keys = low(low_back(matmul(normed, qkv_weight[:, 1])))
    values = low(low_back(matmul(normed, qkv_weight[:, 2]) + qv_shift[1]))
    head_shape = (-1, SEQ, HEADS, HEAD_DIM)
    mixed = lax.map(jax.checkpoint(attend), (query.reshape(head_shape), keys.reshape(head_shape), values.reshape(head_shape)))
    mixed = low(low_back(mixed.reshape(-1, D)))
    middle = resid + low_back(matmul(mixed, out_weight) + out_shift)
    normed_two = low(layer_norm(middle, gain_two, shift_two))
    before = low_back(matmul(normed_two, up_weight) + up_shift)
    hidden = low(jax.nn.gelu(before, approximate=False))
    return middle + low_back(matmul(hidden, down_weight) + down_shift)

def reference(images, norm_gain1, norm_bias1, w_qkv, qv_bias, w_out, out_bias, norm_gain2, norm_bias2, w_up, up_bias, w_down, down_bias, cotangent):
    params = tuple((array_in.astype(jnp.float32) for array_in in (norm_gain1, norm_bias1, w_qkv, qv_bias, w_out, out_bias, norm_gain2, norm_bias2, w_up, up_bias, w_down, down_bias)))

    def forward(resid, weights):
        for layer_index in range(LAYERS):
            resid = layer(resid, tuple((array_in[layer_index] for array_in in weights)))
        return resid

    def group(totals, paired):
        inputs, upstream = paired
        result, pullback = jax.vjp(forward, inputs, params)
        input_grad, param_grads = pullback(upstream)
        return (jax.tree.map(jnp.add, totals, param_grads), (result.astype(jnp.bfloat16), input_grad))
    group_width = 4 * SEQ
    grouped = images.astype(jnp.float32).reshape(-1, group_width, D)
    upstreams = cotangent.astype(jnp.float32).reshape(-1, group_width, D)
    totals, (encoded, grad_input) = lax.scan(group, jax.tree.map(jnp.zeros_like, params), (grouped, upstreams))
    return (encoded.reshape(-1, D), grad_input.reshape(-1, D), totals[2], totals[4], totals[8], totals[10], totals[0], totals[1], totals[3], totals[5], totals[6], totals[7], totals[9], totals[11])
```

```python
import functools

import jax
import jax.numpy as jnp
from jax import lax
from jax.experimental import pallas as pl
from jax.experimental.pallas import tpu as pltpu
from jax.sharding import PartitionSpec as P

BF = jnp.bfloat16
F32 = jnp.float32
LAYERS = 2
GROUP = 8
TOK = 40
SEQ = 320
D = 1024
HALF = 512
HEAD_DIM = 64
EPS = 1e-6
ROOT_HALF = 0.7071067811865476
INV_ROOT_TAU = 0.3989422804014327
MESH = pl.DeviceIdType.MESH


def dot(a, b):
    return jnp.dot(a, b, preferred_element_type=F32)


def dot_last(a, b):
    return lax.dot_general(a, b, (((1,), (1,)), ((), ())), preferred_element_type=F32)


def dot_first(a, b):
    return lax.dot_general(a, b, (((0,), (0,)), ((), ())), preferred_element_type=F32)


def lanes(parts):
    return jnp.concatenate(parts, axis=1)


def kernel(
    images, gain1, bias1, wqkv, qvb, wout, outb, gain2, bias2, wup, upb, wdown, downb, cot,
    enc_o, gin_o, gqkv_o, gout_o, gup_o, gdown_o, gg1_o, gb1_o, gqv_o, gob_o, gg2_o, gb2_o, gub_o, gdb_o,
    in_f, in_r, out_f, out_r,
    vec_s, vec_g, wq_g, wo_g, wu_g, wd_g,
    ag, rs_s, rs_r,
    gq_s, go_s, gu_s, gd_s, gq_r, go_r, gu_r, gd_r, sq, so, su, sd, tq, to, tu, td,
    stream, normal_k, scale_k, prob_k, qkv_k, mixed_k, hidden_k, slope_k, grad_k,
    vacc, vcol, vs_s, vs_r, vb_s, vb_r, vt_s, vt_r, vfin,
    in_ss, in_rs, out_ss, out_rs, vec_sem, w_ss, w_rs, ag_ss, ag_rs, rs_ss, rs_rs, g_ss, g_rs, x_ss, x_rs, v_ss, v_rs,
):
    core = lax.axis_index("dp")
    row = lax.axis_index("row")
    col = lax.axis_index("col")
    x = lax.div(col, 2)
    yh = lax.rem(col, 2)
    t = 2 * x + core

    def group_dev(j):
        return (lax.rem(j, 2), row, 2 * lax.div(j, 2) + yh)

    def plane_dev(r):
        return (yh, r, 2 * x + core)

    def push(src, dst, ssem, rsem, dev):
        pltpu.make_async_remote_copy(
            src_ref=src, dst_ref=dst, send_sem=ssem, recv_sem=rsem, device_id=dev, device_id_type=MESH
        ).start()

    def drain(ref, sem):
        pltpu.make_async_copy(ref, ref, sem).wait()

    def fan(me, own, src, dst, ssem, rsem, dev):
        @pl.when(own)
        def _():
            pltpu.make_async_copy(src(me), dst, rsem).start()

        @pl.when(jnp.logical_not(own))
        def _():
            push(src(me), dst, ssem, rsem, dev(me))

        @pl.loop(1, GROUP)
        def _(k):
            j = lax.rem(me + k, GROUP)
            push(src(j), dst, ssem, rsem, dev(j))

    def fan_sent(own, ref, ssem):
        @pl.when(own)
        def _():
            drain(ref.at[pl.ds(0, GROUP - 1)], ssem)

        @pl.when(jnp.logical_not(own))
        def _():
            drain(ref, ssem)

    own_plane = yh == core
    own_tile = jnp.logical_and(row == col, yh == core)

    in_f[0] = images[...].astype(F32).reshape(GROUP, TOK, 128)
    in_f[1] = cot[...].astype(F32).reshape(GROUP, TOK, 128)

    def tile_dev(j):
        return (lax.rem(j, 2), col, 2 * lax.div(j, 2) + core)

    def tiles_in(n):
        fan(t, own_tile, lambda j: in_f.at[n, j], in_r.at[n, row], in_ss.at[n], in_rs.at[n], tile_dev)

    tiles_in(0)

    vec_s[...] = jnp.zeros_like(vec_s)
    for l in range(LAYERS):
        for i, ref in enumerate((gain1, bias1, outb, gain2, bias2, downb)):
            vec_s[l, i : i + 1, :] = ref[l : l + 1, :]
        vec_s[2 + l, 0:2, :] = qvb[l]
        for j in range(4):
            vec_s[2 + l, 2 + j : 3 + j, :] = upb[l : l + 1, 128 * j : 128 * j + 128]
    fan(row, own_plane, lambda j: vec_s, vec_g.at[row], vec_sem.at[0], vec_sem.at[1], plane_dev)

    weights = ((wqkv, wq_g), (wout, wo_g), (wup, wu_g), (wdown, wd_g))

    def weights_in(l):
        for m, (src, dst) in enumerate(weights):
            fan(row, own_plane, lambda j, src=src: src.at[l], dst.at[l, row], w_ss.at[l, m], w_rs.at[l, m], plane_dev)

    def weight_wait(l, m):
        drain(weights[m][1].at[l], w_rs.at[l, m])

    weights_in(0)
    tiles_in(1)

    def gather_start(l, s, value):
        folded = jnp.concatenate([value[:, :HALF], value[:, HALF:]], axis=0).astype(BF)
        ag[l, s, t] = folded

        @pl.loop(1, GROUP)
        def _(k):
            j = lax.rem(t + k, GROUP)
            push(ag.at[l, s, t], ag.at[l, s, t], ag_ss.at[l, s], ag_rs.at[l, s], group_dev(j))

    def gather_wait(l, s):
        drain(ag.at[l, s, pl.ds(0, GROUP - 1)], ag_rs.at[l, s])

    def gather_read(l, s):
        whole = ag[l, s].astype(F32)
        left = whole[:, :TOK].reshape(SEQ, HALF).astype(BF)
        right = whole[:, TOK:].reshape(SEQ, HALF).astype(BF)
        return left, right

    def scatter_start(l, s, left, right):
        both = jnp.concatenate([left.reshape(GROUP, TOK, HALF), right.reshape(GROUP, TOK, HALF)], axis=1)
        rs_s[l, s] = both.astype(BF)
        rs_r[l, s, t] = rs_s[l, s, t]

        @pl.loop(1, GROUP)
        def _(k):
            j = lax.rem(t + k, GROUP)
            push(rs_s.at[l, s, j], rs_r.at[l, s, t], rs_ss.at[l, s], rs_rs.at[l, s], group_dev(j))

    def scatter_wait(l, s):
        drain(rs_r.at[l, s, pl.ds(0, GROUP - 1)], rs_rs.at[l, s])
        total = jnp.sum(rs_r[l, s].astype(F32), axis=0)
        return lanes([total[:TOK], total[TOK:]])

    def vec_row(l, i):
        return lanes([vec_g[r, l, i : i + 1, :] for r in range(GROUP)])

    def norm_forward(l, s, value):
        center = jnp.mean(value, axis=1, keepdims=True)
        shifted = value - center
        scaled = lax.rsqrt(jnp.mean(shifted * shifted, axis=1, keepdims=True) + EPS)
        normal = shifted * scaled
        normal_k[l, s] = normal
        scale_k[l, s] = jnp.broadcast_to(scaled, (TOK, 128))
        return normal * vec_row(l, 3 * s) + vec_row(l, 3 * s + 1)

    def norm_backward(l, s, grad_out):
        normal = normal_k[l, s]
        scaled = scale_k[l, s][:, 0:1]
        vacc[l, 3 * s : 3 * s + 1, :] = jnp.sum(grad_out * normal, axis=0, keepdims=True)
        vacc[l, 3 * s + 1 : 3 * s + 2, :] = jnp.sum(grad_out, axis=0, keepdims=True)
        upstream = grad_out * vec_row(l, 3 * s)
        mean_part = jnp.mean(upstream, axis=1, keepdims=True)
        proj_part = jnp.mean(upstream * normal, axis=1, keepdims=True)
        return scaled * (upstream - mean_part - normal * proj_part)

    def qkv_half(l, h):
        return wq_g[l, 4 * h : 4 * h + 4].reshape(HALF, 384)

    def out_half(l, h):
        return lanes([wo_g[l, 4 * h + r] for r in range(4)])

    def up_half(l, h):
        return wu_g[l, 4 * h : 4 * h + 4].reshape(HALF, 512)

    def down_half(l, h):
        return lanes([wd_g[l, 4 * h + r] for r in range(4)])

    def head_mask(h):
        lane = lax.broadcasted_iota(jnp.int32, (SEQ, 128), 1)
        return (lane < HEAD_DIM) if h == 0 else (lane >= HEAD_DIM)

    def pick(pair):
        return jnp.where(head_mask(0), pair[0], pair[1])

    def only(h, value):
        return jnp.where(head_mask(h), value, jnp.zeros_like(value))

    drain(in_r.at[0], in_rs.at[0])
    drain(vec_g, vec_sem.at[1])
    stream[...] = lanes([in_r[0, r] for r in range(GROUP)])

    @pl.loop(0, LAYERS)
    def _(l):
        gather_start(l, 0, norm_forward(l, 0, stream[...]))

        @pl.when(l == 0)
        def _():
            weights_in(1)

        weight_wait(l, 0)
        gather_wait(l, 0)
        left, right = gather_read(l, 0)
        projected = dot(left, qkv_half(l, 0)) + dot(right, qkv_half(l, 1))
        shift = vec_g[0, 2 + l]
        query = (projected[:, :128] + shift[0:1]).astype(BF)
        keys = projected[:, 128:256].astype(BF)
        values = (projected[:, 256:] + shift[1:2]).astype(BF)
        qkv_k[l, 0] = query
        qkv_k[l, 1] = keys
        qkv_k[l, 2] = values
        mixed = []
        for h in range(2):
            scores = dot_last(only(h, query), keys) * HEAD_DIM ** -0.5
            raised = jnp.exp(scores - jnp.max(scores, axis=1, keepdims=True))
            probs = raised / jnp.sum(raised, axis=1, keepdims=True)
            prob_k[l, h] = probs
            mixed.append(dot(probs.astype(BF), values))
        mixed = pick(mixed).astype(BF)
        mixed_k[l] = mixed
        weight_wait(l, 1)
        scatter_start(l, 0, dot(mixed, out_half(l, 0)), dot(mixed, out_half(l, 1)))
        base = stream[...] + vec_row(l, 2)
        middle = base + scatter_wait(l, 0)
        stream[...] = middle
        gather_start(l, 1, norm_forward(l, 1, middle))
        weight_wait(l, 2)
        gather_wait(l, 1)
        left, right = gather_read(l, 1)
        before = dot(left, up_half(l, 0)) + dot(right, up_half(l, 1))
        shift = vec_g[0, 2 + l]
        before = before + lanes([shift[2 + j : 3 + j] for j in range(4)])
        phi = 0.5 * (1.0 + lax.erf(before * ROOT_HALF))
        hidden = (before * phi).astype(BF)
        hidden_k[l] = hidden
        weight_wait(l, 3)
        scatter_start(l, 1, dot(hidden, down_half(l, 0)), dot(hidden, down_half(l, 1)))
        slope_k[l] = phi + before * INV_ROOT_TAU * jnp.exp(-0.5 * before * before)
        base = stream[...] + vec_row(l, 5)
        stream[...] = base + scatter_wait(l, 1)

    def back_dev(r):
        return (yh, r, row)

    def tiles_out(n, value):
        for r in range(GROUP):
            out_f[n, r] = value[:, 128 * r : 128 * r + 128]
        fan(row, own_tile, lambda j: out_f.at[n, j], out_r.at[n, t], out_ss.at[n], out_rs.at[n], back_dev)

    tiles_out(0, stream[...])

    drain(in_r.at[1], in_rs.at[1])
    grad_k[...] = lanes([in_r[1, r] for r in range(GROUP)])
    vacc[...] = jnp.zeros_like(vacc)
    vcol[...] = jnp.zeros_like(vcol)

    grads = ((gq_s, gq_r, sq, tq), (go_s, go_r, so, to), (gu_s, gu_r, su, tu), (gd_s, gd_r, sd, td))

    def grads_out(l, m):
        src, dst = grads[m][:2]
        fan(row, own_plane, lambda j: src.at[l, j], dst.at[l, row], g_ss.at[l, m], g_rs.at[l, m], plane_dev)

    @pl.loop(0, LAYERS)
    def _(step):
        l = LAYERS - 1 - step
        branch2 = grad_k[...]
        gather_start(l, 2, branch2)
        vacc[l, 5:6, :] = jnp.sum(branch2.astype(BF).astype(F32), axis=0, keepdims=True)
        gather_wait(l, 2)
        left, right = gather_read(l, 2)
        hidden_grad = dot_last(left, down_half(l, 0)) + dot_last(right, down_half(l, 1))
        before_grad = (hidden_grad * slope_k[l]).astype(BF)
        scatter_start(l, 2, dot_last(before_grad, up_half(l, 0)), dot_last(before_grad, up_half(l, 1)))
        sums = jnp.sum(before_grad.astype(F32), axis=0, keepdims=True)
        for j in range(4):
            vcol[l, 2 + j : 3 + j, :] = sums[:, 128 * j : 128 * j + 128]
        for h, part in enumerate((left, right)):
            product = dot_first(hidden_k[l], part).astype(BF)
            for r in range(4):
                gd_s[l, 4 * h + r] = product[:, 128 * r : 128 * r + 128]
        grads_out(l, 3)
        for h, part in enumerate(gather_read(l, 1)):
            gu_s[l, 4 * h : 4 * h + 4] = dot_first(part, before_grad).astype(BF).reshape(4, 128, 512)
        grads_out(l, 2)
        grad_mid = grad_k[...] + norm_backward(l, 1, scatter_wait(l, 2))
        grad_k[...] = grad_mid
        gather_start(l, 3, grad_mid)
        vacc[l, 2:3, :] = jnp.sum(grad_mid.astype(BF).astype(F32), axis=0, keepdims=True)
        gather_wait(l, 3)
        left, right = gather_read(l, 3)
        mixed_grad = (dot_last(left, out_half(l, 0)) + dot_last(right, out_half(l, 1))).astype(BF)
        query = qkv_k[l, 0]
        keys = qkv_k[l, 1]
        values = qkv_k[l, 2]
        value_grads, query_grads, key_grads = [], [], []
        for h in range(2):
            probs = prob_k[l, h]
            probs_grad = dot_last(only(h, mixed_grad), values)
            inner = jnp.sum(probs * probs_grad, axis=1, keepdims=True)
            scores_grad = (probs * (probs_grad - inner)).astype(BF)
            value_grads.append(dot_first(probs.astype(BF), mixed_grad))
            query_grads.append(dot(scores_grad, keys))
            key_grads.append(dot_first(scores_grad, query))
        query_grad = (pick(query_grads) * HEAD_DIM ** -0.5).astype(BF)
        keys_grad = (pick(key_grads) * HEAD_DIM ** -0.5).astype(BF)
        values_grad = pick(value_grads).astype(BF)
        joined = lanes([query_grad, keys_grad, values_grad])
        scatter_start(l, 3, dot_last(joined, qkv_half(l, 0)), dot_last(joined, qkv_half(l, 1)))
        vcol[l, 0:1, :] = jnp.sum(query_grad.astype(F32), axis=0, keepdims=True)
        vcol[l, 1:2, :] = jnp.sum(values_grad.astype(F32), axis=0, keepdims=True)
        for h, part in enumerate(gather_read(l, 0)):
            gq_s[l, 4 * h : 4 * h + 4] = dot_first(part, joined).astype(BF).reshape(4, 128, 384)
        grads_out(l, 0)
        for h, part in enumerate((left, right)):
            product = dot_first(mixed_k[l], part).astype(BF)
            for r in range(4):
                go_s[l, 4 * h + r] = product[:, 128 * r : 128 * r + 128]
        grads_out(l, 1)
        grad_k[...] = grad_k[...] + norm_backward(l, 0, scatter_wait(l, 3))

    tiles_out(1, grad_k[...])

    for j in range(GROUP):
        vs_s[j] = vacc[:, :, 128 * j : 128 * j + 128]
    vs_r[t] = vs_s[t]

    @pl.loop(1, GROUP)
    def _(k):
        j = lax.rem(t + k, GROUP)
        push(vs_s.at[j], vs_r.at[t], v_ss.at[0], v_rs.at[0], group_dev(j))

    sibling = (1 - core, row, col)

    def sum_terms(l):
        for m in (3, 2, 1, 0):
            src, dst, part, other = grads[m]
            drain(dst.at[l], g_rs.at[l, m])
            total = dst[l, 0].astype(F32)
            for r in range(1, GROUP):
                total += dst[l, r].astype(F32)
            part[l] = total
            push(part.at[l], other.at[l], x_ss.at[l, m], x_rs.at[l, m], sibling)

    sum_terms(1)

    drain(vs_r.at[pl.ds(0, GROUP - 1)], v_rs.at[0])
    vb_s[0:2] = jnp.sum(vs_r[...], axis=0)
    vb_s[2:4] = vcol[...]
    fan(row, own_plane, lambda j: vb_s, vb_r.at[row], v_ss.at[1], v_rs.at[1], plane_dev)

    drain(out_r.at[0], out_rs.at[0])
    enc_o[...] = out_r[0].reshape(SEQ, 128).astype(BF)

    drain(vb_r, v_rs.at[1])
    vt_s[...] = jnp.sum(vb_r[...], axis=0)
    push(vt_s, vt_r, v_ss.at[2], v_rs.at[2], sibling)

    sum_terms(0)

    drain(vt_r, v_rs.at[2])
    vt_s_total = vt_s[...] + vt_r[...]

    @pl.when(row == col)
    def _():
        vfin[...] = vt_s_total[0:2]

        @pl.loop(1, GROUP)
        def _(k):
            push(vfin, vfin, v_ss.at[3], v_rs.at[3], (core, row, lax.rem(col + k, GROUP)))

    for l in range(LAYERS):
        gqv_o[l] = vt_s_total[2 + l, 0:2]
        for j in range(4):
            gub_o[l : l + 1, 128 * j : 128 * j + 128] = vt_s_total[2 + l, 2 + j : 3 + j]

    drain(out_r.at[1], out_rs.at[1])
    gin_o[...] = out_r[1].reshape(SEQ, 128)

    @pl.when(row != col)
    def _():
        drain(vfin, v_rs.at[3])

    for l in range(LAYERS):
        for i, ref in enumerate((gg1_o, gb1_o, gob_o, gg2_o, gb2_o, gdb_o)):
            ref[l : l + 1, :] = vfin[l, i : i + 1, :]

    for l in (1, 0):
        for m, ref in ((3, gdown_o), (2, gup_o), (1, gout_o), (0, gqkv_o)):
            part, other = grads[m][2:]
            drain(other.at[l], x_rs.at[l, m])
            ref[l] = part[l] + other[l]

    for n in range(2):
        fan_sent(own_tile, in_f.at[n], in_ss.at[n])
        fan_sent(own_tile, out_f.at[n], out_ss.at[n])
    fan_sent(own_plane, vec_g, vec_sem.at[0])
    fan_sent(own_plane, vb_r, v_ss.at[1])
    drain(vs_s.at[pl.ds(0, GROUP - 1)], v_ss.at[0])
    drain(vt_s, v_ss.at[2])

    @pl.when(row == col)
    def _():
        drain(vs_r.at[pl.ds(0, GROUP - 1)], v_ss.at[3])

    @pl.loop(0, LAYERS)
    def _(l):
        for m in range(4):
            fan_sent(own_plane, weights[m][1].at[l], w_ss.at[l, m])
            fan_sent(own_plane, grads[m][0].at[l], g_ss.at[l, m])
            drain(grads[m][2].at[l], x_ss.at[l, m])
        for s in range(4):
            drain(ag.at[l, s, pl.ds(0, GROUP - 1)], ag_ss.at[l, s])
            drain(rs_s.at[l, s, pl.ds(0, GROUP - 1)], rs_ss.at[l, s])


def on_device(images, gain1, bias1, wqkv, qvb, wout, outb, gain2, bias2, wup, upb, wdown, downb, cot):
    L = LAYERS
    wqkv = wqkv.reshape(L, 128, 384)
    vmem = pl.BlockSpec(memory_space=pltpu.VMEM)
    shape = jax.ShapeDtypeStruct
    dma = pltpu.SemaphoreType.DMA
    V = pltpu.VMEM
    results = pl.pallas_call(
        kernel,
        out_shape=(
            shape((SEQ, 128), BF),
            shape((SEQ, 128), F32),
            shape((L, 128, 384), F32),
            shape((L, 128, 128), F32),
            shape((L, 128, 512), F32),
            shape((L, 512, 128), F32),
            shape((L, 128), F32),
            shape((L, 128), F32),
            shape((L, 2, 128), F32),
            shape((L, 128), F32),
            shape((L, 128), F32),
            shape((L, 128), F32),
            shape((L, 512), F32),
            shape((L, 128), F32),
        ),
        in_specs=[vmem] * 14,
        out_specs=(vmem,) * 14,
        scratch_shapes=[
            V((2, 8, TOK, 128), F32), V((2, 8, TOK, 128), F32), V((2, 8, TOK, 128), F32), V((2, 8, TOK, 128), F32),
            V((4, 8, 128), F32), V((8, 4, 8, 128), F32),
            V((L, 8, 128, 384), BF), V((L, 8, 128, 128), BF), V((L, 8, 128, 512), BF), V((L, 8, 512, 128), BF),
            V((L, 4, 8, 2 * TOK, HALF), BF), V((L, 4, 8, 2 * TOK, HALF), BF), V((L, 4, 8, 2 * TOK, HALF), BF),
            V((L, 8, 128, 384), BF), V((L, 8, 128, 128), BF), V((L, 8, 128, 512), BF), V((L, 8, 512, 128), BF),
            V((L, 8, 128, 384), BF), V((L, 8, 128, 128), BF), V((L, 8, 128, 512), BF), V((L, 8, 512, 128), BF),
            V((L, 128, 384), F32), V((L, 128, 128), F32), V((L, 128, 512), F32), V((L, 512, 128), F32),
            V((L, 128, 384), F32), V((L, 128, 128), F32), V((L, 128, 512), F32), V((L, 512, 128), F32),
            V((TOK, D), F32), V((L, 2, TOK, D), F32), V((L, 2, TOK, 128), F32), V((L, 2, SEQ, SEQ), F32),
            V((L, 3, SEQ, 128), BF), V((L, SEQ, 128), BF), V((L, SEQ, 512), BF), V((L, SEQ, 512), F32),
            V((TOK, D), F32),
            V((L, 8, D), F32), V((L, 8, 128), F32),
            V((8, L, 8, 128), F32), V((8, L, 8, 128), F32),
            V((4, 8, 128), F32), V((8, 4, 8, 128), F32),
            V((4, 8, 128), F32), V((4, 8, 128), F32), V((L, 8, 128), F32),
            dma((2,)), dma((2,)), dma((2,)), dma((2,)), dma((2,)),
            dma((L, 4)), dma((L, 4)), dma((L, 4)), dma((L, 4)), dma((L, 4)), dma((L, 4)),
            dma((L, 4)), dma((L, 4)), dma((L, 4)), dma((L, 4)), dma((4,)), dma((4,)),
        ],
        compiler_params=pltpu.CompilerParams(has_side_effects=True, vmem_limit_bytes=60 * 1024 * 1024),
        cost_estimate=pl.CostEstimate(flops=6 * 10**9, bytes_accessed=5 * 10**6, transcendentals=10**6),
    )(images, gain1, bias1, wqkv, qvb, wout, outb, gain2, bias2, wup, upb, wdown, downb, cot)
    results = list(results)
    results[2] = results[2].reshape(L, 128, 3, 128)
    return tuple(results)


def solution(mesh):
    return jax.shard_map(
        on_device,
        mesh=mesh,
        in_specs=(
            P(("dp", "col"), "row"),
            P(None, "row"),
            P(None, "row"),
            P(None, "row", None, "col"),
            P(None, None, "col"),
            P(None, "col", "row"),
            P(None, "row"),
            P(None, "row"),
            P(None, "row"),
            P(None, "row", "col"),
            P(None, "col"),
            P(None, "col", "row"),
            P(None, "row"),
            P(("dp", "col"), "row"),
        ),
        out_specs=(
            P(("dp", "col"), "row"),
            P(("dp", "col"), "row"),
            P(None, "row", None, "col"),
            P(None, "col", "row"),
            P(None, "row", "col"),
            P(None, "col", "row"),
            P(None, "row"),
            P(None, "row"),
            P(None, None, "col"),
            P(None, "row"),
            P(None, "row"),
            P(None, "row"),
            P(None, "col"),
            P(None, "row"),
        ),
        check_vma=False,
    )
```

```python
import functools

import jax
import jax.numpy as jnp
from jax import lax
from jax.experimental import pallas as pl
from jax.experimental.pallas import tpu as pltpu
from jax.sharding import PartitionSpec as P

BF = jnp.bfloat16
F32 = jnp.float32
LAYERS = 2
GROUP = 8
TOK = 40
SEQ = 320
D = 1024
HALF = 512
HEAD_DIM = 64
EPS = 1e-6
ROOT_HALF = 0.7071067811865476
INV_ROOT_TAU = 0.3989422804014327
MESH = pl.DeviceIdType.MESH


def dot(a, b):
    return jnp.dot(a, b, preferred_element_type=F32)


def dot_last(a, b):
    return lax.dot_general(a, b, (((1,), (1,)), ((), ())), preferred_element_type=F32)


def dot_first(a, b):
    return lax.dot_general(a, b, (((0,), (0,)), ((), ())), preferred_element_type=F32)


def lanes(parts):
    return jnp.concatenate(parts, axis=1)


def kernel(
    images_h, gain1_h, bias1_h, wqkv, qvb_h, wout, outb_h, gain2_h, bias2_h, wup, upb_h, wdown, downb_h, cot_h,
    enc_h, gin_h, gqkv_h, gout_h, gup_h, gdown_h, gg1_h, gb1_h, gqv_h, gob_h, gg2_h, gb2_h, gub_h, gdb_h,
    images, gain1, bias1, qvb, outb, gain2, bias2, upb, downb, cot,
    enc_o, gin_o, gqkv_o, gout_o, gup_o, gdown_o, gg1_o, gb1_o, gqv_o, gob_o, gg2_o, gb2_o, gub_o, gdb_o,
    in_f, in_r, out_f, out_r,
    vec_s, vec_g, wq_g, wo_g, wu_g, wd_g,
    ag, rs_s, rs_b, rs_c, rs_r,
    gq_s, go_s, gu_s, gd_s, gq_r, go_r, gu_r, gd_r, sq, so, su, sd, tq, to, tu, td,
    stream, normal_k, scale_k, prob_k, qkv_k, mixed_k, hidden_k, slope_k, grad_k,
    vacc, vcol, vs_s, vs_r, vh_r, vb_r, vt_s, vt_r,
    op_sem, res_sem, in_ss, in_rs, out_ss, out_rs, vec_sem, w_ss, w_rs,
    ag_ss, ag_rs, ag_fs, rs_bs, rs_br, rs_ss, rs_rs, g_ss, g_rs, x_ss, x_rs, v_ss, v_rs,
):
    core = lax.axis_index("dp")
    row = lax.axis_index("row")
    col = lax.axis_index("col")
    x = lax.div(col, 2)
    yh = lax.rem(col, 2)
    t = 2 * x + core
    u = 4 * core + x
    sibling = (1 - core, row, col)

    def chip_dev(c):
        return (core, row, 2 * c + yh)

    def plane_dev(r):
        return (yh, r, 2 * x + core)

    def push(src, dst, ssem, rsem, dev):
        pltpu.make_async_remote_copy(
            src_ref=src, dst_ref=dst, send_sem=ssem, recv_sem=rsem, device_id=dev, device_id_type=MESH
        ).start()

    def drain(ref, sem):
        pltpu.make_async_copy(ref, ref, sem).wait()

    def fan(me, own, src, dst, ssem, rsem, dev):
        @pl.when(own)
        def _():
            pltpu.make_async_copy(src(me), dst, rsem).start()

        @pl.when(jnp.logical_not(own))
        def _():
            push(src(me), dst, ssem, rsem, dev(me))

        @pl.loop(1, GROUP)
        def _(k):
            j = lax.rem(me + k, GROUP)
            push(src(j), dst, ssem, rsem, dev(j))

    def fan_sent(own, ref, ssem):
        @pl.when(own)
        def _():
            drain(ref.at[pl.ds(0, GROUP - 1)], ssem)

        @pl.when(jnp.logical_not(own))
        def _():
            drain(ref, ssem)

    own_plane = yh == core
    own_tile = row == t

    small = (
        (images_h, images), (gain1_h, gain1), (bias1_h, bias1), (outb_h, outb), (gain2_h, gain2), (bias2_h, bias2),
        (downb_h, downb), (qvb_h, qvb), (upb_h, upb), (cot_h, cot),
    )
    fetches = [pltpu.make_async_copy(src, dst, op_sem.at[n]) for n, (src, dst) in enumerate(small)]
    for fetch in fetches:
        fetch.start()

    def tile_dev(j):
        return (lax.div(j, 4), t, 2 * lax.rem(j, 4) + yh)

    def tiles_in(n, ref):
        in_f[n, :, 0:TOK] = ref[...].astype(F32).reshape(GROUP, TOK, 128).astype(BF)
        fan(u, own_tile, lambda j: in_f.at[n, j], in_r.at[n, row], in_ss.at[n], in_rs.at[n], tile_dev)

    def tiles_read(ref, n):
        whole = ref[n].astype(F32)
        return [whole[r, 0:TOK] for r in range(GROUP)]

    in_f[...] = jnp.zeros_like(in_f)
    out_f[...] = jnp.zeros_like(out_f)
    fetches[0].wait()
    tiles_in(0, images)

    for fetch in fetches[1:9]:
        fetch.wait()
    vec_s[...] = jnp.zeros_like(vec_s)
    for l in range(LAYERS):
        for i, ref in enumerate((gain1, bias1, outb, gain2, bias2, downb)):
            vec_s[l, i : i + 1, :] = ref[l : l + 1, :]
        vec_s[2 + l, 0:2, :] = qvb[l]
        for j in range(4):
            vec_s[2 + l, 2 + j : 3 + j, :] = upb[l : l + 1, 128 * j : 128 * j + 128]
    fan(row, own_plane, lambda j: vec_s, vec_g.at[row], vec_sem.at[0], vec_sem.at[1], plane_dev)

    weights = ((wqkv, wq_g), (wout, wo_g), (wup, wu_g), (wdown, wd_g))

    def weights_in(l):
        for m, (src, dst) in enumerate(weights):
            fan(row, own_plane, lambda j, src=src: src.at[l], dst.at[l, row], w_ss.at[l, m], w_rs.at[l, m], plane_dev)

    def weight_wait(l, m):
        drain(weights[m][1].at[l], w_rs.at[l, m])

    weights_in(0)
    fetches[9].wait()
    tiles_in(1, cot)

    def chip_at(k):
        return lax.rem(x + k, 4)

    def gather_start(l, s, value):
        folded = jnp.concatenate([value[:, :HALF], value[:, HALF:]], axis=0).astype(BF)
        ag[l, s, core, x] = folded
        mine = ag.at[l, s, core, x]
        for k in (2, 1, 3):
            push(mine, mine, ag_ss.at[l, s], ag_rs.at[l, s, k], chip_dev(chip_at(k)))
        push(mine, mine, ag_fs.at[l, s], ag_rs.at[l, s, 0], sibling)

    def gather_wait(l, s):
        for k in (1, 3, 2):
            came = ag.at[l, s, core, chip_at(4 - k)]
            drain(came, ag_rs.at[l, s, k])
            push(came, came, ag_fs.at[l, s], ag_rs.at[l, s, 0], sibling)
        drain(ag.at[l, s, 0], ag_rs.at[l, s, 0])

    def gather_read(l, s):
        whole = ag[l, s].astype(F32).reshape(GROUP, 2 * TOK, HALF)
        left = whole[:, :TOK].reshape(SEQ, HALF).astype(BF)
        right = whole[:, TOK:].reshape(SEQ, HALF).astype(BF)
        return left, right

    def scatter_start(l, s, left, right):
        both = jnp.concatenate([left.reshape(GROUP, TOK, HALF), right.reshape(GROUP, TOK, HALF)], axis=1)
        rs_s[l, s] = both.astype(BF).reshape(2, 4, 2 * TOK, HALF)
        for k in (2, 1, 3, 0):
            c = chip_at(k)
            push(rs_s.at[l, s, 1 - core, c], rs_b.at[l, s, c], rs_bs.at[l, s], rs_br.at[l, s, k], sibling)

    def pair_sum(l, s, k):
        c = chip_at(k)
        drain(rs_b.at[l, s, c], rs_br.at[l, s, k])
        return rs_s[l, s, core, c].astype(F32) + rs_b[l, s, c].astype(F32)

    def scatter_relay(l, s):
        for k in (2, 1, 3):
            rs_c[l, s, k] = pair_sum(l, s, k).astype(BF)
            push(rs_c.at[l, s, k], rs_r.at[l, s, k], rs_ss.at[l, s], rs_rs.at[l, s, k], chip_dev(chip_at(k)))

    def scatter_wait(l, s):
        total = pair_sum(l, s, 0)
        for k in (1, 3, 2):
            drain(rs_r.at[l, s, k], rs_rs.at[l, s, k])
            total += rs_r[l, s, k].astype(F32)
        return lanes([total[:TOK], total[TOK:]])

    def vec_row(l, i):
        return lanes([vec_g[r, l, i : i + 1, :] for r in range(GROUP)])

    def norm_forward(l, s, value):
        center = jnp.mean(value, axis=1, keepdims=True)
        shifted = value - center
        scaled = lax.rsqrt(jnp.mean(shifted * shifted, axis=1, keepdims=True) + EPS)
        normal = shifted * scaled
        normal_k[l, s] = normal
        scale_k[l, s] = jnp.broadcast_to(scaled, (TOK, 128))
        return normal * vec_row(l, 3 * s) + vec_row(l, 3 * s + 1)

    def norm_backward(l, s, grad_out):
        normal = normal_k[l, s]
        scaled = scale_k[l, s][:, 0:1]
        vacc[l, 3 * s : 3 * s + 1, :] = jnp.sum(grad_out * normal, axis=0, keepdims=True)
        vacc[l, 3 * s + 1 : 3 * s + 2, :] = jnp.sum(grad_out, axis=0, keepdims=True)
        upstream = grad_out * vec_row(l, 3 * s)
        mean_part = jnp.mean(upstream, axis=1, keepdims=True)
        proj_part = jnp.mean(upstream * normal, axis=1, keepdims=True)
        return scaled * (upstream - mean_part - normal * proj_part)

    def qkv_half(l, h):
        return jnp.concatenate([lanes([wq_g[l, 4 * h + r, j] for j in range(3)]) for r in range(4)], axis=0)

    def out_half(l, h):
        return lanes([wo_g[l, 4 * h + r] for r in range(4)])

    def up_half(l, h):
        return wu_g[l, 4 * h : 4 * h + 4].reshape(HALF, 512)

    def down_half(l, h):
        return lanes([wd_g[l, 4 * h + r] for r in range(4)])

    def head_mask(h):
        lane = lax.broadcasted_iota(jnp.int32, (SEQ, 128), 1)
        return (lane < HEAD_DIM) if h == 0 else (lane >= HEAD_DIM)

    def pick(pair):
        return jnp.where(head_mask(0), pair[0], pair[1])

    def only(h, value):
        return jnp.where(head_mask(h), value, jnp.zeros_like(value))

    drain(in_r.at[0], in_rs.at[0])
    stream[...] = lanes(tiles_read(in_r, 0))
    drain(vec_g, vec_sem.at[1])

    @pl.loop(0, LAYERS)
    def _(l):
        gather_start(l, 0, norm_forward(l, 0, stream[...]))

        @pl.when(l == 0)
        def _():
            weights_in(1)

        gather_wait(l, 0)
        left, right = gather_read(l, 0)
        weight_wait(l, 0)
        projected = dot(left, qkv_half(l, 0)) + dot(right, qkv_half(l, 1))
        shift = vec_g[0, 2 + l]
        query = (projected[:, :128] + shift[0:1]).astype(BF)
        keys = projected[:, 128:256].astype(BF)
        values = (projected[:, 256:] + shift[1:2]).astype(BF)
        qkv_k[l, 0] = query
        qkv_k[l, 1] = keys
        qkv_k[l, 2] = values
        mixed = []
        for h in range(2):
            scores = dot_last(only(h, query), keys) * HEAD_DIM ** -0.5
            raised = jnp.exp(scores - jnp.max(scores, axis=1, keepdims=True))
            probs = raised / jnp.sum(raised, axis=1, keepdims=True)
            prob_k[l, h] = probs
            mixed.append(dot(probs.astype(BF), values))
        mixed = pick(mixed).astype(BF)
        mixed_k[l] = mixed
        weight_wait(l, 1)
        scatter_start(l, 0, dot(mixed, out_half(l, 0)), dot(mixed, out_half(l, 1)))
        scatter_relay(l, 0)
        base = stream[...] + vec_row(l, 2)
        middle = base + scatter_wait(l, 0)
        stream[...] = middle
        gather_start(l, 1, norm_forward(l, 1, middle))
        gather_wait(l, 1)
        left, right = gather_read(l, 1)
        weight_wait(l, 2)
        before = dot(left, up_half(l, 0)) + dot(right, up_half(l, 1))
        shift = vec_g[0, 2 + l]
        before = before + lanes([shift[2 + j : 3 + j] for j in range(4)])
        phi = 0.5 * (1.0 + lax.erf(before * ROOT_HALF))
        hidden = (before * phi).astype(BF)
        hidden_k[l] = hidden
        weight_wait(l, 3)
        scatter_start(l, 1, dot(hidden, down_half(l, 0)), dot(hidden, down_half(l, 1)))
        scatter_relay(l, 1)
        slope_k[l] = phi + before * INV_ROOT_TAU * jnp.exp(-0.5 * before * before)
        base = stream[...] + vec_row(l, 5)
        stream[...] = base + scatter_wait(l, 1)

    def back_dev(r):
        return (lax.rem(row, 2), r, 2 * lax.div(row, 2) + yh)

    def tiles_out(n, value):
        for r in range(GROUP):
            out_f[n, r, 0:TOK] = value[:, 128 * r : 128 * r + 128].astype(BF)
        fan(row, own_tile, lambda j: out_f.at[n, j], out_r.at[n, u], out_ss.at[n], out_rs.at[n], back_dev)

    tiles_out(0, stream[...])

    drain(in_r.at[1], in_rs.at[1])
    grad_k[...] = lanes(tiles_read(in_r, 1))
    vacc[...] = jnp.zeros_like(vacc)
    vcol[...] = jnp.zeros_like(vcol)

    grads = (
        (gq_s, gq_r, sq, tq, gqkv_o, gqkv_h), (go_s, go_r, so, to, gout_o, gout_h),
        (gu_s, gu_r, su, tu, gup_o, gup_h), (gd_s, gd_r, sd, td, gdown_o, gdown_h),
    )

    def grads_out(l, m):
        src, dst = grads[m][:2]
        fan(row, own_plane, lambda j: src.at[l, j], dst.at[l, row], g_ss.at[l, m], g_rs.at[l, m], plane_dev)

    def sum_terms(l, m):
        src, dst, part, other = grads[m][:4]
        drain(dst.at[l], g_rs.at[l, m])
        total = dst[l, 0].astype(F32)
        for r in range(1, GROUP):
            total += dst[l, r].astype(F32)
        part[l] = total
        push(part.at[l], other.at[l], x_ss.at[l, m], x_rs.at[l, m], sibling)

    @pl.loop(0, LAYERS)
    def _(step):
        l = LAYERS - 1 - step
        branch2 = grad_k[...]
        gather_start(l, 2, branch2)
        vacc[l, 5:6, :] = jnp.sum(branch2.astype(BF).astype(F32), axis=0, keepdims=True)
        gather_wait(l, 2)
        left, right = gather_read(l, 2)
        hidden_grad = dot_last(left, down_half(l, 0)) + dot_last(right, down_half(l, 1))
        before_grad = (hidden_grad * slope_k[l]).astype(BF)
        scatter_start(l, 2, dot_last(before_grad, up_half(l, 0)), dot_last(before_grad, up_half(l, 1)))
        sums = jnp.sum(before_grad.astype(F32), axis=0, keepdims=True)
        for j in range(4):
            vcol[l, 2 + j : 3 + j, :] = sums[:, 128 * j : 128 * j + 128]
        scatter_relay(l, 2)
        for h, part in enumerate((left, right)):
            product = dot_first(hidden_k[l], part).astype(BF)
            for r in range(4):
                gd_s[l, 4 * h + r] = product[:, 128 * r : 128 * r + 128]
        grads_out(l, 3)
        for h, part in enumerate(gather_read(l, 1)):
            gu_s[l, 4 * h : 4 * h + 4] = dot_first(part, before_grad).astype(BF).reshape(4, 128, 512)
        grads_out(l, 2)
        grad_mid = grad_k[...] + norm_backward(l, 1, scatter_wait(l, 2))
        grad_k[...] = grad_mid
        gather_start(l, 3, grad_mid)
        vacc[l, 2:3, :] = jnp.sum(grad_mid.astype(BF).astype(F32), axis=0, keepdims=True)
        gather_wait(l, 3)
        left, right = gather_read(l, 3)
        mixed_grad = (dot_last(left, out_half(l, 0)) + dot_last(right, out_half(l, 1))).astype(BF)
        query = qkv_k[l, 0]
        keys = qkv_k[l, 1]
        values = qkv_k[l, 2]
        value_grads, query_grads, key_grads = [], [], []
        for h in range(2):
            probs = prob_k[l, h]
            probs_grad = dot_last(only(h, mixed_grad), values)
            inner = jnp.sum(probs * probs_grad, axis=1, keepdims=True)
            scores_grad = (probs * (probs_grad - inner)).astype(BF)
            value_grads.append(dot_first(probs.astype(BF), mixed_grad))
            query_grads.append(dot(scores_grad, keys))
            key_grads.append(dot_first(scores_grad, query))
        query_grad = (pick(query_grads) * HEAD_DIM ** -0.5).astype(BF)
        keys_grad = (pick(key_grads) * HEAD_DIM ** -0.5).astype(BF)
        values_grad = pick(value_grads).astype(BF)
        joined = lanes([query_grad, keys_grad, values_grad])
        scatter_start(l, 3, dot_last(joined, qkv_half(l, 0)), dot_last(joined, qkv_half(l, 1)))
        vcol[l, 0:1, :] = jnp.sum(query_grad.astype(F32), axis=0, keepdims=True)
        vcol[l, 1:2, :] = jnp.sum(values_grad.astype(F32), axis=0, keepdims=True)
        scatter_relay(l, 3)
        for h, part in enumerate(gather_read(l, 0)):
            product = dot_first(part, joined).astype(BF)
            for r in range(4):
                for j in range(3):
                    gq_s[l, 4 * h + r, j] = product[128 * r : 128 * r + 128, 128 * j : 128 * j + 128]
        grads_out(l, 0)
        for h, part in enumerate((left, right)):
            product = dot_first(mixed_k[l], part).astype(BF)
            for r in range(4):
                go_s[l, 4 * h + r] = product[:, 128 * r : 128 * r + 128]
        grads_out(l, 1)

        @pl.when(l == 0)
        def _():
            fan(row, own_plane, lambda j: vcol, vb_r.at[row], v_ss.at[1], v_rs.at[1], plane_dev)
            for m in (3, 2, 0, 1):
                sum_terms(1, m)

        grad_k[...] = grad_k[...] + norm_backward(l, 0, scatter_wait(l, 3))

    tiles_out(1, grad_k[...])

    for j in range(GROUP):
        vs_s[j] = vacc[:, :, 128 * j : 128 * j + 128]
    fan(row, own_plane, lambda j: vs_s.at[j], vs_r.at[row], v_ss.at[0], v_rs.at[0], plane_dev)

    results = []

    def result(src, dst):
        copy = pltpu.make_async_copy(src, dst, res_sem.at[len(results)])
        copy.start()
        results.append(copy)

    drain(out_r.at[0], out_rs.at[0])
    enc_o[...] = out_r[0].astype(F32)[:, 0:TOK].reshape(SEQ, 128).astype(BF)
    result(enc_o, enc_h)

    drain(vb_r, v_rs.at[1])
    vt_s[...] = jnp.sum(vb_r[...], axis=0)
    push(vt_s, vt_r, v_ss.at[2], v_rs.at[2], sibling)

    for m in (3, 2):
        sum_terms(0, m)

    drain(vs_r, v_rs.at[0])
    place = 2 * col + core
    vh_r[place] = jnp.sum(vs_r[...], axis=0)

    @pl.loop(1, 2 * GROUP)
    def _(k):
        j = lax.rem(place + k, 2 * GROUP)
        push(vh_r.at[place], vh_r.at[place], v_ss.at[3], v_rs.at[3], (lax.rem(j, 2), row, lax.div(j, 2)))

    for m in (0, 1):
        sum_terms(0, m)

    drain(vt_r, v_rs.at[2])
    columns = vt_s[...] + vt_r[...]
    for l in range(LAYERS):
        gqv_o[l] = columns[l, 0:2]
        for j in range(4):
            gub_o[l : l + 1, 128 * j : 128 * j + 128] = columns[l, 2 + j : 3 + j]
    result(gqv_o, gqv_h)
    result(gub_o, gub_h)

    drain(out_r.at[1], out_rs.at[1])
    gin_o[...] = out_r[1].astype(F32)[:, 0:TOK].reshape(SEQ, 128)
    result(gin_o, gin_h)

    for m in (3, 2, 0, 1):
        part, other, out, out_hbm = grads[m][2:]
        for l in (1, 0):
            drain(other.at[l], x_rs.at[l, m])
            out[l] = part[l] + other[l]
        result(out, out_hbm)

    drain(vh_r.at[pl.ds(0, 2 * GROUP - 1)], v_rs.at[3])
    rows = jnp.sum(vh_r[...], axis=0)
    for i, (ref, out_hbm) in enumerate(
        ((gg1_o, gg1_h), (gb1_o, gb1_h), (gob_o, gob_h), (gg2_o, gg2_h), (gb2_o, gb2_h), (gdb_o, gdb_h))
    ):
        for l in range(LAYERS):
            ref[l : l + 1, :] = rows[l, i : i + 1, :]
        result(ref, out_hbm)

    for n in range(2):
        fan_sent(own_tile, in_f.at[n], in_ss.at[n])
        fan_sent(own_tile, out_f.at[n], out_ss.at[n])
    fan_sent(own_plane, vec_g, vec_sem.at[0])
    fan_sent(own_plane, vb_r, v_ss.at[1])
    fan_sent(own_plane, vs_s, v_ss.at[0])
    drain(vt_s, v_ss.at[2])
    drain(vh_r.at[pl.ds(0, 2 * GROUP - 1)], v_ss.at[3])

    @pl.loop(0, LAYERS)
    def _(l):
        for m in range(4):
            fan_sent(own_plane, weights[m][1].at[l], w_ss.at[l, m])
            fan_sent(own_plane, grads[m][0].at[l], g_ss.at[l, m])
            drain(grads[m][2].at[l], x_ss.at[l, m])
        for s in range(4):
            drain(ag.at[l, s, 0, pl.ds(0, 3)], ag_ss.at[l, s])
            drain(ag.at[l, s, 0], ag_fs.at[l, s])
            drain(rs_b.at[l, s], rs_bs.at[l, s])
            drain(rs_c.at[l, s, pl.ds(1, 3)], rs_ss.at[l, s])

    for copy in results:
        copy.wait()


def finish(*refs):
    count = len(refs) // 2
    sems = refs[-1]
    copies = [pltpu.make_async_copy(refs[n], refs[count + n], sems.at[n]) for n in range(count)]
    for copy in copies:
        copy.start()
    for copy in copies:
        copy.wait()


def on_device(images, gain1, bias1, wqkv, qvb, wout, outb, gain2, bias2, wup, upb, wdown, downb, cot):
    L = LAYERS
    wqkv = wqkv.transpose(0, 2, 1, 3)
    hbm = pl.BlockSpec(memory_space=pl.ANY)
    shape = jax.ShapeDtypeStruct
    dma = pltpu.SemaphoreType.DMA
    V = pltpu.VMEM
    out_shape = (
        shape((SEQ, 128), BF),
        shape((SEQ, 128), F32),
        shape((L, 3, 128, 128), F32),
        shape((L, 128, 128), F32),
        shape((L, 128, 512), F32),
        shape((L, 512, 128), F32),
        shape((L, 128), F32),
        shape((L, 128), F32),
        shape((L, 2, 128), F32),
        shape((L, 128), F32),
        shape((L, 128), F32),
        shape((L, 128), F32),
        shape((L, 512), F32),
        shape((L, 128), F32),
    )
    operands = (images, gain1, bias1, wqkv, qvb, wout, outb, gain2, bias2, wup, upb, wdown, downb, cot)
    staged = [V(a.shape, a.dtype) for a in (images, gain1, bias1, qvb, outb, gain2, bias2, upb, downb, cot)]
    results = pl.pallas_call(
        kernel,
        out_shape=out_shape,
        in_specs=[hbm] * 14,
        out_specs=(hbm,) * 14,
        scratch_shapes=staged + [V(a.shape, a.dtype) for a in out_shape] + [
            V((2, 8, 48, 128), BF), V((2, 8, 48, 128), BF), V((2, 8, 48, 128), BF), V((2, 8, 48, 128), BF),
            V((4, 8, 128), F32), V((8, 4, 8, 128), F32),
            V((L, 8, 3, 128, 128), BF), V((L, 8, 128, 128), BF), V((L, 8, 128, 512), BF), V((L, 8, 512, 128), BF),
            V((L, 4, 2, 4, 2 * TOK, HALF), BF), V((L, 4, 2, 4, 2 * TOK, HALF), BF),
            V((L, 4, 4, 2 * TOK, HALF), BF), V((L, 4, 4, 2 * TOK, HALF), BF), V((L, 4, 4, 2 * TOK, HALF), BF),
            V((L, 8, 3, 128, 128), BF), V((L, 8, 128, 128), BF), V((L, 8, 128, 512), BF), V((L, 8, 512, 128), BF),
            V((L, 8, 3, 128, 128), BF), V((L, 8, 128, 128), BF), V((L, 8, 128, 512), BF), V((L, 8, 512, 128), BF),
            V((L, 3, 128, 128), F32), V((L, 128, 128), F32), V((L, 128, 512), F32), V((L, 512, 128), F32),
            V((L, 3, 128, 128), F32), V((L, 128, 128), F32), V((L, 128, 512), F32), V((L, 512, 128), F32),
            V((TOK, D), F32), V((L, 2, TOK, D), F32), V((L, 2, TOK, 128), F32), V((L, 2, SEQ, SEQ), F32),
            V((L, 3, SEQ, 128), BF), V((L, SEQ, 128), BF), V((L, SEQ, 512), BF), V((L, SEQ, 512), F32),
            V((TOK, D), F32),
            V((L, 8, D), F32), V((L, 8, 128), F32),
            V((8, L, 8, 128), F32), V((8, L, 8, 128), F32), V((16, L, 8, 128), F32),
            V((8, L, 8, 128), F32), V((L, 8, 128), F32), V((L, 8, 128), F32),
            dma((10,)), dma((14,)), dma((2,)), dma((2,)), dma((2,)), dma((2,)), dma((2,)), dma((L, 4)), dma((L, 4)),
            dma((L, 4)), dma((L, 4, 4)), dma((L, 4)), dma((L, 4)), dma((L, 4, 4)), dma((L, 4)), dma((L, 4, 4)),
            dma((L, 4)), dma((L, 4)), dma((L, 4)), dma((L, 4)), dma((4,)), dma((4,)),
        ],
        compiler_params=pltpu.CompilerParams(has_side_effects=True, vmem_limit_bytes=60 * 1024 * 1024),
        cost_estimate=pl.CostEstimate(flops=6 * 10**9, bytes_accessed=5 * 10**6, transcendentals=10**6),
    )(*operands)
    results = pl.pallas_call(
        finish,
        out_shape=out_shape,
        in_specs=[hbm] * 14,
        out_specs=(hbm,) * 14,
        scratch_shapes=[dma((14,))],
    )(*results)
    results = list(results)
    results[2] = results[2].transpose(0, 2, 1, 3)
    return tuple(results)


def solution(mesh):
    return jax.shard_map(
        on_device,
        mesh=mesh,
        in_specs=(
            P(("dp", "col"), "row"),
            P(None, "row"),
            P(None, "row"),
            P(None, "row", None, "col"),
            P(None, None, "col"),
            P(None, "col", "row"),
            P(None, "row"),
            P(None, "row"),
            P(None, "row"),
            P(None, "row", "col"),
            P(None, "col"),
            P(None, "col", "row"),
            P(None, "row"),
            P(("dp", "col"), "row"),
        ),
        out_specs=(
            P(("dp", "col"), "row"),
            P(("dp", "col"), "row"),
            P(None, "row", None, "col"),
            P(None, "col", "row"),
            P(None, "row", "col"),
            P(None, "col", "row"),
            P(None, "row"),
            P(None, "row"),
            P(None, None, "col"),
            P(None, "row"),
            P(None, "row"),
            P(None, "row"),
            P(None, "col"),
            P(None, "row"),
        ),
        check_vma=False,
    )
```

```python
import functools

import jax
import jax.numpy as jnp
from jax import lax
from jax.experimental import pallas as pl
from jax.experimental.pallas import tpu as pltpu
from jax.sharding import PartitionSpec as P

BF = jnp.bfloat16
F32 = jnp.float32
LAYERS = 2
GROUP = 8
TOK = 40
SEQ = 320
D = 1024
HALF = 512
HEAD_DIM = 64
EPS = 1e-6
ROOT_HALF = 0.7071067811865476
INV_ROOT_TAU = 0.3989422804014327
MESH = pl.DeviceIdType.MESH


def dot(a, b):
    return jnp.dot(a, b, preferred_element_type=F32)


def dot_last(a, b):
    return lax.dot_general(a, b, (((1,), (1,)), ((), ())), preferred_element_type=F32)


def dot_first(a, b):
    return lax.dot_general(a, b, (((0,), (0,)), ((), ())), preferred_element_type=F32)


def lanes(parts):
    return jnp.concatenate(parts, axis=1)


def kernel(
    images_h, gain1_h, bias1_h, wqkv, qvb_h, wout, outb_h, gain2_h, bias2_h, wup, upb_h, wdown, downb_h, cot_h,
    enc_h, gin_h, gqkv_h, gout_h, gup_h, gdown_h, gg1_h, gb1_h, gqv_h, gob_h, gg2_h, gb2_h, gub_h, gdb_h,
    images, gain1, bias1, qvb, outb, gain2, bias2, upb, downb, cot,
    enc_o, gin_o, gqkv_o, gout_o, gup_o, gdown_o, gg1_o, gb1_o, gqv_o, gob_o, gg2_o, gb2_o, gub_o, gdb_o,
    in_f, in_r, out_f, out_r,
    vec_s, vec_g, wq_g, wo_g, wu_g, wd_g,
    ag, rs_s, rs_b, rs_c, rs_r,
    gq_s, go_s, gu_s, gd_s, gq_r, go_r, gu_r, gd_r, gu_c, gu_f, gd_c, gd_f, sq, so, su, sd, tq, to, tu, td,
    stream, normal_k, scale_k, prob_k, qkv_k, mixed_k, hidden_k, slope_k, grad_k,
    vacc, vcol, vs_s, vs_r, vh_r, vb_r, vt_s, vt_r,
    op_sem, res_sem, in_ss, in_rs, out_ss, out_rs, vec_sem, w_ss, w_rs, wf_ss, wf_rs,
    ag_ss, ag_rs, ag_fs, rs_bs, rs_br, rs_ss, rs_rs, g_ss, g_rs, gf_ss, gf_rs, x_ss, x_rs, v_ss, v_rs,
):
    core = lax.axis_index("dp")
    row = lax.axis_index("row")
    col = lax.axis_index("col")
    x = lax.div(col, 2)
    yh = lax.rem(col, 2)
    z = lax.div(row, 2)
    yl = lax.rem(row, 2)
    y = 2 * yh + yl
    t = 2 * x + core
    u = 4 * core + x
    sibling = (1 - core, row, col)

    def chip_dev(c):
        return (core, row, 2 * c + yh)

    def plane_dev(r):
        return (yh, r, 2 * x + core)

    def push(src, dst, ssem, rsem, dev):
        pltpu.make_async_remote_copy(
            src_ref=src, dst_ref=dst, send_sem=ssem, recv_sem=rsem, device_id=dev, device_id_type=MESH
        ).start()

    def drain(ref, sem):
        pltpu.make_async_copy(ref, ref, sem).wait()

    def fan(me, own, src, dst, ssem, rsem, dev):
        @pl.when(own)
        def _():
            pltpu.make_async_copy(src(me), dst, rsem).start()

        @pl.when(jnp.logical_not(own))
        def _():
            push(src(me), dst, ssem, rsem, dev(me))

        @pl.loop(1, GROUP)
        def _(k):
            j = lax.rem(me + k, GROUP)
            push(src(j), dst, ssem, rsem, dev(j))

    def fan_sent(own, ref, ssem):
        @pl.when(own)
        def _():
            drain(ref.at[pl.ds(0, GROUP - 1)], ssem)

        @pl.when(jnp.logical_not(own))
        def _():
            drain(ref, ssem)

    own_plane = yh == core
    own_tile = row == t
    place = 2 * col + core

    def tile_dev(j):
        return (lax.div(j, 4), t, 2 * lax.rem(j, 4) + yh)

    def back_dev(r):
        return (lax.rem(row, 2), r, 2 * lax.div(row, 2) + yh)

    def y_dev(k):
        other = lax.rem(y + k, 4)
        return (core, 2 * z + lax.rem(other, 2), 2 * x + lax.div(other, 2))

    def z_at(k):
        return lax.rem(z + k, 4)

    def z_dev(k):
        return (core, 2 * z_at(k) + yl, col)

    def row_dev(j):
        return (lax.rem(j, 2), row, lax.div(j, 2))

    barrier = pltpu.get_barrier_semaphore()

    def greet(me, own, dev):
        @pl.when(jnp.logical_not(own))
        def _():
            pl.semaphore_signal(barrier, inc=1, device_id=dev(me), device_id_type=MESH)

        @pl.loop(1, GROUP)
        def _(k):
            pl.semaphore_signal(barrier, inc=1, device_id=dev(lax.rem(me + k, GROUP)), device_id_type=MESH)

    greet(u, own_tile, tile_dev)
    greet(row, own_tile, back_dev)
    greet(row, own_plane, plane_dev)
    for k in (1, 2, 3):
        pl.semaphore_signal(barrier, inc=1, device_id=y_dev(k), device_id_type=MESH)
        pl.semaphore_signal(barrier, inc=1, device_id=z_dev(k), device_id_type=MESH)

    @pl.loop(1, 2 * GROUP)
    def _(k):
        pl.semaphore_signal(barrier, inc=1, device_id=row_dev(lax.rem(place + k, 2 * GROUP)), device_id_type=MESH)

    small = (
        (images_h, images), (gain1_h, gain1), (bias1_h, bias1), (outb_h, outb), (gain2_h, gain2), (bias2_h, bias2),
        (downb_h, downb), (qvb_h, qvb), (upb_h, upb), (cot_h, cot),
    )
    fetches = [pltpu.make_async_copy(src, dst, op_sem.at[n]) for n, (src, dst) in enumerate(small)]
    for fetch in fetches:
        fetch.start()

    def tiles_fold(n, ref):
        in_f[n, :, 0:TOK] = ref[...].astype(F32).reshape(GROUP, TOK, 128).astype(BF)

    def tiles_in(n):
        fan(u, own_tile, lambda j: in_f.at[n, j], in_r.at[n, row], in_ss.at[n], in_rs.at[n], tile_dev)

    def tiles_read(ref, n):
        whole = ref[n].astype(F32)
        return [whole[r, 0:TOK] for r in range(GROUP)]

    in_f[...] = jnp.zeros_like(in_f)
    out_f[...] = jnp.zeros_like(out_f)
    fetches[0].wait()
    tiles_fold(0, images)

    greeted = 3 * GROUP + 6 + 2 * GROUP - 1
    pl.semaphore_wait(barrier, greeted - jnp.where(own_plane, 1, 0) - jnp.where(own_tile, 2, 0))
    tiles_in(0)

    for fetch in fetches[1:9]:
        fetch.wait()
    vec_s[...] = jnp.zeros_like(vec_s)
    for l in range(LAYERS):
        for i, ref in enumerate((gain1, bias1, outb, gain2, bias2, downb)):
            vec_s[l, i : i + 1, :] = ref[l : l + 1, :]
        vec_s[2 + l, 0:2, :] = qvb[l]
        for j in range(4):
            vec_s[2 + l, 2 + j : 3 + j, :] = upb[l : l + 1, 128 * j : 128 * j + 128]
    fan(row, own_plane, lambda j: vec_s, vec_g.at[row], vec_sem.at[0], vec_sem.at[1], plane_dev)

    weights = ((wqkv, wq_g), (wout, wo_g), (wup, wu_g), (wdown, wd_g))

    def y_first(m):
        return m in (0, 3)

    def weight_slot(m, r):
        return r if y_first(m) else 4 * (r % 2) + r // 2

    def weights_in(l):
        @pl.when(own_plane)
        def _():
            for m, (src, dst) in enumerate(weights):
                block = dst.at[l, row if y_first(m) else 4 * yl + z]
                pltpu.make_async_copy(src.at[l], block, w_rs.at[l, m]).start()
                for k in (2, 1, 3):
                    push(src.at[l], block, w_ss.at[l, m], w_rs.at[l, m], (y_dev if y_first(m) else z_dev)(k))

    def weights_relay(l, m):
        dst = weights[m][1]
        if y_first(m):
            pair = dst.at[l, pl.ds(2 * z, 2)]
            drain(pair, w_rs.at[l, m])
            for k in (2, 1, 3):
                push(pair, pair, wf_ss.at[l, m], wf_rs.at[l, m], z_dev(k))
        else:

            @pl.when(own_plane)
            def _():
                four = dst.at[l, pl.ds(4 * yl, 4)]
                drain(four, w_rs.at[l, m])
                for k in (2, 1, 3):
                    push(four, four, wf_ss.at[l, m], wf_rs.at[l, m], y_dev(k))

    def weight_wait(l, m):
        dst = weights[m][1]
        if y_first(m):
            drain(dst.at[l, pl.ds(0, 6)], wf_rs.at[l, m])
        else:

            @pl.when(own_plane)
            def _():
                drain(dst.at[l, pl.ds(0, 4)], wf_rs.at[l, m])

            @pl.when(jnp.logical_not(own_plane))
            def _():
                drain(dst.at[l], wf_rs.at[l, m])

    def weights_sent(l, m):
        dst = weights[m][1]

        @pl.when(own_plane)
        def _():
            drain(dst.at[l, pl.ds(0, 3)], w_ss.at[l, m])

        if y_first(m):
            drain(dst.at[l, pl.ds(0, 6)], wf_ss.at[l, m])
        else:

            @pl.when(own_plane)
            def _():
                drain(dst.at[:, pl.ds(0, 6)], wf_ss.at[l, m])

    weights_in(0)
    fetches[9].wait()
    tiles_fold(1, cot)
    tiles_in(1)

    def chip_at(k):
        return lax.rem(x + k, 4)

    def gather_start(l, s, value):
        folded = jnp.concatenate([value[:, :HALF], value[:, HALF:]], axis=0).astype(BF)
        ag[l, s, core, x] = folded
        mine = ag.at[l, s, core, x]
        for k in (2, 1, 3):
            push(mine, mine, ag_ss.at[l, s], ag_rs.at[l, s, k], chip_dev(chip_at(k)))
        push(mine, mine, ag_fs.at[l, s], ag_rs.at[l, s, 0], sibling)

    def gather_wait(l, s):
        for k in (1, 3, 2):
            came = ag.at[l, s, core, chip_at(4 - k)]
            drain(came, ag_rs.at[l, s, k])
            push(came, came, ag_fs.at[l, s], ag_rs.at[l, s, 0], sibling)
        drain(ag.at[l, s, 0], ag_rs.at[l, s, 0])

    def gather_read(l, s):
        whole = ag[l, s].astype(F32).reshape(GROUP, 2 * TOK, HALF)
        left = whole[:, :TOK].reshape(SEQ, HALF).astype(BF)
        right = whole[:, TOK:].reshape(SEQ, HALF).astype(BF)
        return left, right

    def scatter_start(l, s, left, right):
        both = jnp.concatenate([left.reshape(GROUP, TOK, HALF), right.reshape(GROUP, TOK, HALF)], axis=1)
        rs_s[l, s] = both.astype(BF).reshape(2, 4, 2 * TOK, HALF)
        for k in (2, 1, 3, 0):
            c = chip_at(k)
            push(rs_s.at[l, s, 1 - core, c], rs_b.at[l, s, c], rs_bs.at[l, s], rs_br.at[l, s, k], sibling)

    def pair_sum(l, s, k):
        c = chip_at(k)
        drain(rs_b.at[l, s, c], rs_br.at[l, s, k])
        return rs_s[l, s, core, c].astype(F32) + rs_b[l, s, c].astype(F32)

    def scatter_relay(l, s):
        for k in (2, 1, 3):
            rs_c[l, s, k] = pair_sum(l, s, k).astype(BF)
            push(rs_c.at[l, s, k], rs_r.at[l, s, k], rs_ss.at[l, s], rs_rs.at[l, s, k], chip_dev(chip_at(k)))

    def scatter_wait(l, s):
        total = pair_sum(l, s, 0)
        for k in (1, 3, 2):
            drain(rs_r.at[l, s, k], rs_rs.at[l, s, k])
            total += rs_r[l, s, k].astype(F32)
        return lanes([total[:TOK], total[TOK:]])

    def vec_row(l, i):
        return lanes([vec_g[r, l, i : i + 1, :] for r in range(GROUP)])

    def norm_forward(l, s, value):
        center = jnp.mean(value, axis=1, keepdims=True)
        shifted = value - center
        scaled = lax.rsqrt(jnp.mean(shifted * shifted, axis=1, keepdims=True) + EPS)
        normal = shifted * scaled
        normal_k[l, s] = normal
        scale_k[l, s] = jnp.broadcast_to(scaled, (TOK, 128))
        return normal * vec_row(l, 3 * s) + vec_row(l, 3 * s + 1)

    def norm_backward(l, s, grad_out):
        normal = normal_k[l, s]
        scaled = scale_k[l, s][:, 0:1]
        vacc[l, 3 * s : 3 * s + 1, :] = jnp.sum(grad_out * normal, axis=0, keepdims=True)
        vacc[l, 3 * s + 1 : 3 * s + 2, :] = jnp.sum(grad_out, axis=0, keepdims=True)
        upstream = grad_out * vec_row(l, 3 * s)
        mean_part = jnp.mean(upstream, axis=1, keepdims=True)
        proj_part = jnp.mean(upstream * normal, axis=1, keepdims=True)
        return scaled * (upstream - mean_part - normal * proj_part)

    def qkv_half(l, h):
        return jnp.concatenate([lanes([wq_g[l, weight_slot(0, 4 * h + r), j] for j in range(3)]) for r in range(4)], axis=0)

    def out_half(l, h):
        return lanes([wo_g[l, weight_slot(1, 4 * h + r)] for r in range(4)])

    def up_half(l, h):
        return jnp.concatenate([wu_g[l, weight_slot(2, 4 * h + r)] for r in range(4)], axis=0)

    def down_half(l, h):
        return lanes([wd_g[l, weight_slot(3, 4 * h + r)] for r in range(4)])

    def head_mask(h):
        lane = lax.broadcasted_iota(jnp.int32, (SEQ, 128), 1)
        return (lane < HEAD_DIM) if h == 0 else (lane >= HEAD_DIM)

    def pick(pair):
        return jnp.where(head_mask(0), pair[0], pair[1])

    def only(h, value):
        return jnp.where(head_mask(h), value, jnp.zeros_like(value))

    drain(in_r.at[0], in_rs.at[0])
    stream[...] = lanes(tiles_read(in_r, 0))
    drain(vec_g, vec_sem.at[1])

    @pl.loop(0, LAYERS)
    def _(l):
        gather_start(l, 0, norm_forward(l, 0, stream[...]))

        @pl.when(l == 0)
        def _():
            for m in (0, 1, 2):
                weights_relay(0, m)

        gather_wait(l, 0)
        left, right = gather_read(l, 0)
        weight_wait(l, 0)
        projected = dot(left, qkv_half(l, 0)) + dot(right, qkv_half(l, 1))
        shift = vec_g[0, 2 + l]
        query = (projected[:, :128] + shift[0:1]).astype(BF)
        keys = projected[:, 128:256].astype(BF)
        values = (projected[:, 256:] + shift[1:2]).astype(BF)
        qkv_k[l, 0] = query
        qkv_k[l, 1] = keys
        qkv_k[l, 2] = values
        mixed = []
        for h in range(2):
            scores = dot_last(only(h, query), keys) * HEAD_DIM ** -0.5
            raised = jnp.exp(scores - jnp.max(scores, axis=1, keepdims=True))
            probs = raised / jnp.sum(raised, axis=1, keepdims=True)
            prob_k[l, h] = probs
            mixed.append(dot(probs.astype(BF), values))
        mixed = pick(mixed).astype(BF)
        mixed_k[l] = mixed
        weight_wait(l, 1)
        scatter_start(l, 0, dot(mixed, out_half(l, 0)), dot(mixed, out_half(l, 1)))
        scatter_relay(l, 0)

        @pl.when(l == 0)
        def _():
            weights_relay(0, 3)
            weights_in(1)

        base = stream[...] + vec_row(l, 2)
        middle = base + scatter_wait(l, 0)
        stream[...] = middle
        gather_start(l, 1, norm_forward(l, 1, middle))
        gather_wait(l, 1)
        left, right = gather_read(l, 1)
        weight_wait(l, 2)
        before = dot(left, up_half(l, 0)) + dot(right, up_half(l, 1))
        shift = vec_g[0, 2 + l]
        before = before + lanes([shift[2 + j : 3 + j] for j in range(4)])
        phi = 0.5 * (1.0 + lax.erf(before * ROOT_HALF))
        hidden = (before * phi).astype(BF)
        hidden_k[l] = hidden
        weight_wait(l, 3)
        scatter_start(l, 1, dot(hidden, down_half(l, 0)), dot(hidden, down_half(l, 1)))
        scatter_relay(l, 1)

        @pl.when(l == 0)
        def _():
            for m in range(4):
                weights_relay(1, m)

        slope_k[l] = phi + before * INV_ROOT_TAU * jnp.exp(-0.5 * before * before)
        base = stream[...] + vec_row(l, 5)
        stream[...] = base + scatter_wait(l, 1)

    def tiles_out(n, value):
        for r in range(GROUP):
            out_f[n, r, 0:TOK] = value[:, 128 * r : 128 * r + 128].astype(BF)
        fan(row, own_tile, lambda j: out_f.at[n, j], out_r.at[n, u], out_ss.at[n], out_rs.at[n], back_dev)

    tiles_out(0, stream[...])

    drain(in_r.at[1], in_rs.at[1])
    grad_k[...] = lanes(tiles_read(in_r, 1))
    vacc[...] = jnp.zeros_like(vacc)
    vcol[...] = jnp.zeros_like(vcol)

    grads = (
        (gq_s, gq_r, sq, tq, gqkv_o, gqkv_h), (go_s, go_r, so, to, gout_o, gout_h),
        (gu_s, gu_r, su, tu, gup_o, gup_h), (gd_s, gd_r, sd, td, gdown_o, gdown_h),
    )

    def grad_slot(m, r):
        return 4 * (r % 2) + r // 2 if m == 3 else r

    def pair_fan(src, dst, ssem, rsem):
        def dev(j):
            return plane_dev(2 * z + j)

        @pl.when(own_plane)
        def _():
            pltpu.make_async_copy(src(yl), dst, rsem).start()

        @pl.when(jnp.logical_not(own_plane))
        def _():
            push(src(yl), dst, ssem, rsem, dev(yl))

        push(src(1 - yl), dst, ssem, rsem, dev(1 - yl))

    def grads_out(l, m):
        src, dst = grads[m][:2]
        if m == 2:
            for k in (2, 1, 3):
                push(src.at[l, pl.ds(2 * z_at(k), 2)], dst.at[l, k], g_ss.at[l, m], g_rs.at[l, m], z_dev(k))
        elif m == 3:
            pair_fan(lambda j: src.at[l, pl.ds(4 * j, 4)], dst.at[l, yl], g_ss.at[l, m], g_rs.at[l, m])
        else:
            fan(row, own_plane, lambda j: src.at[l, j], dst.at[l, row], g_ss.at[l, m], g_rs.at[l, m], plane_dev)

    def up_relay(l):
        drain(gu_r.at[l, pl.ds(1, 3)], g_rs.at[l, 2])
        for j in range(2):
            total = gu_s[l, 2 * z + j].astype(F32)
            for k in (1, 2, 3):
                total += gu_r[l, k, j].astype(F32)
            gu_c[l, j] = total.astype(BF)
        pair_fan(lambda j: gu_c.at[l, j], gu_f.at[l, yl], gf_ss.at[l, 0], gf_rs.at[l, 0])

    def down_relay(l):
        drain(gd_r.at[l], g_rs.at[l, 3])
        for j in range(4):
            gd_c[l, j] = (gd_r[l, 0, j].astype(F32) + gd_r[l, 1, j].astype(F32)).astype(BF)
        for k in (2, 1, 3):
            push(gd_c.at[l, z_at(k)], gd_f.at[l, k], gf_ss.at[l, 1], gf_rs.at[l, 1], z_dev(k))

    def pair_sent(ref, ssem):
        @pl.when(own_plane)
        def _():
            drain(ref.at[0], ssem)

        @pl.when(jnp.logical_not(own_plane))
        def _():
            drain(ref, ssem)

    def grads_sent(l, m):
        src, dst = grads[m][:2]
        if m == 2:
            drain(dst.at[l, pl.ds(1, 3)], g_ss.at[l, m])
            pair_sent(gu_c.at[l], gf_ss.at[l, 0])
        elif m == 3:
            pair_sent(dst.at[l], g_ss.at[l, m])
            drain(gd_f.at[l, pl.ds(1, 3)], gf_ss.at[l, 1])
        else:
            fan_sent(own_plane, src.at[l], g_ss.at[l, m])

    def sum_terms(l, m):
        src, dst, part, other = grads[m][:4]
        if m == 2:
            drain(gu_f.at[l], gf_rs.at[l, 0])
            total = gu_f[l, 0].astype(F32) + gu_f[l, 1].astype(F32)
        elif m == 3:
            drain(gd_f.at[l, pl.ds(1, 3)], gf_rs.at[l, 1])
            total = gd_c[l, z].astype(F32)
            for k in (1, 2, 3):
                total += gd_f[l, k].astype(F32)
        else:
            drain(dst.at[l], g_rs.at[l, m])
            total = dst[l, 0].astype(F32)
            for r in range(1, GROUP):
                total += dst[l, r].astype(F32)
        part[l] = total
        push(part.at[l], other.at[l], x_ss.at[l, m], x_rs.at[l, m], sibling)

    @pl.loop(0, LAYERS)
    def _(step):
        l = LAYERS - 1 - step
        branch2 = grad_k[...]
        gather_start(l, 2, branch2)
        vacc[l, 5:6, :] = jnp.sum(branch2.astype(BF).astype(F32), axis=0, keepdims=True)
        gather_wait(l, 2)
        left, right = gather_read(l, 2)
        hidden_grad = dot_last(left, down_half(l, 0)) + dot_last(right, down_half(l, 1))
        before_grad = (hidden_grad * slope_k[l]).astype(BF)
        scatter_start(l, 2, dot_last(before_grad, up_half(l, 0)), dot_last(before_grad, up_half(l, 1)))
        sums = jnp.sum(before_grad.astype(F32), axis=0, keepdims=True)
        for j in range(4):
            vcol[l, 2 + j : 3 + j, :] = sums[:, 128 * j : 128 * j + 128]
        scatter_relay(l, 2)
        for h, part in enumerate((left, right)):
            product = dot_first(hidden_k[l], part).astype(BF)
            for r in range(4):
                gd_s[l, grad_slot(3, 4 * h + r)] = product[:, 128 * r : 128 * r + 128]
        grads_out(l, 3)
        for h, part in enumerate(gather_read(l, 1)):
            gu_s[l, 4 * h : 4 * h + 4] = dot_first(part, before_grad).astype(BF).reshape(4, 128, 512)
        grads_out(l, 2)
        grad_mid = grad_k[...] + norm_backward(l, 1, scatter_wait(l, 2))
        grad_k[...] = grad_mid
        gather_start(l, 3, grad_mid)
        vacc[l, 2:3, :] = jnp.sum(grad_mid.astype(BF).astype(F32), axis=0, keepdims=True)
        gather_wait(l, 3)
        left, right = gather_read(l, 3)
        mixed_grad = (dot_last(left, out_half(l, 0)) + dot_last(right, out_half(l, 1))).astype(BF)
        for h, part in enumerate((left, right)):
            product = dot_first(mixed_k[l], part).astype(BF)
            for r in range(4):
                go_s[l, 4 * h + r] = product[:, 128 * r : 128 * r + 128]
        grads_out(l, 1)
        query = qkv_k[l, 0]
        keys = qkv_k[l, 1]
        values = qkv_k[l, 2]
        value_grads, query_grads, key_grads = [], [], []
        for h in range(2):
            probs = prob_k[l, h]
            probs_grad = dot_last(only(h, mixed_grad), values)
            inner = jnp.sum(probs * probs_grad, axis=1, keepdims=True)
            scores_grad = (probs * (probs_grad - inner)).astype(BF)
            value_grads.append(dot_first(probs.astype(BF), mixed_grad))
            query_grads.append(dot(scores_grad, keys))
            key_grads.append(dot_first(scores_grad, query))
        query_grad = (pick(query_grads) * HEAD_DIM ** -0.5).astype(BF)
        keys_grad = (pick(key_grads) * HEAD_DIM ** -0.5).astype(BF)
        values_grad = pick(value_grads).astype(BF)
        joined = lanes([query_grad, keys_grad, values_grad])
        scatter_start(l, 3, dot_last(joined, qkv_half(l, 0)), dot_last(joined, qkv_half(l, 1)))
        vcol[l, 0:1, :] = jnp.sum(query_grad.astype(F32), axis=0, keepdims=True)
        vcol[l, 1:2, :] = jnp.sum(values_grad.astype(F32), axis=0, keepdims=True)
        scatter_relay(l, 3)
        for h, part in enumerate(gather_read(l, 0)):
            product = dot_first(part, joined).astype(BF)
            for r in range(4):
                for j in range(3):
                    gq_s[l, 4 * h + r, j] = product[128 * r : 128 * r + 128, 128 * j : 128 * j + 128]
        grads_out(l, 0)
        up_relay(l)
        down_relay(l)

        @pl.when(l == 0)
        def _():
            fan(row, own_plane, lambda j: vcol, vb_r.at[row], v_ss.at[1], v_rs.at[1], plane_dev)
            for m in (3, 2, 0, 1):
                sum_terms(1, m)

        grad_k[...] = grad_k[...] + norm_backward(l, 0, scatter_wait(l, 3))

    tiles_out(1, grad_k[...])

    for j in range(GROUP):
        vs_s[j] = vacc[:, :, 128 * j : 128 * j + 128]
    fan(row, own_plane, lambda j: vs_s.at[j], vs_r.at[row], v_ss.at[0], v_rs.at[0], plane_dev)

    results = []

    def result(src, dst):
        copy = pltpu.make_async_copy(src, dst, res_sem.at[len(results)])
        copy.start()
        results.append(copy)

    drain(out_r.at[0], out_rs.at[0])
    enc_o[...] = out_r[0].astype(F32)[:, 0:TOK].reshape(SEQ, 128).astype(BF)
    result(enc_o, enc_h)

    drain(vb_r, v_rs.at[1])
    vt_s[...] = jnp.sum(vb_r[...], axis=0)
    push(vt_s, vt_r, v_ss.at[2], v_rs.at[2], sibling)

    for m in (3, 2):
        sum_terms(0, m)

    drain(vs_r, v_rs.at[0])
    vh_r[place] = jnp.sum(vs_r[...], axis=0)

    @pl.loop(1, 2 * GROUP)
    def _(k):
        push(vh_r.at[place], vh_r.at[place], v_ss.at[3], v_rs.at[3], row_dev(lax.rem(place + k, 2 * GROUP)))

    for m in (0, 1):
        sum_terms(0, m)

    drain(vt_r, v_rs.at[2])
    columns = vt_s[...] + vt_r[...]
    for l in range(LAYERS):
        gqv_o[l] = columns[l, 0:2]
        for j in range(4):
            gub_o[l : l + 1, 128 * j : 128 * j + 128] = columns[l, 2 + j : 3 + j]
    result(gqv_o, gqv_h)
    result(gub_o, gub_h)

    drain(out_r.at[1], out_rs.at[1])
    gin_o[...] = out_r[1].astype(F32)[:, 0:TOK].reshape(SEQ, 128)
    result(gin_o, gin_h)

    for m in (3, 2, 0, 1):
        part, other, out, out_hbm = grads[m][2:]
        for l in (1, 0):
            drain(other.at[l], x_rs.at[l, m])
            out[l] = part[l] + other[l]
        result(out, out_hbm)

    drain(vh_r.at[pl.ds(0, 2 * GROUP - 1)], v_rs.at[3])
    rows = jnp.sum(vh_r[...], axis=0)
    for i, (ref, out_hbm) in enumerate(
        ((gg1_o, gg1_h), (gb1_o, gb1_h), (gob_o, gob_h), (gg2_o, gg2_h), (gb2_o, gb2_h), (gdb_o, gdb_h))
    ):
        for l in range(LAYERS):
            ref[l : l + 1, :] = rows[l, i : i + 1, :]
        result(ref, out_hbm)

    for n in range(2):
        fan_sent(own_tile, in_f.at[n], in_ss.at[n])
        fan_sent(own_tile, out_f.at[n], out_ss.at[n])
    fan_sent(own_plane, vec_g, vec_sem.at[0])
    fan_sent(own_plane, vb_r, v_ss.at[1])
    fan_sent(own_plane, vs_s, v_ss.at[0])
    drain(vt_s, v_ss.at[2])
    drain(vh_r.at[pl.ds(0, 2 * GROUP - 1)], v_ss.at[3])

    @pl.loop(0, LAYERS)
    def _(l):
        for m in range(4):
            weights_sent(l, m)
            grads_sent(l, m)
            drain(grads[m][2].at[l], x_ss.at[l, m])
        for s in range(4):
            drain(ag.at[l, s, 0, pl.ds(0, 3)], ag_ss.at[l, s])
            drain(ag.at[l, s, 0], ag_fs.at[l, s])
            drain(rs_b.at[l, s], rs_bs.at[l, s])
            drain(rs_c.at[l, s, pl.ds(1, 3)], rs_ss.at[l, s])

    for copy in results:
        copy.wait()


def finish(*refs):
    count = (len(refs) - 2) // 3
    ins, outs, held = refs[:count], refs[count : 2 * count], refs[2 * count : 3 * count]
    in_sem, out_sem = refs[3 * count :]
    loads = [pltpu.make_async_copy(ins[n], held[n], in_sem.at[n]) for n in range(count)]
    stores = [pltpu.make_async_copy(held[n], outs[n], out_sem.at[n]) for n in range(count)]
    for copy in loads:
        copy.start()
    for load, store in zip(loads, stores):
        load.wait()
        store.start()
    for copy in stores:
        copy.wait()


def on_device(images, gain1, bias1, wqkv, qvb, wout, outb, gain2, bias2, wup, upb, wdown, downb, cot):
    L = LAYERS
    wqkv = wqkv.transpose(0, 2, 1, 3)
    hbm = pl.BlockSpec(memory_space=pl.ANY)
    shape = jax.ShapeDtypeStruct
    dma = pltpu.SemaphoreType.DMA
    V = pltpu.VMEM
    out_shape = (
        shape((SEQ, 128), BF),
        shape((SEQ, 128), F32),
        shape((L, 3, 128, 128), F32),
        shape((L, 128, 128), F32),
        shape((L, 128, 512), F32),
        shape((L, 512, 128), F32),
        shape((L, 128), F32),
        shape((L, 128), F32),
        shape((L, 2, 128), F32),
        shape((L, 128), F32),
        shape((L, 128), F32),
        shape((L, 128), F32),
        shape((L, 512), F32),
        shape((L, 128), F32),
    )
    operands = (images, gain1, bias1, wqkv, qvb, wout, outb, gain2, bias2, wup, upb, wdown, downb, cot)
    staged = [V(a.shape, a.dtype) for a in (images, gain1, bias1, qvb, outb, gain2, bias2, upb, downb, cot)]
    results = pl.pallas_call(
        kernel,
        out_shape=out_shape,
        in_specs=[hbm] * 14,
        out_specs=(hbm,) * 14,
        scratch_shapes=staged + [V(a.shape, a.dtype) for a in out_shape] + [
            V((2, 8, 48, 128), BF), V((2, 8, 48, 128), BF), V((2, 8, 48, 128), BF), V((2, 8, 48, 128), BF),
            V((4, 8, 128), F32), V((8, 4, 8, 128), F32),
            V((L, 8, 3, 128, 128), BF), V((L, 8, 128, 128), BF), V((L, 8, 128, 512), BF), V((L, 8, 512, 128), BF),
            V((L, 4, 2, 4, 2 * TOK, HALF), BF), V((L, 4, 2, 4, 2 * TOK, HALF), BF),
            V((L, 4, 4, 2 * TOK, HALF), BF), V((L, 4, 4, 2 * TOK, HALF), BF), V((L, 4, 4, 2 * TOK, HALF), BF),
            V((L, 8, 3, 128, 128), BF), V((L, 8, 128, 128), BF), V((L, 8, 128, 512), BF), V((L, 8, 512, 128), BF),
            V((L, 8, 3, 128, 128), BF), V((L, 8, 128, 128), BF), V((L, 4, 2, 128, 512), BF), V((L, 2, 4, 512, 128), BF),
            V((L, 2, 128, 512), BF), V((L, 2, 128, 512), BF), V((L, 4, 512, 128), BF), V((L, 4, 512, 128), BF),
            V((L, 3, 128, 128), F32), V((L, 128, 128), F32), V((L, 128, 512), F32), V((L, 512, 128), F32),
            V((L, 3, 128, 128), F32), V((L, 128, 128), F32), V((L, 128, 512), F32), V((L, 512, 128), F32),
            V((TOK, D), F32), V((L, 2, TOK, D), F32), V((L, 2, TOK, 128), F32), V((L, 2, SEQ, SEQ), F32),
            V((L, 3, SEQ, 128), BF), V((L, SEQ, 128), BF), V((L, SEQ, 512), BF), V((L, SEQ, 512), F32),
            V((TOK, D), F32),
            V((L, 8, D), F32), V((L, 8, 128), F32),
            V((8, L, 8, 128), F32), V((8, L, 8, 128), F32), V((16, L, 8, 128), F32),
            V((8, L, 8, 128), F32), V((L, 8, 128), F32), V((L, 8, 128), F32),
            dma((10,)), dma((14,)), dma((2,)), dma((2,)), dma((2,)), dma((2,)), dma((2,)), dma((L, 4)), dma((L, 4)), dma((L, 4)), dma((L, 4)),
            dma((L, 4)), dma((L, 4, 4)), dma((L, 4)), dma((L, 4)), dma((L, 4, 4)), dma((L, 4)), dma((L, 4, 4)),
            dma((L, 4)), dma((L, 4)), dma((L, 2)), dma((L, 2)), dma((L, 4)), dma((L, 4)), dma((4,)), dma((4,)),
        ],
        compiler_params=pltpu.CompilerParams(collective_id=0, has_side_effects=True, vmem_limit_bytes=60 * 1024 * 1024),
        cost_estimate=pl.CostEstimate(flops=6 * 10**9, bytes_accessed=5 * 10**6, transcendentals=10**6),
    )(*operands)
    results = pl.pallas_call(
        finish,
        out_shape=out_shape,
        in_specs=[hbm] * 14,
        out_specs=(hbm,) * 14,
        scratch_shapes=[V(a.shape, a.dtype) for a in out_shape] + [dma((14,)), dma((14,))],
    )(*results)
    results = list(results)
    results[2] = results[2].transpose(0, 2, 1, 3)
    return tuple(results)


def solution(mesh):
    return jax.shard_map(
        on_device,
        mesh=mesh,
        in_specs=(
            P(("dp", "col"), "row"),
            P(None, "row"),
            P(None, "row"),
            P(None, "row", None, "col"),
            P(None, None, "col"),
            P(None, "col", "row"),
            P(None, "row"),
            P(None, "row"),
            P(None, "row"),
            P(None, "row", "col"),
            P(None, "col"),
            P(None, "col", "row"),
            P(None, "row"),
            P(("dp", "col"), "row"),
        ),
        out_specs=(
            P(("dp", "col"), "row"),
            P(("dp", "col"), "row"),
            P(None, "row", None, "col"),
            P(None, "col", "row"),
            P(None, "row", "col"),
            P(None, "col", "row"),
            P(None, "row"),
            P(None, "row"),
            P(None, None, "col"),
            P(None, "row"),
            P(None, "row"),
            P(None, "row"),
            P(None, "col"),
            P(None, "row"),
        ),
        check_vma=False,
    )
```

```python
import functools

import jax
import jax.numpy as jnp
from jax import lax
from jax.experimental import pallas as pl
from jax.experimental.pallas import tpu as pltpu
from jax.sharding import PartitionSpec as P

BF = jnp.bfloat16
F32 = jnp.float32
LAYERS = 2
GROUP = 8
TOK = 40
ROWS = (40,)
FIRST = (0,)
PARTS = (0,)
SEQ = 320
D = 1024
HALF = 512
HEAD_DIM = 64
EPS = 1e-6
ROOT_HALF = 0.7071067811865476
INV_ROOT_TAU = 0.3989422804014327
MESH = pl.DeviceIdType.MESH


def dot(a, b):
    return jnp.dot(a, b, preferred_element_type=F32)


def dot_last(a, b):
    return lax.dot_general(a, b, (((1,), (1,)), ((), ())), preferred_element_type=F32)


def dot_first(a, b):
    return lax.dot_general(a, b, (((0,), (0,)), ((), ())), preferred_element_type=F32)


def lanes(parts):
    return jnp.concatenate(parts, axis=1)


def kernel(
    images_h, gain1_h, bias1_h, wqkv, qvb_h, wout, outb_h, gain2_h, bias2_h, wup, upb_h, wdown, downb_h, cot_h,
    enc_h, gin_h, gqkv_h, gout_h, gup_h, gdown_h, gg1_h, gb1_h, gqv_h, gob_h, gg2_h, gb2_h, gub_h, gdb_h,
    images, gain1, bias1, qvb, outb, gain2, bias2, upb, downb, cot,
    enc_o, gin_o, gqkv_o, gout_o, gup_o, gdown_o, gg1_o, gb1_o, gqv_o, gob_o, gg2_o, gb2_o, gub_o, gdb_o,
    in_f, in_r, out_f, out_r,
    vec_s, vec_g, wq_g, wo_g, wu_g, wd_g,
    ag, rs_s, rs_b, rs_c, rs_r,
    gq_s, go_s, gu_s, gd_s, gq_r, go_r, gu_r, gd_r, gu_c, gu_f, gd_c, gd_f, sq, so, su, sd, tq, to, tu, td,
    stream, normal_k, scale_k, prob_k, qkv_k, mixed_k, hidden_k, slope_k, before_k, before_grad_k, grad_k,
    vacc, vcol, vs_s, vs_r, vh_r, vb_r, vt_s, vt_r,
    op_sem, res_sem, in_ss, in_rs, out_ss, out_rs, vec_sem, w_ss, w_rs, wf_ss, wf_rs,
    ag_ss, ag_rs, ag_fs, rs_bs, rs_br, rs_ss, rs_rs, g_ss, g_rs, gf_ss, gf_rs, x_ss, x_rs, v_ss, v_rs,
):
    core = lax.axis_index("dp")
    row = lax.axis_index("row")
    col = lax.axis_index("col")
    x = lax.div(col, 2)
    yh = lax.rem(col, 2)
    z = lax.div(row, 2)
    yl = lax.rem(row, 2)
    y = 2 * yh + yl
    t = 2 * x + core
    u = 4 * core + x
    sibling = (1 - core, row, col)

    def chip_dev(c):
        return (core, row, 2 * c + yh)

    def plane_dev(r):
        return (yh, r, 2 * x + core)

    def push(src, dst, ssem, rsem, dev):
        pltpu.make_async_remote_copy(
            src_ref=src, dst_ref=dst, send_sem=ssem, recv_sem=rsem, device_id=dev, device_id_type=MESH
        ).start()

    def drain(ref, sem):
        pltpu.make_async_copy(ref, ref, sem).wait()

    def fan(me, own, src, dst, ssem, rsem, dev):
        @pl.when(own)
        def _():
            pltpu.make_async_copy(src(me), dst, rsem).start()

        @pl.when(jnp.logical_not(own))
        def _():
            push(src(me), dst, ssem, rsem, dev(me))

        @pl.loop(1, GROUP)
        def _(k):
            j = lax.rem(me + k, GROUP)
            push(src(j), dst, ssem, rsem, dev(j))

    def fan_sent(own, ref, ssem):
        @pl.when(own)
        def _():
            drain(ref.at[pl.ds(0, GROUP - 1)], ssem)

        @pl.when(jnp.logical_not(own))
        def _():
            drain(ref, ssem)

    own_plane = yh == core
    own_tile = row == t
    place = 2 * col + core

    def tile_dev(j):
        return (lax.div(j, 4), t, 2 * lax.rem(j, 4) + yh)

    def back_dev(r):
        return (lax.rem(row, 2), r, 2 * lax.div(row, 2) + yh)

    def y_dev(k):
        other = lax.rem(y + k, 4)
        return (core, 2 * z + lax.rem(other, 2), 2 * x + lax.div(other, 2))

    def z_at(k):
        return lax.rem(z + k, 4)

    def z_dev(k):
        return (core, 2 * z_at(k) + yl, col)

    def row_dev(j):
        return (lax.rem(j, 2), row, lax.div(j, 2))

    barrier = pltpu.get_barrier_semaphore()

    def greet(me, own, dev):
        @pl.when(jnp.logical_not(own))
        def _():
            pl.semaphore_signal(barrier, inc=1, device_id=dev(me), device_id_type=MESH)

        @pl.loop(1, GROUP)
        def _(k):
            pl.semaphore_signal(barrier, inc=1, device_id=dev(lax.rem(me + k, GROUP)), device_id_type=MESH)

    greet(u, own_tile, tile_dev)
    greet(row, own_tile, back_dev)
    greet(row, own_plane, plane_dev)
    for k in (1, 2, 3):
        pl.semaphore_signal(barrier, inc=1, device_id=y_dev(k), device_id_type=MESH)
        pl.semaphore_signal(barrier, inc=1, device_id=z_dev(k), device_id_type=MESH)

    @pl.loop(1, 2 * GROUP)
    def _(k):
        pl.semaphore_signal(barrier, inc=1, device_id=row_dev(lax.rem(place + k, 2 * GROUP)), device_id_type=MESH)

    small = (
        (images_h, images), (gain1_h, gain1), (bias1_h, bias1), (outb_h, outb), (gain2_h, gain2), (bias2_h, bias2),
        (downb_h, downb), (qvb_h, qvb), (upb_h, upb), (cot_h, cot),
    )
    fetches = [pltpu.make_async_copy(src, dst, op_sem.at[n]) for n, (src, dst) in enumerate(small)]
    for fetch in fetches:
        fetch.start()

    def tiles_fold(n, ref):
        in_f[n, :, 0:TOK] = ref[...].astype(F32).reshape(GROUP, TOK, 128).astype(BF)

    def tiles_in(n):
        fan(u, own_tile, lambda j: in_f.at[n, j], in_r.at[n, row], in_ss.at[n], in_rs.at[n], tile_dev)

    def tiles_read(ref, n):
        whole = ref[n].astype(F32)
        return [whole[r, 0:TOK] for r in range(GROUP)]

    in_f[...] = jnp.zeros_like(in_f)
    out_f[...] = jnp.zeros_like(out_f)
    fetches[0].wait()
    tiles_fold(0, images)

    greeted = 3 * GROUP + 6 + 2 * GROUP - 1
    pl.semaphore_wait(barrier, greeted - jnp.where(own_plane, 1, 0) - jnp.where(own_tile, 2, 0))
    tiles_in(0)

    for fetch in fetches[1:9]:
        fetch.wait()
    vec_s[...] = jnp.zeros_like(vec_s)
    for l in range(LAYERS):
        for i, ref in enumerate((gain1, bias1, outb, gain2, bias2, downb)):
            vec_s[l, i : i + 1, :] = ref[l : l + 1, :]
        vec_s[2 + l, 0:2, :] = qvb[l]
        for j in range(4):
            vec_s[2 + l, 2 + j : 3 + j, :] = upb[l : l + 1, 128 * j : 128 * j + 128]
    fan(row, own_plane, lambda j: vec_s, vec_g.at[row], vec_sem.at[0], vec_sem.at[1], plane_dev)

    weights = ((wqkv, wq_g), (wout, wo_g), (wup, wu_g), (wdown, wd_g))

    def y_first(m):
        return m in (0, 3)

    def weight_slot(m, r):
        return r if y_first(m) else 4 * (r % 2) + r // 2

    def qkv_in(l):
        fan(row, own_plane, lambda j: wqkv.at[l], wq_g.at[l, row], w_ss.at[l, 0], w_rs.at[l, 0], plane_dev)

    def weights_in(l):
        @pl.when(own_plane)
        def _():
            for m in (1, 2, 3):
                src, dst = weights[m]
                block = dst.at[l, row if y_first(m) else 4 * yl + z]
                pltpu.make_async_copy(src.at[l], block, w_rs.at[l, m]).start()
                for k in (2, 1, 3):
                    push(src.at[l], block, w_ss.at[l, m], w_rs.at[l, m], (y_dev if y_first(m) else z_dev)(k))

    def weights_relay(l, m):
        dst = weights[m][1]
        if m == 3:
            pair = dst.at[l, pl.ds(2 * z, 2)]
            drain(pair, w_rs.at[l, m])
            for k in (2, 1, 3):
                push(pair, pair, wf_ss.at[l, m], wf_rs.at[l, m], z_dev(k))
        else:

            @pl.when(own_plane)
            def _():
                four = dst.at[l, pl.ds(4 * yl, 4)]
                drain(four, w_rs.at[l, m])
                for k in (2, 1, 3):
                    push(four, four, wf_ss.at[l, m], wf_rs.at[l, m], y_dev(k))

    def weight_wait(l, m):
        dst = weights[m][1]
        if m == 0:
            drain(dst.at[l], w_rs.at[l, m])
        elif m == 3:
            drain(dst.at[l, pl.ds(0, 6)], wf_rs.at[l, m])
        else:

            @pl.when(own_plane)
            def _():
                drain(dst.at[l, pl.ds(0, 4)], wf_rs.at[l, m])

            @pl.when(jnp.logical_not(own_plane))
            def _():
                drain(dst.at[l], wf_rs.at[l, m])

    def weights_sent(l, m):
        dst = weights[m][1]
        if m == 0:
            fan_sent(own_plane, dst.at[l], w_ss.at[l, m])
            return

        @pl.when(own_plane)
        def _():
            drain(dst.at[l, pl.ds(0, 3)], w_ss.at[l, m])

        if m == 3:
            drain(dst.at[l, pl.ds(0, 6)], wf_ss.at[l, m])
        else:

            @pl.when(own_plane)
            def _():
                drain(dst.at[:, pl.ds(0, 6)], wf_ss.at[l, m])

    weights_in(0)
    qkv_in(0)

    def chip_at(k):
        return lax.rem(x + k, 4)

    def own_rows(p):
        return slice(FIRST[p], FIRST[p] + ROWS[p])

    def all_rows(p):
        return slice(GROUP * FIRST[p], GROUP * (FIRST[p] + ROWS[p]))

    def gather_start(l, s, p, value):
        folded = jnp.concatenate([value[:, :HALF], value[:, HALF:]], axis=0).astype(BF)
        ag[p][l, s, core, x] = folded
        mine = ag[p].at[l, s, core, x]
        for k in (2, 1, 3):
            push(mine, mine, ag_ss.at[l, s, p], ag_rs.at[l, s, p, k], chip_dev(chip_at(k)))
        push(mine, mine, ag_fs.at[l, s, p], ag_rs.at[l, s, p, 0], sibling)

    def gather_wait(l, s, p):
        for k in (1, 3, 2):
            came = ag[p].at[l, s, core, chip_at(4 - k)]
            drain(came, ag_rs.at[l, s, p, k])
            push(came, came, ag_fs.at[l, s, p], ag_rs.at[l, s, p, 0], sibling)
        drain(ag[p].at[l, s, 0], ag_rs.at[l, s, p, 0])

    def gather_read(l, s, p):
        rows = ROWS[p]
        whole = ag[p][l, s].astype(F32).reshape(GROUP, 2 * rows, HALF)
        left = whole[:, :rows].reshape(GROUP * rows, HALF).astype(BF)
        right = whole[:, rows:].reshape(GROUP * rows, HALF).astype(BF)
        return left, right

    def gather_whole(l, s):
        parts = [gather_read(l, s, p) for p in PARTS]
        return [jnp.concatenate([part[h] for part in parts], axis=0) for h in range(2)]

    def scatter_start(l, s, p, left, right):
        rows = ROWS[p]
        both = jnp.concatenate([left.reshape(GROUP, rows, HALF), right.reshape(GROUP, rows, HALF)], axis=1)
        rs_s[p][l, s] = both.astype(BF).reshape(2, 4, 2 * rows, HALF)
        for k in (2, 1, 3, 0):
            c = chip_at(k)
            push(rs_s[p].at[l, s, 1 - core, c], rs_b[p].at[l, s, c], rs_bs.at[l, s, p], rs_br.at[l, s, p, k], sibling)

    def pair_sum(l, s, p, k):
        c = chip_at(k)
        drain(rs_b[p].at[l, s, c], rs_br.at[l, s, p, k])
        return rs_s[p][l, s, core, c].astype(F32) + rs_b[p][l, s, c].astype(F32)

    def scatter_relay(l, s, p):
        for k in (2, 1, 3):
            rs_c[p][l, s, k] = pair_sum(l, s, p, k).astype(BF)
            push(rs_c[p].at[l, s, k], rs_r[p].at[l, s, k], rs_ss.at[l, s, p], rs_rs.at[l, s, p, k], chip_dev(chip_at(k)))

    def scatter_wait(l, s, p):
        rows = ROWS[p]
        total = pair_sum(l, s, p, 0)
        for k in (1, 3, 2):
            drain(rs_r[p].at[l, s, k], rs_rs.at[l, s, p, k])
            total += rs_r[p][l, s, k].astype(F32)
        return lanes([total[:rows], total[rows:]])

    def vec_row(l, i):
        return lanes([vec_g[r, l, i : i + 1, :] for r in range(GROUP)])

    def norm_forward(l, s, p, value):
        center = jnp.mean(value, axis=1, keepdims=True)
        shifted = value - center
        scaled = lax.rsqrt(jnp.mean(shifted * shifted, axis=1, keepdims=True) + EPS)
        normal = shifted * scaled
        normal_k[l, s, own_rows(p)] = normal
        scale_k[l, s, own_rows(p)] = jnp.broadcast_to(scaled, (ROWS[p], 128))
        return normal * vec_row(l, 3 * s) + vec_row(l, 3 * s + 1)

    def add_row(l, i, value):
        vacc[l, i : i + 1, :] += jnp.sum(value, axis=0, keepdims=True)

    def norm_backward(l, s, p, grad_out):
        normal = normal_k[l, s, own_rows(p)]
        scaled = scale_k[l, s, own_rows(p)][:, 0:1]
        add_row(l, 3 * s, grad_out * normal)
        add_row(l, 3 * s + 1, grad_out)
        upstream = grad_out * vec_row(l, 3 * s)
        mean_part = jnp.mean(upstream, axis=1, keepdims=True)
        proj_part = jnp.mean(upstream * normal, axis=1, keepdims=True)
        return scaled * (upstream - mean_part - normal * proj_part)

    def qkv_half(l, h):
        return jnp.concatenate([lanes([wq_g[l, weight_slot(0, 4 * h + r), j] for j in range(3)]) for r in range(4)], axis=0)

    def out_half(l, h):
        return lanes([wo_g[l, weight_slot(1, 4 * h + r)] for r in range(4)])

    def up_half(l, h):
        return jnp.concatenate([wu_g[l, weight_slot(2, 4 * h + r)] for r in range(4)], axis=0)

    def down_half(l, h):
        return lanes([wd_g[l, weight_slot(3, 4 * h + r)] for r in range(4)])

    def head_mask(h):
        lane = lax.broadcasted_iota(jnp.int32, (SEQ, 128), 1)
        return (lane < HEAD_DIM) if h == 0 else (lane >= HEAD_DIM)

    def pick(pair):
        return jnp.where(head_mask(0), pair[0], pair[1])

    def only(h, value):
        return jnp.where(head_mask(h), value, jnp.zeros_like(value))

    drain(in_r.at[0], in_rs.at[0])
    stream[...] = lanes(tiles_read(in_r, 0))
    drain(vec_g, vec_sem.at[1])
    for p in PARTS:
        gather_start(0, 0, p, norm_forward(0, 0, p, stream[own_rows(p)]))
    for m in (1, 2, 3):
        weights_relay(0, m)
    fetches[9].wait()
    tiles_fold(1, cot)
    tiles_in(1)

    def hidden_part(l, p):
        left, right = gather_read(l, 1, p)
        before = dot(left, up_half(l, 0)) + dot(right, up_half(l, 1))
        shift = vec_g[0, 2 + l]
        before = before + lanes([shift[2 + j : 3 + j] for j in range(4)])
        phi = 0.5 * (1.0 + lax.erf(before * ROOT_HALF))
        hidden = (before * phi).astype(BF)
        hidden_k[l, all_rows(p)] = hidden
        before_k[all_rows(p)] = before
        slope_k[l, all_rows(p)] = phi
        if p == 0:
            weight_wait(l, 3)
        scatter_start(l, 1, p, dot(hidden, down_half(l, 0)), dot(hidden, down_half(l, 1)))

    @pl.loop(0, LAYERS)
    def _(l):
        for p in PARTS:
            gather_wait(l, 0, p)
            left, right = gather_read(l, 0, p)
            if p == 0:
                weight_wait(l, 0)
            projected = dot(left, qkv_half(l, 0)) + dot(right, qkv_half(l, 1))
            shift = vec_g[0, 2 + l]
            qkv_k[l, 0, all_rows(p)] = (projected[:, :128] + shift[0:1]).astype(BF)
            qkv_k[l, 1, all_rows(p)] = projected[:, 128:256].astype(BF)
            qkv_k[l, 2, all_rows(p)] = (projected[:, 256:] + shift[1:2]).astype(BF)
        query = qkv_k[l, 0]
        keys = qkv_k[l, 1]
        values = qkv_k[l, 2]
        mixed = []
        for h in range(2):
            scores = dot_last(only(h, query), keys) * HEAD_DIM ** -0.5
            raised = jnp.exp(scores - jnp.max(scores, axis=1, keepdims=True))
            probs = raised / jnp.sum(raised, axis=1, keepdims=True)
            prob_k[l, h] = probs
            mixed.append(dot(probs.astype(BF), values))
        mixed = pick(mixed).astype(BF)
        mixed_k[l] = mixed
        weight_wait(l, 1)
        for p in PARTS:
            part = mixed[all_rows(p)]
            scatter_start(l, 0, p, dot(part, out_half(l, 0)), dot(part, out_half(l, 1)))
        for p in PARTS:
            scatter_relay(l, 0, p)
        @pl.when(l == 0)
        def _():
            weights_in(1)
            qkv_in(1)

        for p in PARTS:
            middle = stream[own_rows(p)] + vec_row(l, 2) + scatter_wait(l, 0, p)
            stream[own_rows(p)] = middle
            gather_start(l, 1, p, norm_forward(l, 1, p, middle))
        for p in PARTS:
            gather_wait(l, 1, p)
            if p == 0:
                weight_wait(l, 2)
            else:
                scatter_relay(l, 1, p - 1)
            hidden_part(l, p)
        scatter_relay(l, 1, PARTS[-1])

        @pl.when(l == 0)
        def _():
            for m in (1, 2, 3):
                weights_relay(1, m)
            drain(in_r.at[1], in_rs.at[1])
            grad_k[...] = lanes(tiles_read(in_r, 1))
            for p in PARTS:
                gather_start(LAYERS - 1, 2, p, grad_k[own_rows(p)])

        before = before_k[...]
        slope_k[l] = slope_k[l] + before * INV_ROOT_TAU * jnp.exp(-0.5 * before * before)

        @pl.when(l == 0)
        def _():
            for p in PARTS:
                value = stream[own_rows(p)] + vec_row(0, 5) + scatter_wait(0, 1, p)
                stream[own_rows(p)] = value
                gather_start(1, 0, p, norm_forward(1, 0, p, value))

    def tiles_out(n, value):
        for r in range(GROUP):
            out_f[n, r, 0:TOK] = value[:, 128 * r : 128 * r + 128].astype(BF)
        fan(row, own_tile, lambda j: out_f.at[n, j], out_r.at[n, u], out_ss.at[n], out_rs.at[n], back_dev)

    vacc[...] = jnp.zeros_like(vacc)
    vcol[...] = jnp.zeros_like(vcol)

    grads = (
        (gq_s, gq_r, sq, tq, gqkv_o, gqkv_h), (go_s, go_r, so, to, gout_o, gout_h),
        (gu_s, gu_r, su, tu, gup_o, gup_h), (gd_s, gd_r, sd, td, gdown_o, gdown_h),
    )

    def grad_slot(m, r):
        return 4 * (r % 2) + r // 2 if m == 3 else r

    def pair_fan(src, dst, ssem, rsem):
        def dev(j):
            return plane_dev(2 * z + j)

        @pl.when(own_plane)
        def _():
            pltpu.make_async_copy(src(yl), dst, rsem).start()

        @pl.when(jnp.logical_not(own_plane))
        def _():
            push(src(yl), dst, ssem, rsem, dev(yl))

        push(src(1 - yl), dst, ssem, rsem, dev(1 - yl))

    def grads_out(l, m):
        src, dst = grads[m][:2]
        if m == 2:
            for k in (2, 1, 3):
                push(src.at[l, pl.ds(2 * z_at(k), 2)], dst.at[l, k], g_ss.at[l, m], g_rs.at[l, m], z_dev(k))
        elif m == 3:
            pair_fan(lambda j: src.at[l, pl.ds(4 * j, 4)], dst.at[l, yl], g_ss.at[l, m], g_rs.at[l, m])
        else:
            fan(row, own_plane, lambda j: src.at[l, j], dst.at[l, row], g_ss.at[l, m], g_rs.at[l, m], plane_dev)

    def up_relay(l):
        drain(gu_r.at[l, pl.ds(1, 3)], g_rs.at[l, 2])
        for j in range(2):
            total = gu_s[l, 2 * z + j].astype(F32)
            for k in (1, 2, 3):
                total += gu_r[l, k, j].astype(F32)
            gu_c[l, j] = total.astype(BF)
        pair_fan(lambda j: gu_c.at[l, j], gu_f.at[l, yl], gf_ss.at[l, 0], gf_rs.at[l, 0])

    def down_relay(l):
        drain(gd_r.at[l], g_rs.at[l, 3])
        for j in range(4):
            gd_c[l, j] = (gd_r[l, 0, j].astype(F32) + gd_r[l, 1, j].astype(F32)).astype(BF)
        for k in (2, 1, 3):
            push(gd_c.at[l, z_at(k)], gd_f.at[l, k], gf_ss.at[l, 1], gf_rs.at[l, 1], z_dev(k))

    def pair_sent(ref, ssem):
        @pl.when(own_plane)
        def _():
            drain(ref.at[0], ssem)

        @pl.when(jnp.logical_not(own_plane))
        def _():
            drain(ref, ssem)

    def grads_sent(l, m):
        src, dst = grads[m][:2]
        if m == 2:
            drain(dst.at[l, pl.ds(1, 3)], g_ss.at[l, m])
            pair_sent(gu_c.at[l], gf_ss.at[l, 0])
        elif m == 3:
            pair_sent(dst.at[l], g_ss.at[l, m])
            drain(gd_f.at[l, pl.ds(1, 3)], gf_ss.at[l, 1])
        else:
            fan_sent(own_plane, src.at[l], g_ss.at[l, m])

    def sum_terms(l, m):
        src, dst, part, other = grads[m][:4]
        if m == 2:
            drain(gu_f.at[l], gf_rs.at[l, 0])
            total = gu_f[l, 0].astype(F32) + gu_f[l, 1].astype(F32)
        elif m == 3:
            drain(gd_f.at[l, pl.ds(1, 3)], gf_rs.at[l, 1])
            total = gd_c[l, z].astype(F32)
            for k in (1, 2, 3):
                total += gd_f[l, k].astype(F32)
        else:
            drain(dst.at[l], g_rs.at[l, m])
            total = dst[l, 0].astype(F32)
            for r in range(1, GROUP):
                total += dst[l, r].astype(F32)
        part[l] = total
        push(part.at[l], other.at[l], x_ss.at[l, m], x_rs.at[l, m], sibling)

    def hidden_back(l, p):
        left, right = gather_read(l, 2, p)
        hidden_grad = dot_last(left, down_half(l, 0)) + dot_last(right, down_half(l, 1))
        before_grad = (hidden_grad * slope_k[l, all_rows(p)]).astype(BF)
        before_grad_k[all_rows(p)] = before_grad
        scatter_start(l, 2, p, dot_last(before_grad, up_half(l, 0)), dot_last(before_grad, up_half(l, 1)))

    @pl.loop(0, LAYERS)
    def _(step):
        l = LAYERS - 1 - step
        add_row(l, 5, grad_k[...].astype(BF).astype(F32))
        for p in PARTS:
            gather_wait(l, 2, p)
            if p > 0:
                scatter_relay(l, 2, p - 1)
            hidden_back(l, p)
        scatter_relay(l, 2, PARTS[-1])
        before_grad = before_grad_k[...]
        for h, part in enumerate(gather_whole(l, 2)):
            product = dot_first(hidden_k[l], part).astype(BF)
            for r in range(4):
                gd_s[l, grad_slot(3, 4 * h + r)] = product[:, 128 * r : 128 * r + 128]
        grads_out(l, 3)
        for h, part in enumerate(gather_whole(l, 1)):
            gu_s[l, 4 * h : 4 * h + 4] = dot_first(part, before_grad).astype(BF).reshape(4, 128, 512)
        grads_out(l, 2)
        for p in PARTS:
            grad_mid = grad_k[own_rows(p)] + norm_backward(l, 1, p, scatter_wait(l, 2, p))
            grad_k[own_rows(p)] = grad_mid
            gather_start(l, 3, p, grad_mid)
        sums = jnp.sum(before_grad.astype(F32), axis=0, keepdims=True)
        for j in range(4):
            vcol[l, 2 + j : 3 + j, :] = sums[:, 128 * j : 128 * j + 128]
        add_row(l, 2, grad_k[...].astype(BF).astype(F32))

        @pl.when(step == 0)
        def _():
            for p in PARTS:
                stream[own_rows(p)] = stream[own_rows(p)] + vec_row(LAYERS - 1, 5) + scatter_wait(LAYERS - 1, 1, p)
            tiles_out(0, stream[...])

        mixed_grad = []
        for p in PARTS:
            gather_wait(l, 3, p)
            left, right = gather_read(l, 3, p)
            mixed_grad.append((dot_last(left, out_half(l, 0)) + dot_last(right, out_half(l, 1))).astype(BF))
        mixed_grad = jnp.concatenate(mixed_grad, axis=0)
        query = qkv_k[l, 0]
        keys = qkv_k[l, 1]
        values = qkv_k[l, 2]
        value_grads, query_grads, key_grads = [], [], []
        for h in range(2):
            probs = prob_k[l, h]
            probs_grad = dot_last(only(h, mixed_grad), values)
            inner = jnp.sum(probs * probs_grad, axis=1, keepdims=True)
            scores_grad = (probs * (probs_grad - inner)).astype(BF)
            value_grads.append(dot_first(probs.astype(BF), mixed_grad))
            query_grads.append(dot(scores_grad, keys))
            key_grads.append(dot_first(scores_grad, query))
        query_grad = (pick(query_grads) * HEAD_DIM ** -0.5).astype(BF)
        keys_grad = (pick(key_grads) * HEAD_DIM ** -0.5).astype(BF)
        values_grad = pick(value_grads).astype(BF)
        joined = lanes([query_grad, keys_grad, values_grad])
        for p in PARTS:
            part = joined[all_rows(p)]
            scatter_start(l, 3, p, dot_last(part, qkv_half(l, 0)), dot_last(part, qkv_half(l, 1)))
        for p in PARTS:
            scatter_relay(l, 3, p)
        for h, part in enumerate(gather_whole(l, 0)):
            product = dot_first(part, joined).astype(BF)
            for r in range(4):
                for j in range(3):
                    gq_s[l, 4 * h + r, j] = product[128 * r : 128 * r + 128, 128 * j : 128 * j + 128]
        grads_out(l, 0)
        for h, part in enumerate(gather_whole(l, 3)):
            product = dot_first(mixed_k[l], part).astype(BF)
            for r in range(4):
                go_s[l, 4 * h + r] = product[:, 128 * r : 128 * r + 128]
        grads_out(l, 1)
        up_relay(l)
        down_relay(l)
        vcol[l, 0:1, :] = jnp.sum(query_grad.astype(F32), axis=0, keepdims=True)
        vcol[l, 1:2, :] = jnp.sum(values_grad.astype(F32), axis=0, keepdims=True)

        @pl.when(l == 0)
        def _():
            fan(row, own_plane, lambda j: vcol, vb_r.at[row], v_ss.at[1], v_rs.at[1], plane_dev)
            for m in (3, 2, 0, 1):
                sum_terms(1, m)

        for p in PARTS:
            grad_k[own_rows(p)] = grad_k[own_rows(p)] + norm_backward(l, 0, p, scatter_wait(l, 3, p))

            @pl.when(l > 0)
            def _():
                gather_start(l - 1, 2, p, grad_k[own_rows(p)])

    tiles_out(1, grad_k[...])

    for j in range(GROUP):
        vs_s[j] = vacc[:, :, 128 * j : 128 * j + 128]
    fan(row, own_plane, lambda j: vs_s.at[j], vs_r.at[row], v_ss.at[0], v_rs.at[0], plane_dev)

    results = []

    def result(src, dst):
        copy = pltpu.make_async_copy(src, dst, res_sem.at[len(results)])
        copy.start()
        results.append(copy)

    drain(out_r.at[0], out_rs.at[0])
    enc_o[...] = out_r[0].astype(F32)[:, 0:TOK].reshape(SEQ, 128).astype(BF)
    result(enc_o, enc_h)

    drain(vb_r, v_rs.at[1])
    vt_s[...] = jnp.sum(vb_r[...], axis=0)
    push(vt_s, vt_r, v_ss.at[2], v_rs.at[2], sibling)

    for m in (3, 2):
        sum_terms(0, m)

    drain(vs_r, v_rs.at[0])
    vh_r[place] = jnp.sum(vs_r[...], axis=0)

    @pl.loop(1, 2 * GROUP)
    def _(k):
        push(vh_r.at[place], vh_r.at[place], v_ss.at[3], v_rs.at[3], row_dev(lax.rem(place + k, 2 * GROUP)))

    for m in (0, 1):
        sum_terms(0, m)

    drain(vt_r, v_rs.at[2])
    columns = vt_s[...] + vt_r[...]
    for l in range(LAYERS):
        gqv_o[l] = columns[l, 0:2]
        for j in range(4):
            gub_o[l : l + 1, 128 * j : 128 * j + 128] = columns[l, 2 + j : 3 + j]
    result(gqv_o, gqv_h)
    result(gub_o, gub_h)

    drain(out_r.at[1], out_rs.at[1])
    gin_o[...] = out_r[1].astype(F32)[:, 0:TOK].reshape(SEQ, 128)
    result(gin_o, gin_h)

    for m in (3, 2, 0, 1):
        part, other, out, out_hbm = grads[m][2:]
        for l in (1, 0):
            drain(other.at[l], x_rs.at[l, m])
            out[l] = part[l] + other[l]
        result(out, out_hbm)

    drain(vh_r.at[pl.ds(0, 2 * GROUP - 1)], v_rs.at[3])
    rows = jnp.sum(vh_r[...], axis=0)
    for i, (ref, out_hbm) in enumerate(
        ((gg1_o, gg1_h), (gb1_o, gb1_h), (gob_o, gob_h), (gg2_o, gg2_h), (gb2_o, gb2_h), (gdb_o, gdb_h))
    ):
        for l in range(LAYERS):
            ref[l : l + 1, :] = rows[l, i : i + 1, :]
        result(ref, out_hbm)

    for n in range(2):
        fan_sent(own_tile, in_f.at[n], in_ss.at[n])
        fan_sent(own_tile, out_f.at[n], out_ss.at[n])
    fan_sent(own_plane, vec_g, vec_sem.at[0])
    fan_sent(own_plane, vb_r, v_ss.at[1])
    fan_sent(own_plane, vs_s, v_ss.at[0])
    drain(vt_s, v_ss.at[2])
    drain(vh_r.at[pl.ds(0, 2 * GROUP - 1)], v_ss.at[3])

    @pl.loop(0, LAYERS)
    def _(l):
        for m in range(4):
            weights_sent(l, m)
            grads_sent(l, m)
            drain(grads[m][2].at[l], x_ss.at[l, m])
        for s in range(4):
            for p in PARTS:
                drain(ag[p].at[l, s, 0, pl.ds(0, 3)], ag_ss.at[l, s, p])
                drain(ag[p].at[l, s, 0], ag_fs.at[l, s, p])
                drain(rs_b[p].at[l, s], rs_bs.at[l, s, p])
                drain(rs_c[p].at[l, s, pl.ds(1, 3)], rs_ss.at[l, s, p])

    for copy in results:
        copy.wait()


def finish(*refs):
    count = (len(refs) - 2) // 3
    ins, outs, held = refs[:count], refs[count : 2 * count], refs[2 * count : 3 * count]
    in_sem, out_sem = refs[3 * count :]
    loads = [pltpu.make_async_copy(ins[n], held[n], in_sem.at[n]) for n in range(count)]
    stores = [pltpu.make_async_copy(held[n], outs[n], out_sem.at[n]) for n in range(count)]
    for copy in loads:
        copy.start()
    for load, store in zip(loads, stores):
        load.wait()
        store.start()
    for copy in stores:
        copy.wait()


def on_device(images, gain1, bias1, wqkv, qvb, wout, outb, gain2, bias2, wup, upb, wdown, downb, cot):
    L = LAYERS
    N = len(PARTS)
    wqkv = wqkv.transpose(0, 2, 1, 3)
    hbm = pl.BlockSpec(memory_space=pl.ANY)
    shape = jax.ShapeDtypeStruct
    dma = pltpu.SemaphoreType.DMA
    V = pltpu.VMEM
    out_shape = (
        shape((SEQ, 128), BF),
        shape((SEQ, 128), F32),
        shape((L, 3, 128, 128), F32),
        shape((L, 128, 128), F32),
        shape((L, 128, 512), F32),
        shape((L, 512, 128), F32),
        shape((L, 128), F32),
        shape((L, 128), F32),
        shape((L, 2, 128), F32),
        shape((L, 128), F32),
        shape((L, 128), F32),
        shape((L, 128), F32),
        shape((L, 512), F32),
        shape((L, 128), F32),
    )
    operands = (images, gain1, bias1, wqkv, qvb, wout, outb, gain2, bias2, wup, upb, wdown, downb, cot)
    staged = [V(a.shape, a.dtype) for a in (images, gain1, bias1, qvb, outb, gain2, bias2, upb, downb, cot)]
    results = pl.pallas_call(
        kernel,
        out_shape=out_shape,
        in_specs=[hbm] * 14,
        out_specs=(hbm,) * 14,
        scratch_shapes=staged + [V(a.shape, a.dtype) for a in out_shape] + [
            V((2, 8, 48, 128), BF), V((2, 8, 48, 128), BF), V((2, 8, 48, 128), BF), V((2, 8, 48, 128), BF),
            V((4, 8, 128), F32), V((8, 4, 8, 128), F32),
            V((L, 8, 3, 128, 128), BF), V((L, 8, 128, 128), BF), V((L, 8, 128, 512), BF), V((L, 8, 512, 128), BF),
            *[tuple(V((L, 4, 2, 4, 2 * rows, HALF), BF) for rows in ROWS) for _ in range(2)],
            *[tuple(V((L, 4, 4, 2 * rows, HALF), BF) for rows in ROWS) for _ in range(3)],
            V((L, 8, 3, 128, 128), BF), V((L, 8, 128, 128), BF), V((L, 8, 128, 512), BF), V((L, 8, 512, 128), BF),
            V((L, 8, 3, 128, 128), BF), V((L, 8, 128, 128), BF), V((L, 4, 2, 128, 512), BF), V((L, 2, 4, 512, 128), BF),
            V((L, 2, 128, 512), BF), V((L, 2, 128, 512), BF), V((L, 4, 512, 128), BF), V((L, 4, 512, 128), BF),
            V((L, 3, 128, 128), F32), V((L, 128, 128), F32), V((L, 128, 512), F32), V((L, 512, 128), F32),
            V((L, 3, 128, 128), F32), V((L, 128, 128), F32), V((L, 128, 512), F32), V((L, 512, 128), F32),
            V((TOK, D), F32), V((L, 2, TOK, D), F32), V((L, 2, TOK, 128), F32), V((L, 2, SEQ, SEQ), F32),
            V((L, 3, SEQ, 128), BF), V((L, SEQ, 128), BF), V((L, SEQ, 512), BF), V((L, SEQ, 512), F32),
            V((SEQ, 512), F32), V((SEQ, 512), BF), V((TOK, D), F32),
            V((L, 8, D), F32), V((L, 8, 128), F32),
            V((8, L, 8, 128), F32), V((8, L, 8, 128), F32), V((16, L, 8, 128), F32),
            V((8, L, 8, 128), F32), V((L, 8, 128), F32), V((L, 8, 128), F32),
            dma((10,)), dma((14,)), dma((2,)), dma((2,)), dma((2,)), dma((2,)), dma((2,)), dma((L, 4)), dma((L, 4)), dma((L, 4)), dma((L, 4)),
            dma((L, 4, N)), dma((L, 4, N, 4)), dma((L, 4, N)), dma((L, 4, N)), dma((L, 4, N, 4)), dma((L, 4, N)),
            dma((L, 4, N, 4)),
            dma((L, 4)), dma((L, 4)), dma((L, 2)), dma((L, 2)), dma((L, 4)), dma((L, 4)), dma((4,)), dma((4,)),
        ],
        compiler_params=pltpu.CompilerParams(collective_id=0, has_side_effects=True, vmem_limit_bytes=60 * 1024 * 1024),
        cost_estimate=pl.CostEstimate(flops=6 * 10**9, bytes_accessed=5 * 10**6, transcendentals=10**6),
    )(*operands)
    results = pl.pallas_call(
        finish,
        out_shape=out_shape,
        in_specs=[hbm] * 14,
        out_specs=(hbm,) * 14,
        scratch_shapes=[V(a.shape, a.dtype) for a in out_shape] + [dma((14,)), dma((14,))],
    )(*results)
    results = list(results)
    results[2] = results[2].transpose(0, 2, 1, 3)
    return tuple(results)


def solution(mesh):
    return jax.shard_map(
        on_device,
        mesh=mesh,
        in_specs=(
            P(("dp", "col"), "row"),
            P(None, "row"),
            P(None, "row"),
            P(None, "row", None, "col"),
            P(None, None, "col"),
            P(None, "col", "row"),
            P(None, "row"),
            P(None, "row"),
            P(None, "row"),
            P(None, "row", "col"),
            P(None, "col"),
            P(None, "col", "row"),
            P(None, "row"),
            P(("dp", "col"), "row"),
        ),
        out_specs=(
            P(("dp", "col"), "row"),
            P(("dp", "col"), "row"),
            P(None, "row", None, "col"),
            P(None, "col", "row"),
            P(None, "row", "col"),
            P(None, "col", "row"),
            P(None, "row"),
            P(None, "row"),
            P(None, None, "col"),
            P(None, "row"),
            P(None, "row"),
            P(None, "row"),
            P(None, "col"),
            P(None, "row"),
        ),
        check_vma=False,
    )
```

```python
import functools

import jax
import jax.numpy as jnp
from jax import lax
from jax.experimental import pallas as pl
from jax.experimental.pallas import tpu as pltpu
from jax.sharding import PartitionSpec as P

BF = jnp.bfloat16
F32 = jnp.float32
LAYERS = 2
GROUP = 8
TOK = 40
ROWS = (40,)
FIRST = (0,)
PARTS = (0,)
SEQ = 320
D = 1024
HALF = 512
HEAD_DIM = 64
EPS = 1e-6
ROOT_HALF = 0.7071067811865476
INV_ROOT_TAU = 0.3989422804014327
MESH = pl.DeviceIdType.MESH


def dot(a, b):
    return jnp.dot(a, b, preferred_element_type=F32)


def dot_last(a, b):
    return lax.dot_general(a, b, (((1,), (1,)), ((), ())), preferred_element_type=F32)


def dot_first(a, b):
    return lax.dot_general(a, b, (((0,), (0,)), ((), ())), preferred_element_type=F32)


def lanes(parts):
    return jnp.concatenate(parts, axis=1)


def kernel(
    images_h, gain1_h, bias1_h, wqkv, qvb_h, wout, outb_h, gain2_h, bias2_h, wup, upb_h, wdown, downb_h, cot_h,
    enc_h, gin_h, gqkv_h, gout_h, gup_h, gdown_h, gg1_h, gb1_h, gqv_h, gob_h, gg2_h, gb2_h, gub_h, gdb_h,
    images, gain1, bias1, qvb, outb, gain2, bias2, upb, downb, cot,
    enc_o, gin_o, gqkv_o, gout_o, gup_o, gdown_o, gg1_o, gb1_o, gqv_o, gob_o, gg2_o, gb2_o, gub_o, gdb_o,
    in_f, in_r, out_f, out_r,
    vec_s, vec_g, wq_g, wo_g, wu_g, wd_g,
    ag, rs_s, rs_b, rs_c, rs_r,
    gq_s, go_s, gu_s, gd_s, gq_r, go_r, gu_r, gd_r, gu_c, gu_f, gd_p, gd_q, gd_c, gd_f, sq, so, su, sd, tq, to, tu, td,
    stream, normal_k, scale_k, prob_k, qkv_k, mixed_k, hidden_k, slope_k, before_k, before_grad_k, grad_k,
    vacc, vcol, vs_s, vs_r, vh_r, vb_r, vt_s, vt_r,
    op_sem, res_sem, in_ss, in_rs, out_ss, out_rs, vec_sem, w_ss, w_rs, wf_ss, wf_rs,
    ag_ss, ag_rs, ag_fs, rs_bs, rs_br, rs_ss, rs_rs, g_ss, g_rs, gf_ss, gf_rs, x_ss, x_rs, v_ss, v_rs,
):
    core = lax.axis_index("dp")
    row = lax.axis_index("row")
    col = lax.axis_index("col")
    x = lax.div(col, 2)
    yh = lax.rem(col, 2)
    z = lax.div(row, 2)
    yl = lax.rem(row, 2)
    y = 2 * yh + yl
    t = 2 * x + core
    u = 4 * core + x
    sibling = (1 - core, row, col)

    def chip_dev(c):
        return (core, row, 2 * c + yh)

    def plane_dev(r):
        return (yh, r, 2 * x + core)

    def push(src, dst, ssem, rsem, dev):
        pltpu.make_async_remote_copy(
            src_ref=src, dst_ref=dst, send_sem=ssem, recv_sem=rsem, device_id=dev, device_id_type=MESH
        ).start()

    def drain(ref, sem):
        pltpu.make_async_copy(ref, ref, sem).wait()

    def fan(me, own, src, dst, ssem, rsem, dev):
        @pl.when(own)
        def _():
            pltpu.make_async_copy(src(me), dst, rsem).start()

        @pl.when(jnp.logical_not(own))
        def _():
            push(src(me), dst, ssem, rsem, dev(me))

        @pl.loop(1, GROUP)
        def _(k):
            j = lax.rem(me + k, GROUP)
            push(src(j), dst, ssem, rsem, dev(j))

    def fan_sent(own, ref, ssem):
        @pl.when(own)
        def _():
            drain(ref.at[pl.ds(0, GROUP - 1)], ssem)

        @pl.when(jnp.logical_not(own))
        def _():
            drain(ref, ssem)

    own_plane = yh == core
    own_tile = row == t
    place = 2 * col + core

    def tile_dev(j):
        return (lax.div(j, 4), t, 2 * lax.rem(j, 4) + yh)

    def back_dev(r):
        return (lax.rem(row, 2), r, 2 * lax.div(row, 2) + yh)

    def y_dev(k):
        other = lax.rem(y + k, 4)
        return (core, 2 * z + lax.rem(other, 2), 2 * x + lax.div(other, 2))

    def z_at(k):
        return lax.rem(z + k, 4)

    def z_dev(k):
        return (core, 2 * z_at(k) + yl, col)

    def row_dev(j):
        return (lax.rem(j, 2), row, lax.div(j, 2))

    barrier = pltpu.get_barrier_semaphore()

    def greet(me, own, dev):
        @pl.when(jnp.logical_not(own))
        def _():
            pl.semaphore_signal(barrier, inc=1, device_id=dev(me), device_id_type=MESH)

        @pl.loop(1, GROUP)
        def _(k):
            pl.semaphore_signal(barrier, inc=1, device_id=dev(lax.rem(me + k, GROUP)), device_id_type=MESH)

    greet(u, own_tile, tile_dev)
    greet(row, own_tile, back_dev)
    greet(row, own_plane, plane_dev)
    for k in (1, 2, 3):
        pl.semaphore_signal(barrier, inc=1, device_id=y_dev(k), device_id_type=MESH)
        pl.semaphore_signal(barrier, inc=1, device_id=z_dev(k), device_id_type=MESH)

    @pl.loop(1, 2 * GROUP)
    def _(k):
        pl.semaphore_signal(barrier, inc=1, device_id=row_dev(lax.rem(place + k, 2 * GROUP)), device_id_type=MESH)

    small = (
        (images_h, images), (gain1_h, gain1), (bias1_h, bias1), (outb_h, outb), (gain2_h, gain2), (bias2_h, bias2),
        (downb_h, downb), (qvb_h, qvb), (upb_h, upb), (cot_h, cot),
    )
    fetches = [pltpu.make_async_copy(src, dst, op_sem.at[n]) for n, (src, dst) in enumerate(small)]
    for fetch in fetches:
        fetch.start()

    def tiles_fold(n, ref):
        in_f[n, :, 0:TOK] = ref[...].astype(F32).reshape(GROUP, TOK, 128).astype(BF)

    def tiles_in(n):
        fan(u, own_tile, lambda j: in_f.at[n, j], in_r.at[n, row], in_ss.at[n], in_rs.at[n], tile_dev)

    def tiles_read(ref, n):
        whole = ref[n].astype(F32)
        return [whole[r, 0:TOK] for r in range(GROUP)]

    in_f[...] = jnp.zeros_like(in_f)
    out_f[...] = jnp.zeros_like(out_f)
    fetches[0].wait()
    tiles_fold(0, images)

    greeted = 3 * GROUP + 6 + 2 * GROUP - 1
    pl.semaphore_wait(barrier, greeted - jnp.where(own_plane, 1, 0) - jnp.where(own_tile, 2, 0))
    tiles_in(0)

    for fetch in fetches[1:9]:
        fetch.wait()
    vec_s[...] = jnp.zeros_like(vec_s)
    for l in range(LAYERS):
        for i, ref in enumerate((gain1, bias1, outb, gain2, bias2, downb)):
            vec_s[l, i : i + 1, :] = ref[l : l + 1, :]
        vec_s[2 + l, 0:2, :] = qvb[l]
        for j in range(4):
            vec_s[2 + l, 2 + j : 3 + j, :] = upb[l : l + 1, 128 * j : 128 * j + 128]
    fan(row, own_plane, lambda j: vec_s, vec_g.at[row], vec_sem.at[0], vec_sem.at[1], plane_dev)

    weights = ((wqkv, wq_g), (wout, wo_g), (wup, wu_g), (wdown, wd_g))

    def y_first(m):
        return m in (0, 3)

    def weight_slot(m, r):
        return r if y_first(m) else 4 * (r % 2) + r // 2

    def qkv_in(l):
        fan(row, own_plane, lambda j: wqkv.at[l], wq_g.at[l, row], w_ss.at[l, 0], w_rs.at[l, 0], plane_dev)

    def weights_in(l):
        @pl.when(own_plane)
        def _():
            for m in (1, 2, 3):
                src, dst = weights[m]
                block = dst.at[l, row if y_first(m) else 4 * yl + z]
                pltpu.make_async_copy(src.at[l], block, w_rs.at[l, m]).start()
                for k in (2, 1, 3):
                    push(src.at[l], block, w_ss.at[l, m], w_rs.at[l, m], (y_dev if y_first(m) else z_dev)(k))

    def weights_relay(l, m):
        dst = weights[m][1]
        if m == 3:
            pair = dst.at[l, pl.ds(2 * z, 2)]
            drain(pair, w_rs.at[l, m])
            for k in (2, 1, 3):
                push(pair, pair, wf_ss.at[l, m], wf_rs.at[l, m], z_dev(k))
        else:

            @pl.when(own_plane)
            def _():
                four = dst.at[l, pl.ds(4 * yl, 4)]
                drain(four, w_rs.at[l, m])
                for k in (2, 1, 3):
                    push(four, four, wf_ss.at[l, m], wf_rs.at[l, m], y_dev(k))

    def weight_wait(l, m):
        dst = weights[m][1]
        if m == 0:
            drain(dst.at[l], w_rs.at[l, m])
        elif m == 3:
            drain(dst.at[l, pl.ds(0, 6)], wf_rs.at[l, m])
        else:

            @pl.when(own_plane)
            def _():
                drain(dst.at[l, pl.ds(0, 4)], wf_rs.at[l, m])

            @pl.when(jnp.logical_not(own_plane))
            def _():
                drain(dst.at[l], wf_rs.at[l, m])

    def weights_sent(l, m):
        dst = weights[m][1]
        if m == 0:
            fan_sent(own_plane, dst.at[l], w_ss.at[l, m])
            return

        @pl.when(own_plane)
        def _():
            drain(dst.at[l, pl.ds(0, 3)], w_ss.at[l, m])

        if m == 3:
            drain(dst.at[l, pl.ds(0, 6)], wf_ss.at[l, m])
        else:

            @pl.when(own_plane)
            def _():
                drain(dst.at[:, pl.ds(0, 6)], wf_ss.at[l, m])

    weights_in(0)
    qkv_in(0)

    def chip_at(k):
        return lax.rem(x + k, 4)

    def own_rows(p):
        return slice(FIRST[p], FIRST[p] + ROWS[p])

    def all_rows(p):
        return slice(GROUP * FIRST[p], GROUP * (FIRST[p] + ROWS[p]))

    def gather_start(l, s, p, value):
        folded = jnp.concatenate([value[:, :HALF], value[:, HALF:]], axis=0).astype(BF)
        ag[p][l, s, core, x] = folded
        mine = ag[p].at[l, s, core, x]
        for k in (2, 1, 3):
            push(mine, mine, ag_ss.at[l, s, p], ag_rs.at[l, s, p, k], chip_dev(chip_at(k)))
        push(mine, mine, ag_fs.at[l, s, p], ag_rs.at[l, s, p, 0], sibling)

    def gather_wait(l, s, p):
        for k in (1, 3, 2):
            came = ag[p].at[l, s, core, chip_at(4 - k)]
            drain(came, ag_rs.at[l, s, p, k])
            push(came, came, ag_fs.at[l, s, p], ag_rs.at[l, s, p, 0], sibling)
        drain(ag[p].at[l, s, 0], ag_rs.at[l, s, p, 0])

    def gather_read(l, s, p):
        rows = ROWS[p]
        whole = ag[p][l, s].astype(F32).reshape(GROUP, 2 * rows, HALF)
        left = whole[:, :rows].reshape(GROUP * rows, HALF).astype(BF)
        right = whole[:, rows:].reshape(GROUP * rows, HALF).astype(BF)
        return left, right

    def gather_whole(l, s):
        parts = [gather_read(l, s, p) for p in PARTS]
        return [jnp.concatenate([part[h] for part in parts], axis=0) for h in range(2)]

    def scatter_start(l, s, p, left, right):
        rows = ROWS[p]
        both = jnp.concatenate([left.reshape(GROUP, rows, HALF), right.reshape(GROUP, rows, HALF)], axis=1)
        rs_s[p][l, s] = both.astype(BF).reshape(2, 4, 2 * rows, HALF)
        for k in (2, 1, 3, 0):
            c = chip_at(k)
            push(rs_s[p].at[l, s, 1 - core, c], rs_b[p].at[l, s, c], rs_bs.at[l, s, p], rs_br.at[l, s, p, k], sibling)

    def pair_sum(l, s, p, k):
        c = chip_at(k)
        drain(rs_b[p].at[l, s, c], rs_br.at[l, s, p, k])
        return rs_s[p][l, s, core, c].astype(F32) + rs_b[p][l, s, c].astype(F32)

    def scatter_relay(l, s, p):
        for k in (2, 1, 3):
            rs_c[p][l, s, k] = pair_sum(l, s, p, k).astype(BF)
            push(rs_c[p].at[l, s, k], rs_r[p].at[l, s, k], rs_ss.at[l, s, p], rs_rs.at[l, s, p, k], chip_dev(chip_at(k)))

    def scatter_wait(l, s, p):
        rows = ROWS[p]
        total = pair_sum(l, s, p, 0)
        for k in (1, 3, 2):
            drain(rs_r[p].at[l, s, k], rs_rs.at[l, s, p, k])
            total += rs_r[p][l, s, k].astype(F32)
        return lanes([total[:rows], total[rows:]])

    def vec_row(l, i):
        return lanes([vec_g[r, l, i : i + 1, :] for r in range(GROUP)])

    def norm_forward(l, s, p, value):
        center = jnp.mean(value, axis=1, keepdims=True)
        shifted = value - center
        scaled = lax.rsqrt(jnp.mean(shifted * shifted, axis=1, keepdims=True) + EPS)
        normal = shifted * scaled
        normal_k[l, s, own_rows(p)] = normal
        scale_k[l, s, own_rows(p)] = jnp.broadcast_to(scaled, (ROWS[p], 128))
        return normal * vec_row(l, 3 * s) + vec_row(l, 3 * s + 1)

    def add_row(l, i, value):
        vacc[l, i : i + 1, :] += jnp.sum(value, axis=0, keepdims=True)

    def norm_backward(l, s, p, grad_out):
        normal = normal_k[l, s, own_rows(p)]
        scaled = scale_k[l, s, own_rows(p)][:, 0:1]
        add_row(l, 3 * s, grad_out * normal)
        add_row(l, 3 * s + 1, grad_out)
        upstream = grad_out * vec_row(l, 3 * s)
        mean_part = jnp.mean(upstream, axis=1, keepdims=True)
        proj_part = jnp.mean(upstream * normal, axis=1, keepdims=True)
        return scaled * (upstream - mean_part - normal * proj_part)

    def qkv_half(l, h):
        return jnp.concatenate([lanes([wq_g[l, weight_slot(0, 4 * h + r), j] for j in range(3)]) for r in range(4)], axis=0)

    def out_half(l, h):
        return lanes([wo_g[l, weight_slot(1, 4 * h + r)] for r in range(4)])

    def up_half(l, h):
        return jnp.concatenate([wu_g[l, weight_slot(2, 4 * h + r)] for r in range(4)], axis=0)

    def down_half(l, h):
        return lanes([wd_g[l, weight_slot(3, 4 * h + r)] for r in range(4)])

    def head_mask(h):
        lane = lax.broadcasted_iota(jnp.int32, (SEQ, 128), 1)
        return (lane < HEAD_DIM) if h == 0 else (lane >= HEAD_DIM)

    def pick(pair):
        return jnp.where(head_mask(0), pair[0], pair[1])

    def only(h, value):
        return jnp.where(head_mask(h), value, jnp.zeros_like(value))

    drain(in_r.at[0], in_rs.at[0])
    stream[...] = lanes(tiles_read(in_r, 0))
    drain(vec_g, vec_sem.at[1])
    for p in PARTS:
        gather_start(0, 0, p, norm_forward(0, 0, p, stream[own_rows(p)]))
    for m in (1, 2, 3):
        weights_relay(0, m)
    fetches[9].wait()
    tiles_fold(1, cot)
    tiles_in(1)

    def hidden_part(l, p):
        left, right = gather_read(l, 1, p)
        before = dot(left, up_half(l, 0)) + dot(right, up_half(l, 1))
        shift = vec_g[0, 2 + l]
        before = before + lanes([shift[2 + j : 3 + j] for j in range(4)])
        phi = 0.5 * (1.0 + lax.erf(before * ROOT_HALF))
        hidden = (before * phi).astype(BF)
        hidden_k[l, all_rows(p)] = hidden
        before_k[all_rows(p)] = before
        slope_k[l, all_rows(p)] = phi
        if p == 0:
            weight_wait(l, 3)
        scatter_start(l, 1, p, dot(hidden, down_half(l, 0)), dot(hidden, down_half(l, 1)))

    @pl.loop(0, LAYERS)
    def _(l):
        for p in PARTS:
            gather_wait(l, 0, p)
            left, right = gather_read(l, 0, p)
            if p == 0:
                weight_wait(l, 0)
            projected = dot(left, qkv_half(l, 0)) + dot(right, qkv_half(l, 1))
            shift = vec_g[0, 2 + l]
            qkv_k[l, 0, all_rows(p)] = (projected[:, :128] + shift[0:1]).astype(BF)
            qkv_k[l, 1, all_rows(p)] = projected[:, 128:256].astype(BF)
            qkv_k[l, 2, all_rows(p)] = (projected[:, 256:] + shift[1:2]).astype(BF)
        query = qkv_k[l, 0]
        keys = qkv_k[l, 1]
        values = qkv_k[l, 2]
        mixed = []
        for h in range(2):
            scores = dot_last(only(h, query), keys) * HEAD_DIM ** -0.5
            raised = jnp.exp(scores - jnp.max(scores, axis=1, keepdims=True))
            probs = raised / jnp.sum(raised, axis=1, keepdims=True)
            prob_k[l, h] = probs
            mixed.append(dot(probs.astype(BF), values))
        mixed = pick(mixed).astype(BF)
        mixed_k[l] = mixed
        weight_wait(l, 1)
        for p in PARTS:
            part = mixed[all_rows(p)]
            scatter_start(l, 0, p, dot(part, out_half(l, 0)), dot(part, out_half(l, 1)))
        for p in PARTS:
            scatter_relay(l, 0, p)
        @pl.when(l == 0)
        def _():
            weights_in(1)
            qkv_in(1)

        for p in PARTS:
            middle = stream[own_rows(p)] + vec_row(l, 2) + scatter_wait(l, 0, p)
            stream[own_rows(p)] = middle
            gather_start(l, 1, p, norm_forward(l, 1, p, middle))
        for p in PARTS:
            gather_wait(l, 1, p)
            if p == 0:
                weight_wait(l, 2)
            else:
                scatter_relay(l, 1, p - 1)
            hidden_part(l, p)
        scatter_relay(l, 1, PARTS[-1])

        @pl.when(l == 0)
        def _():
            for m in (1, 2, 3):
                weights_relay(1, m)
            drain(in_r.at[1], in_rs.at[1])
            grad_k[...] = lanes(tiles_read(in_r, 1))
            for p in PARTS:
                gather_start(LAYERS - 1, 2, p, grad_k[own_rows(p)])

        before = before_k[...]
        slope_k[l] = slope_k[l] + before * INV_ROOT_TAU * jnp.exp(-0.5 * before * before)

        @pl.when(l == 0)
        def _():
            for p in PARTS:
                value = stream[own_rows(p)] + vec_row(0, 5) + scatter_wait(0, 1, p)
                stream[own_rows(p)] = value
                gather_start(1, 0, p, norm_forward(1, 0, p, value))

    def tiles_out(n, value):
        for r in range(GROUP):
            out_f[n, r, 0:TOK] = value[:, 128 * r : 128 * r + 128].astype(BF)
        fan(row, own_tile, lambda j: out_f.at[n, j], out_r.at[n, u], out_ss.at[n], out_rs.at[n], back_dev)

    vacc[...] = jnp.zeros_like(vacc)
    vcol[...] = jnp.zeros_like(vcol)

    grads = (
        (gq_s, gq_r, sq, tq, gqkv_o, gqkv_h), (go_s, go_r, so, to, gout_o, gout_h),
        (gu_s, gu_r, su, tu, gup_o, gup_h), (gd_s, gd_r, sd, td, gdown_o, gdown_h),
    )

    def grad_slot(m, r):
        return 4 * (r % 2) + r // 2 if m == 3 else r

    def pair_fan(src, dst, ssem, rsem):
        def dev(j):
            return plane_dev(2 * z + j)

        @pl.when(own_plane)
        def _():
            pltpu.make_async_copy(src(yl), dst, rsem).start()

        @pl.when(jnp.logical_not(own_plane))
        def _():
            push(src(yl), dst, ssem, rsem, dev(yl))

        push(src(1 - yl), dst, ssem, rsem, dev(1 - yl))

    def grads_out(l, m):
        src, dst = grads[m][:2]
        if m == 2:
            for k in (2, 1, 3):
                push(src.at[l, pl.ds(2 * z_at(k), 2)], dst.at[l, k], g_ss.at[l, m], g_rs.at[l, m], z_dev(k))
        elif m == 3:
            pair_fan(lambda j: src.at[l, pl.ds(4 * j, 4)], dst.at[l, yl], g_ss.at[l, m], g_rs.at[l, m])
        else:
            fan(row, own_plane, lambda j: src.at[l, j], dst.at[l, row], g_ss.at[l, m], g_rs.at[l, m], plane_dev)

    def up_relay(l):
        drain(gu_r.at[l, pl.ds(1, 3)], g_rs.at[l, 2])
        for j in range(2):
            total = gu_s[l, 2 * z + j].astype(F32)
            for k in (1, 2, 3):
                total += gu_r[l, k, j].astype(F32)
            gu_c[l, j] = total.astype(BF)
        pair_fan(lambda j: gu_c.at[l, j], gu_f.at[l, yl], gf_ss.at[l, 0], gf_rs.at[l, 0])

    keeper = lax.div(z, 2) == core

    def down_pair(l):
        drain(gd_r.at[l], g_rs.at[l, 3])
        for j in range(2):
            theirs = 2 * (1 - core) + j
            gd_p[l, j] = (gd_r[l, 0, theirs].astype(F32) + gd_r[l, 1, theirs].astype(F32)).astype(BF)
        push(gd_p.at[l], gd_q.at[l], gf_ss.at[l, 2], gf_rs.at[l, 2], sibling)

    def down_relay(l):
        drain(gd_q.at[l], gf_rs.at[l, 2])
        for j in range(2):
            ours = 2 * core + j
            total = gd_r[l, 0, ours].astype(F32) + gd_r[l, 1, ours].astype(F32) + gd_q[l, j].astype(F32)
            gd_c[l, j] = total.astype(BF)

            @pl.when(ours != z)
            def _():
                push(gd_c.at[l, j], gd_f.at[l, z], gf_ss.at[l, 1], gf_rs.at[l, 1], (core, 2 * ours + yl, col))

        @pl.when(keeper)
        def _():
            gd_f[l, z] = gd_c[l, lax.rem(z, 2)]

    def pair_sent(ref, ssem):
        @pl.when(own_plane)
        def _():
            drain(ref.at[0], ssem)

        @pl.when(jnp.logical_not(own_plane))
        def _():
            drain(ref, ssem)

    def grads_sent(l, m):
        src, dst = grads[m][:2]
        if m == 2:
            drain(dst.at[l, pl.ds(1, 3)], g_ss.at[l, m])
            pair_sent(gu_c.at[l], gf_ss.at[l, 0])
        elif m == 3:
            pair_sent(dst.at[l], g_ss.at[l, m])
            drain(gd_q.at[l], gf_ss.at[l, 2])

            @pl.when(keeper)
            def _():
                drain(gd_c.at[l, 0], gf_ss.at[l, 1])

            @pl.when(jnp.logical_not(keeper))
            def _():
                drain(gd_c.at[l], gf_ss.at[l, 1])
        else:
            fan_sent(own_plane, src.at[l], g_ss.at[l, m])

    def sum_terms(l, m):
        src, dst, part, other = grads[m][:4]
        if m == 2:
            drain(gu_f.at[l], gf_rs.at[l, 0])
            total = gu_f[l, 0].astype(F32) + gu_f[l, 1].astype(F32)
        elif m == 3:

            @pl.when(keeper)
            def _():
                drain(gd_f.at[l, pl.ds(0, 3)], gf_rs.at[l, 1])
                part[l] = jnp.sum(gd_f[l].astype(F32), axis=0)
                push(part.at[l], other.at[l], x_ss.at[l, m], x_rs.at[l, m], sibling)

            return
        else:
            drain(dst.at[l], g_rs.at[l, m])
            total = dst[l, 0].astype(F32)
            for r in range(1, GROUP):
                total += dst[l, r].astype(F32)
        part[l] = total
        push(part.at[l], other.at[l], x_ss.at[l, m], x_rs.at[l, m], sibling)

    def hidden_back(l, p):
        left, right = gather_read(l, 2, p)
        hidden_grad = dot_last(left, down_half(l, 0)) + dot_last(right, down_half(l, 1))
        before_grad = (hidden_grad * slope_k[l, all_rows(p)]).astype(BF)
        before_grad_k[all_rows(p)] = before_grad
        scatter_start(l, 2, p, dot_last(before_grad, up_half(l, 0)), dot_last(before_grad, up_half(l, 1)))

    @pl.loop(0, LAYERS)
    def _(step):
        l = LAYERS - 1 - step
        add_row(l, 5, grad_k[...].astype(BF).astype(F32))
        for p in PARTS:
            gather_wait(l, 2, p)
            if p > 0:
                scatter_relay(l, 2, p - 1)
            hidden_back(l, p)
        scatter_relay(l, 2, PARTS[-1])
        before_grad = before_grad_k[...]
        for h, part in enumerate(gather_whole(l, 2)):
            product = dot_first(hidden_k[l], part).astype(BF)
            for r in range(4):
                gd_s[l, grad_slot(3, 4 * h + r)] = product[:, 128 * r : 128 * r + 128]
        grads_out(l, 3)
        for h, part in enumerate(gather_whole(l, 1)):
            gu_s[l, 4 * h : 4 * h + 4] = dot_first(part, before_grad).astype(BF).reshape(4, 128, 512)
        grads_out(l, 2)
        for p in PARTS:
            grad_mid = grad_k[own_rows(p)] + norm_backward(l, 1, p, scatter_wait(l, 2, p))
            grad_k[own_rows(p)] = grad_mid
            gather_start(l, 3, p, grad_mid)
        sums = jnp.sum(before_grad.astype(F32), axis=0, keepdims=True)
        for j in range(4):
            vcol[l, 2 + j : 3 + j, :] = sums[:, 128 * j : 128 * j + 128]
        add_row(l, 2, grad_k[...].astype(BF).astype(F32))

        @pl.when(step == 0)
        def _():
            for p in PARTS:
                stream[own_rows(p)] = stream[own_rows(p)] + vec_row(LAYERS - 1, 5) + scatter_wait(LAYERS - 1, 1, p)
            tiles_out(0, stream[...])

        mixed_grad = []
        for p in PARTS:
            gather_wait(l, 3, p)
            left, right = gather_read(l, 3, p)
            mixed_grad.append((dot_last(left, out_half(l, 0)) + dot_last(right, out_half(l, 1))).astype(BF))
        mixed_grad = jnp.concatenate(mixed_grad, axis=0)
        query = qkv_k[l, 0]
        keys = qkv_k[l, 1]
        values = qkv_k[l, 2]

        def out_terms():
            for h, part in enumerate(gather_whole(l, 3)):
                product = dot_first(mixed_k[l], part).astype(BF)
                for r in range(4):
                    go_s[l, 4 * h + r] = product[:, 128 * r : 128 * r + 128]
            grads_out(l, 1)

        def qkv_term(j, value):
            for h, part in enumerate(gather_whole(l, 0)):
                product = dot_first(part, value).astype(BF)
                for r in range(4):
                    gq_s[l, 4 * h + r, j] = product[128 * r : 128 * r + 128]
            fan(
                row, own_plane, lambda r: gq_s.at[l, r, j], gq_r.at[l, row, j], g_ss.at[l, 0], g_rs.at[l, 0], plane_dev
            )

        values_grad = pick([dot_first(prob_k[l, h].astype(BF), mixed_grad) for h in range(2)]).astype(BF)

        @pl.when(l == 0)
        def _():
            out_terms()
            qkv_term(2, values_grad)

        query_grads, key_grads = [], []
        for h in range(2):
            probs = prob_k[l, h]
            probs_grad = dot_last(only(h, mixed_grad), values)
            inner = jnp.sum(probs * probs_grad, axis=1, keepdims=True)
            scores_grad = (probs * (probs_grad - inner)).astype(BF)
            query_grads.append(dot(scores_grad, keys))
            key_grads.append(dot_first(scores_grad, query))
        query_grad = (pick(query_grads) * HEAD_DIM ** -0.5).astype(BF)
        keys_grad = (pick(key_grads) * HEAD_DIM ** -0.5).astype(BF)

        @pl.when(l == 0)
        def _():
            qkv_term(0, query_grad)
            qkv_term(1, keys_grad)

        joined = lanes([query_grad, keys_grad, values_grad])
        for p in PARTS:
            part = joined[all_rows(p)]
            scatter_start(l, 3, p, dot_last(part, qkv_half(l, 0)), dot_last(part, qkv_half(l, 1)))
        for p in PARTS:
            scatter_relay(l, 3, p)
        down_pair(l)
        up_relay(l)
        down_relay(l)

        @pl.when(l != 0)
        def _():
            qkv_term(0, query_grad)
            qkv_term(1, keys_grad)
            qkv_term(2, values_grad)
            out_terms()

        vcol[l, 0:1, :] = jnp.sum(query_grad.astype(F32), axis=0, keepdims=True)
        vcol[l, 1:2, :] = jnp.sum(values_grad.astype(F32), axis=0, keepdims=True)

        @pl.when(l == 0)
        def _():
            fan(row, own_plane, lambda j: vcol, vb_r.at[row], v_ss.at[1], v_rs.at[1], plane_dev)
            for m in (3, 2, 0, 1):
                sum_terms(1, m)

        for p in PARTS:
            grad_k[own_rows(p)] = grad_k[own_rows(p)] + norm_backward(l, 0, p, scatter_wait(l, 3, p))

            @pl.when(l > 0)
            def _():
                gather_start(l - 1, 2, p, grad_k[own_rows(p)])

    tiles_out(1, grad_k[...])

    for j in range(GROUP):
        vs_s[j] = vacc[:, :, 128 * j : 128 * j + 128]
    fan(row, own_plane, lambda j: vs_s.at[j], vs_r.at[row], v_ss.at[0], v_rs.at[0], plane_dev)

    results = []

    def result(src, dst):
        copy = pltpu.make_async_copy(src, dst, res_sem.at[len(results)])
        copy.start()
        results.append(copy)

    drain(out_r.at[0], out_rs.at[0])
    enc_o[...] = out_r[0].astype(F32)[:, 0:TOK].reshape(SEQ, 128).astype(BF)
    result(enc_o, enc_h)

    drain(vb_r, v_rs.at[1])
    vt_s[...] = jnp.sum(vb_r[...], axis=0)
    push(vt_s, vt_r, v_ss.at[2], v_rs.at[2], sibling)

    for m in (3, 2):
        sum_terms(0, m)

    drain(vs_r, v_rs.at[0])
    vh_r[place] = jnp.sum(vs_r[...], axis=0)

    @pl.loop(1, 2 * GROUP)
    def _(k):
        push(vh_r.at[place], vh_r.at[place], v_ss.at[3], v_rs.at[3], row_dev(lax.rem(place + k, 2 * GROUP)))

    for m in (0, 1):
        sum_terms(0, m)

    drain(vt_r, v_rs.at[2])
    columns = vt_s[...] + vt_r[...]
    for l in range(LAYERS):
        gqv_o[l] = columns[l, 0:2]
        for j in range(4):
            gub_o[l : l + 1, 128 * j : 128 * j + 128] = columns[l, 2 + j : 3 + j]
    result(gqv_o, gqv_h)
    result(gub_o, gub_h)

    drain(out_r.at[1], out_rs.at[1])
    gin_o[...] = out_r[1].astype(F32)[:, 0:TOK].reshape(SEQ, 128)
    result(gin_o, gin_h)

    for m in (3, 2, 0, 1):
        part, other, out, out_hbm = grads[m][2:]
        for l in (1, 0):
            if m == 3:

                @pl.when(keeper)
                def _():
                    out[l] = part[l]

                @pl.when(jnp.logical_not(keeper))
                def _():
                    drain(other.at[l], x_rs.at[l, m])
                    out[l] = other[l]
            else:
                drain(other.at[l], x_rs.at[l, m])
                out[l] = part[l] + other[l]
        result(out, out_hbm)

    drain(vh_r.at[pl.ds(0, 2 * GROUP - 1)], v_rs.at[3])
    rows = jnp.sum(vh_r[...], axis=0)
    for i, (ref, out_hbm) in enumerate(
        ((gg1_o, gg1_h), (gb1_o, gb1_h), (gob_o, gob_h), (gg2_o, gg2_h), (gb2_o, gb2_h), (gdb_o, gdb_h))
    ):
        for l in range(LAYERS):
            ref[l : l + 1, :] = rows[l, i : i + 1, :]
        result(ref, out_hbm)

    for n in range(2):
        fan_sent(own_tile, in_f.at[n], in_ss.at[n])
        fan_sent(own_tile, out_f.at[n], out_ss.at[n])
    fan_sent(own_plane, vec_g, vec_sem.at[0])
    fan_sent(own_plane, vb_r, v_ss.at[1])
    fan_sent(own_plane, vs_s, v_ss.at[0])
    drain(vt_s, v_ss.at[2])
    drain(vh_r.at[pl.ds(0, 2 * GROUP - 1)], v_ss.at[3])

    @pl.loop(0, LAYERS)
    def _(l):
        for m in range(4):
            weights_sent(l, m)
            grads_sent(l, m)
            if m == 3:

                @pl.when(keeper)
                def _():
                    drain(grads[m][2].at[l], x_ss.at[l, m])
            else:
                drain(grads[m][2].at[l], x_ss.at[l, m])
        for s in range(4):
            for p in PARTS:
                drain(ag[p].at[l, s, 0, pl.ds(0, 3)], ag_ss.at[l, s, p])
                drain(ag[p].at[l, s, 0], ag_fs.at[l, s, p])
                drain(rs_b[p].at[l, s], rs_bs.at[l, s, p])
                drain(rs_c[p].at[l, s, pl.ds(1, 3)], rs_ss.at[l, s, p])

    for copy in results:
        copy.wait()


def finish(*refs):
    count = (len(refs) - 2) // 3
    ins, outs, held = refs[:count], refs[count : 2 * count], refs[2 * count : 3 * count]
    in_sem, out_sem = refs[3 * count :]
    loads = [pltpu.make_async_copy(ins[n], held[n], in_sem.at[n]) for n in range(count)]
    stores = [pltpu.make_async_copy(held[n], outs[n], out_sem.at[n]) for n in range(count)]
    for copy in loads:
        copy.start()
    for load, store in zip(loads, stores):
        load.wait()
        store.start()
    for copy in stores:
        copy.wait()


def on_device(images, gain1, bias1, wqkv, qvb, wout, outb, gain2, bias2, wup, upb, wdown, downb, cot):
    L = LAYERS
    N = len(PARTS)
    wqkv = wqkv.transpose(0, 2, 1, 3)
    hbm = pl.BlockSpec(memory_space=pl.ANY)
    shape = jax.ShapeDtypeStruct
    dma = pltpu.SemaphoreType.DMA
    V = pltpu.VMEM
    out_shape = (
        shape((SEQ, 128), BF),
        shape((SEQ, 128), F32),
        shape((L, 3, 128, 128), F32),
        shape((L, 128, 128), F32),
        shape((L, 128, 512), F32),
        shape((L, 512, 128), F32),
        shape((L, 128), F32),
        shape((L, 128), F32),
        shape((L, 2, 128), F32),
        shape((L, 128), F32),
        shape((L, 128), F32),
        shape((L, 128), F32),
        shape((L, 512), F32),
        shape((L, 128), F32),
    )
    operands = (images, gain1, bias1, wqkv, qvb, wout, outb, gain2, bias2, wup, upb, wdown, downb, cot)
    staged = [V(a.shape, a.dtype) for a in (images, gain1, bias1, qvb, outb, gain2, bias2, upb, downb, cot)]
    results = pl.pallas_call(
        kernel,
        out_shape=out_shape,
        in_specs=[hbm] * 14,
        out_specs=(hbm,) * 14,
        scratch_shapes=staged + [V(a.shape, a.dtype) for a in out_shape] + [
            V((2, 8, 48, 128), BF), V((2, 8, 48, 128), BF), V((2, 8, 48, 128), BF), V((2, 8, 48, 128), BF),
            V((4, 8, 128), F32), V((8, 4, 8, 128), F32),
            V((L, 8, 3, 128, 128), BF), V((L, 8, 128, 128), BF), V((L, 8, 128, 512), BF), V((L, 8, 512, 128), BF),
            *[tuple(V((L, 4, 2, 4, 2 * rows, HALF), BF) for rows in ROWS) for _ in range(2)],
            *[tuple(V((L, 4, 4, 2 * rows, HALF), BF) for rows in ROWS) for _ in range(3)],
            V((L, 8, 3, 128, 128), BF), V((L, 8, 128, 128), BF), V((L, 8, 128, 512), BF), V((L, 8, 512, 128), BF),
            V((L, 8, 3, 128, 128), BF), V((L, 8, 128, 128), BF), V((L, 4, 2, 128, 512), BF), V((L, 2, 4, 512, 128), BF),
            V((L, 2, 128, 512), BF), V((L, 2, 128, 512), BF), V((L, 2, 512, 128), BF), V((L, 2, 512, 128), BF),
            V((L, 2, 512, 128), BF), V((L, 4, 512, 128), BF),
            V((L, 3, 128, 128), F32), V((L, 128, 128), F32), V((L, 128, 512), F32), V((L, 512, 128), F32),
            V((L, 3, 128, 128), F32), V((L, 128, 128), F32), V((L, 128, 512), F32), V((L, 512, 128), F32),
            V((TOK, D), F32), V((L, 2, TOK, D), F32), V((L, 2, TOK, 128), F32), V((L, 2, SEQ, SEQ), F32),
            V((L, 3, SEQ, 128), BF), V((L, SEQ, 128), BF), V((L, SEQ, 512), BF), V((L, SEQ, 512), F32),
            V((SEQ, 512), F32), V((SEQ, 512), BF), V((TOK, D), F32),
            V((L, 8, D), F32), V((L, 8, 128), F32),
            V((8, L, 8, 128), F32), V((8, L, 8, 128), F32), V((16, L, 8, 128), F32),
            V((8, L, 8, 128), F32), V((L, 8, 128), F32), V((L, 8, 128), F32),
            dma((10,)), dma((14,)), dma((2,)), dma((2,)), dma((2,)), dma((2,)), dma((2,)), dma((L, 4)), dma((L, 4)), dma((L, 4)), dma((L, 4)),
            dma((L, 4, N)), dma((L, 4, N, 4)), dma((L, 4, N)), dma((L, 4, N)), dma((L, 4, N, 4)), dma((L, 4, N)),
            dma((L, 4, N, 4)),
            dma((L, 4)), dma((L, 4)), dma((L, 3)), dma((L, 3)), dma((L, 4)), dma((L, 4)), dma((4,)), dma((4,)),
        ],
        compiler_params=pltpu.CompilerParams(collective_id=0, has_side_effects=True, vmem_limit_bytes=60 * 1024 * 1024),
        cost_estimate=pl.CostEstimate(flops=6 * 10**9, bytes_accessed=5 * 10**6, transcendentals=10**6),
    )(*operands)
    results = pl.pallas_call(
        finish,
        out_shape=out_shape,
        in_specs=[hbm] * 14,
        out_specs=(hbm,) * 14,
        scratch_shapes=[V(a.shape, a.dtype) for a in out_shape] + [dma((14,)), dma((14,))],
    )(*results)
    results = list(results)
    results[2] = results[2].transpose(0, 2, 1, 3)
    return tuple(results)


def solution(mesh):
    return jax.shard_map(
        on_device,
        mesh=mesh,
        in_specs=(
            P(("dp", "col"), "row"),
            P(None, "row"),
            P(None, "row"),
            P(None, "row", None, "col"),
            P(None, None, "col"),
            P(None, "col", "row"),
            P(None, "row"),
            P(None, "row"),
            P(None, "row"),
            P(None, "row", "col"),
            P(None, "col"),
            P(None, "col", "row"),
            P(None, "row"),
            P(("dp", "col"), "row"),
        ),
        out_specs=(
            P(("dp", "col"), "row"),
            P(("dp", "col"), "row"),
            P(None, "row", None, "col"),
            P(None, "col", "row"),
            P(None, "row", "col"),
            P(None, "col", "row"),
            P(None, "row"),
            P(None, "row"),
            P(None, None, "col"),
            P(None, "row"),
            P(None, "row"),
            P(None, "row"),
            P(None, "col"),
            P(None, "row"),
        ),
        check_vma=False,
    )
```

```python
import functools

import jax
import jax.numpy as jnp
from jax import lax
from jax.experimental import pallas as pl
from jax.experimental.pallas import tpu as pltpu
from jax.sharding import PartitionSpec as P

BF = jnp.bfloat16
F32 = jnp.float32
LAYERS = 2
GROUP = 8
TOK = 40
ROWS = (40,)
FIRST = (0,)
PARTS = (0,)
SEQ = 320
D = 1024
HALF = 512
HEAD_DIM = 64
EPS = 1e-6
ROOT_HALF = 0.7071067811865476
INV_ROOT_TAU = 0.3989422804014327
MESH = pl.DeviceIdType.MESH


def dot(a, b):
    return jnp.dot(a, b, preferred_element_type=F32)


def dot_last(a, b):
    return lax.dot_general(a, b, (((1,), (1,)), ((), ())), preferred_element_type=F32)


def dot_first(a, b):
    return lax.dot_general(a, b, (((0,), (0,)), ((), ())), preferred_element_type=F32)


def lanes(parts):
    return jnp.concatenate(parts, axis=1)


def kernel(
    images_h, gain1_h, bias1_h, wqkv, qvb_h, wout, outb_h, gain2_h, bias2_h, wup, upb_h, wdown, downb_h, cot_h,
    enc_h, gin_h, gqkv_h, gout_h, gup_h, gdown_h, gg1_h, gb1_h, gqv_h, gob_h, gg2_h, gb2_h, gub_h, gdb_h,
    images, gain1, bias1, qvb, outb, gain2, bias2, upb, downb, cot,
    enc_o, gin_o, gqkv_o, gout_o, gup_o, gdown_o, gg1_o, gb1_o, gqv_o, gob_o, gg2_o, gb2_o, gub_o, gdb_o,
    in_f, in_r, out_f, out_r,
    vec_s, vec_g, wq_g, wo_g, wu_g, wd_g,
    ag, rs_s, rs_b, rs_c, rs_r,
    gq_s, go_s, gu_s, gd_s, gq_r, go_r, gu_r, gd_r, gu_c, gu_f, gd_p, gd_q, gd_c, gd_f, sq, so, su, sd, tq, to, tu, td,
    stream, normal_k, scale_k, prob_k, qkv_k, mixed_k, hidden_k, slope_k, before_k, before_grad_k, grad_k,
    vacc, vcol, vs_s, vs_r, vh_r, vb_r, vt_s, vt_r,
    op_sem, res_sem, in_ss, in_rs, out_ss, out_rs, vec_sem, w_ss, w_rs, wf_ss, wf_rs,
    ag_ss, ag_rs, ag_fs, rs_bs, rs_br, rs_ss, rs_rs, g_ss, g_rs, gf_ss, gf_rs, x_ss, x_rs, v_ss, v_rs,
):
    core = lax.axis_index("dp")
    row = lax.axis_index("row")
    col = lax.axis_index("col")
    x = lax.div(col, 2)
    yh = lax.rem(col, 2)
    z = lax.div(row, 2)
    yl = lax.rem(row, 2)
    y = 2 * yh + yl
    t = 2 * x + core
    u = 4 * core + x
    sibling = (1 - core, row, col)

    def chip_dev(c):
        return (core, row, 2 * c + yh)

    def plane_dev(r):
        return (yh, r, 2 * x + core)

    def push(src, dst, ssem, rsem, dev):
        pltpu.make_async_remote_copy(
            src_ref=src, dst_ref=dst, send_sem=ssem, recv_sem=rsem, device_id=dev, device_id_type=MESH
        ).start()

    def drain(ref, sem):
        pltpu.make_async_copy(ref, ref, sem).wait()

    def fan(me, own, src, dst, ssem, rsem, dev):
        @pl.when(own)
        def _():
            pltpu.make_async_copy(src(me), dst, rsem).start()

        @pl.when(jnp.logical_not(own))
        def _():
            push(src(me), dst, ssem, rsem, dev(me))

        @pl.loop(1, GROUP)
        def _(k):
            j = lax.rem(me + k, GROUP)
            push(src(j), dst, ssem, rsem, dev(j))

    def fan_sent(own, ref, ssem):
        @pl.when(own)
        def _():
            drain(ref.at[pl.ds(0, GROUP - 1)], ssem)

        @pl.when(jnp.logical_not(own))
        def _():
            drain(ref, ssem)

    own_plane = yh == core
    own_tile = row == t
    place = 2 * col + core

    def tile_dev(j):
        return (lax.div(j, 4), t, 2 * lax.rem(j, 4) + yh)

    def back_dev(r):
        return (lax.rem(row, 2), r, 2 * lax.div(row, 2) + yh)

    def y_dev(k):
        other = lax.rem(y + k, 4)
        return (core, 2 * z + lax.rem(other, 2), 2 * x + lax.div(other, 2))

    def z_at(k):
        return lax.rem(z + k, 4)

    def z_dev(k):
        return (core, 2 * z_at(k) + yl, col)

    def row_dev(j):
        return (lax.rem(j, 2), row, lax.div(j, 2))

    barrier = pltpu.get_barrier_semaphore()

    def greet(me, own, dev):
        @pl.when(jnp.logical_not(own))
        def _():
            pl.semaphore_signal(barrier, inc=1, device_id=dev(me), device_id_type=MESH)

        @pl.loop(1, GROUP)
        def _(k):
            pl.semaphore_signal(barrier, inc=1, device_id=dev(lax.rem(me + k, GROUP)), device_id_type=MESH)

    greet(u, own_tile, tile_dev)
    greet(row, own_tile, back_dev)
    greet(row, own_plane, plane_dev)
    for k in (1, 2, 3):
        pl.semaphore_signal(barrier, inc=1, device_id=y_dev(k), device_id_type=MESH)
        pl.semaphore_signal(barrier, inc=1, device_id=z_dev(k), device_id_type=MESH)

    @pl.loop(1, 2 * GROUP)
    def _(k):
        pl.semaphore_signal(barrier, inc=1, device_id=row_dev(lax.rem(place + k, 2 * GROUP)), device_id_type=MESH)

    small = (
        (images_h, images), (gain1_h, gain1), (bias1_h, bias1), (outb_h, outb), (gain2_h, gain2), (bias2_h, bias2),
        (downb_h, downb), (qvb_h, qvb), (upb_h, upb), (cot_h, cot),
    )
    fetches = [pltpu.make_async_copy(src, dst, op_sem.at[n]) for n, (src, dst) in enumerate(small)]
    for fetch in fetches:
        fetch.start()

    def tiles_fold(n, ref):
        in_f[n, :, 0:TOK] = ref[...].astype(F32).reshape(GROUP, TOK, 128).astype(BF)

    def tiles_in(n):
        fan(u, own_tile, lambda j: in_f.at[n, j], in_r.at[n, row], in_ss.at[n], in_rs.at[n], tile_dev)

    def tiles_read(ref, n):
        whole = ref[n].astype(F32)
        return [whole[r, 0:TOK] for r in range(GROUP)]

    in_f[...] = jnp.zeros_like(in_f)
    out_f[...] = jnp.zeros_like(out_f)
    fetches[0].wait()
    tiles_fold(0, images)

    greeted = 3 * GROUP + 6 + 2 * GROUP - 1
    pl.semaphore_wait(barrier, greeted - jnp.where(own_plane, 1, 0) - jnp.where(own_tile, 2, 0))
    tiles_in(0)

    for fetch in fetches[1:9]:
        fetch.wait()
    vec_s[...] = jnp.zeros_like(vec_s)
    for l in range(LAYERS):
        for i, ref in enumerate((gain1, bias1, outb, gain2, bias2, downb)):
            vec_s[l, i : i + 1, :] = ref[l : l + 1, :]
        vec_s[2 + l, 0:2, :] = qvb[l]
        for j in range(4):
            vec_s[2 + l, 2 + j : 3 + j, :] = upb[l : l + 1, 128 * j : 128 * j + 128]
    fan(row, own_plane, lambda j: vec_s, vec_g.at[row], vec_sem.at[0], vec_sem.at[1], plane_dev)

    weights = ((wqkv, wq_g), (wout, wo_g), (wup, wu_g), (wdown, wd_g))

    def y_first(m):
        return m in (0, 3)

    def weight_slot(m, r):
        return r if y_first(m) else 4 * (r % 2) + r // 2

    def qkv_in(l):
        fan(row, own_plane, lambda j: wqkv.at[l], wq_g.at[l, row], w_ss.at[l, 0], w_rs.at[l, 0], plane_dev)

    def weights_in(l):
        @pl.when(own_plane)
        def _():
            for m in (1, 2, 3):
                src, dst = weights[m]
                block = dst.at[l, row if y_first(m) else 4 * yl + z]
                pltpu.make_async_copy(src.at[l], block, w_rs.at[l, m]).start()
                for k in (2, 1, 3):
                    push(src.at[l], block, w_ss.at[l, m], w_rs.at[l, m], (y_dev if y_first(m) else z_dev)(k))

    def weights_relay(l, m):
        dst = weights[m][1]
        if m == 3:
            pair = dst.at[l, pl.ds(2 * z, 2)]
            drain(pair, w_rs.at[l, m])
            for k in (2, 1, 3):
                push(pair, pair, wf_ss.at[l, m], wf_rs.at[l, m], z_dev(k))
        else:

            @pl.when(own_plane)
            def _():
                four = dst.at[l, pl.ds(4 * yl, 4)]
                drain(four, w_rs.at[l, m])
                for k in (2, 1, 3):
                    push(four, four, wf_ss.at[l, m], wf_rs.at[l, m], y_dev(k))

    def weight_wait(l, m):
        dst = weights[m][1]
        if m == 0:
            drain(dst.at[l], w_rs.at[l, m])
        elif m == 3:
            drain(dst.at[l, pl.ds(0, 6)], wf_rs.at[l, m])
        else:

            @pl.when(own_plane)
            def _():
                drain(dst.at[l, pl.ds(0, 4)], wf_rs.at[l, m])

            @pl.when(jnp.logical_not(own_plane))
            def _():
                drain(dst.at[l], wf_rs.at[l, m])

    def weights_sent(l, m):
        dst = weights[m][1]
        if m == 0:
            fan_sent(own_plane, dst.at[l], w_ss.at[l, m])
            return

        @pl.when(own_plane)
        def _():
            drain(dst.at[l, pl.ds(0, 3)], w_ss.at[l, m])

        if m == 3:
            drain(dst.at[l, pl.ds(0, 6)], wf_ss.at[l, m])
        else:

            @pl.when(own_plane)
            def _():
                drain(dst.at[:, pl.ds(0, 6)], wf_ss.at[l, m])

    weights_in(0)
    qkv_in(0)

    def chip_at(k):
        return lax.rem(x + k, 4)

    def own_rows(p):
        return slice(FIRST[p], FIRST[p] + ROWS[p])

    def all_rows(p):
        return slice(GROUP * FIRST[p], GROUP * (FIRST[p] + ROWS[p]))

    def gather_start(l, s, p, value):
        folded = jnp.concatenate([value[:, :HALF], value[:, HALF:]], axis=0).astype(BF)
        ag[p][l, s, core, x] = folded
        mine = ag[p].at[l, s, core, x]
        for k in (2, 1, 3):
            push(mine, mine, ag_ss.at[l, s, p], ag_rs.at[l, s, p, k], chip_dev(chip_at(k)))
        push(mine, mine, ag_fs.at[l, s, p], ag_rs.at[l, s, p, 0], sibling)

    def gather_wait(l, s, p):
        for k in (1, 3, 2):
            came = ag[p].at[l, s, core, chip_at(4 - k)]
            drain(came, ag_rs.at[l, s, p, k])
            push(came, came, ag_fs.at[l, s, p], ag_rs.at[l, s, p, 0], sibling)
        drain(ag[p].at[l, s, 0], ag_rs.at[l, s, p, 0])

    def gather_read(l, s, p):
        rows = ROWS[p]
        whole = ag[p][l, s].astype(F32).reshape(GROUP, 2 * rows, HALF)
        left = whole[:, :rows].reshape(GROUP * rows, HALF).astype(BF)
        right = whole[:, rows:].reshape(GROUP * rows, HALF).astype(BF)
        return left, right

    def gather_whole(l, s):
        parts = [gather_read(l, s, p) for p in PARTS]
        return [jnp.concatenate([part[h] for part in parts], axis=0) for h in range(2)]

    def scatter_start(l, s, p, left, right):
        rows = ROWS[p]
        both = jnp.concatenate([left.reshape(GROUP, rows, HALF), right.reshape(GROUP, rows, HALF)], axis=1)
        rs_s[p][l, s] = both.astype(BF).reshape(2, 4, 2 * rows, HALF)
        for k in (2, 1, 3, 0):
            c = chip_at(k)
            push(rs_s[p].at[l, s, 1 - core, c], rs_b[p].at[l, s, c], rs_bs.at[l, s, p], rs_br.at[l, s, p, k], sibling)

    def pair_sum(l, s, p, k):
        c = chip_at(k)
        drain(rs_b[p].at[l, s, c], rs_br.at[l, s, p, k])
        return rs_s[p][l, s, core, c].astype(F32) + rs_b[p][l, s, c].astype(F32)

    def scatter_relay(l, s, p):
        for k in (2, 1, 3):
            rs_c[p][l, s, k] = pair_sum(l, s, p, k).astype(BF)
            push(rs_c[p].at[l, s, k], rs_r[p].at[l, s, k], rs_ss.at[l, s, p], rs_rs.at[l, s, p, k], chip_dev(chip_at(k)))

    def scatter_wait(l, s, p):
        rows = ROWS[p]
        total = pair_sum(l, s, p, 0)
        for k in (1, 3, 2):
            drain(rs_r[p].at[l, s, k], rs_rs.at[l, s, p, k])
            total += rs_r[p][l, s, k].astype(F32)
        return lanes([total[:rows], total[rows:]])

    def vec_row(l, i):
        return lanes([vec_g[r, l, i : i + 1, :] for r in range(GROUP)])

    def norm_forward(l, s, p, value):
        center = jnp.mean(value, axis=1, keepdims=True)
        shifted = value - center
        scaled = lax.rsqrt(jnp.mean(shifted * shifted, axis=1, keepdims=True) + EPS)
        normal = shifted * scaled
        normal_k[l, s, own_rows(p)] = normal
        scale_k[l, s, own_rows(p)] = jnp.broadcast_to(scaled, (ROWS[p], 128))
        return normal * vec_row(l, 3 * s) + vec_row(l, 3 * s + 1)

    def add_row(l, i, value):
        vacc[l, i : i + 1, :] += jnp.sum(value, axis=0, keepdims=True)

    def norm_backward(l, s, p, grad_out):
        normal = normal_k[l, s, own_rows(p)]
        scaled = scale_k[l, s, own_rows(p)][:, 0:1]
        add_row(l, 3 * s, grad_out * normal)
        add_row(l, 3 * s + 1, grad_out)
        upstream = grad_out * vec_row(l, 3 * s)
        mean_part = jnp.mean(upstream, axis=1, keepdims=True)
        proj_part = jnp.mean(upstream * normal, axis=1, keepdims=True)
        return scaled * (upstream - mean_part - normal * proj_part)

    def qkv_half(l, h):
        return jnp.concatenate([lanes([wq_g[l, weight_slot(0, 4 * h + r), j] for j in range(3)]) for r in range(4)], axis=0)

    def out_half(l, h):
        return lanes([wo_g[l, weight_slot(1, 4 * h + r)] for r in range(4)])

    def up_half(l, h):
        return jnp.concatenate([wu_g[l, weight_slot(2, 4 * h + r)] for r in range(4)], axis=0)

    def down_half(l, h):
        return lanes([wd_g[l, weight_slot(3, 4 * h + r)] for r in range(4)])

    def head_mask(h):
        lane = lax.broadcasted_iota(jnp.int32, (SEQ, 128), 1)
        return (lane < HEAD_DIM) if h == 0 else (lane >= HEAD_DIM)

    def pick(pair):
        return jnp.where(head_mask(0), pair[0], pair[1])

    def only(h, value):
        return jnp.where(head_mask(h), value, jnp.zeros_like(value))

    drain(in_r.at[0], in_rs.at[0])
    stream[...] = lanes(tiles_read(in_r, 0))
    drain(vec_g, vec_sem.at[1])
    for p in PARTS:
        gather_start(0, 0, p, norm_forward(0, 0, p, stream[own_rows(p)]))
    for m in (1, 2, 3):
        weights_relay(0, m)
    fetches[9].wait()
    tiles_fold(1, cot)
    tiles_in(1)

    def hidden_part(l, p):
        left, right = gather_read(l, 1, p)
        before = dot(left, up_half(l, 0)) + dot(right, up_half(l, 1))
        shift = vec_g[0, 2 + l]
        before = before + lanes([shift[2 + j : 3 + j] for j in range(4)])
        phi = 0.5 * (1.0 + lax.erf(before * ROOT_HALF))
        hidden = (before * phi).astype(BF)
        hidden_k[l, all_rows(p)] = hidden
        before_k[all_rows(p)] = before
        slope_k[l, all_rows(p)] = phi
        if p == 0:
            weight_wait(l, 3)
        scatter_start(l, 1, p, dot(hidden, down_half(l, 0)), dot(hidden, down_half(l, 1)))

    @pl.loop(0, LAYERS)
    def _(l):
        for p in PARTS:
            gather_wait(l, 0, p)
            left, right = gather_read(l, 0, p)
            if p == 0:
                weight_wait(l, 0)
            projected = dot(left, qkv_half(l, 0)) + dot(right, qkv_half(l, 1))
            shift = vec_g[0, 2 + l]
            qkv_k[l, 0, all_rows(p)] = (projected[:, :128] + shift[0:1]).astype(BF)
            qkv_k[l, 1, all_rows(p)] = projected[:, 128:256].astype(BF)
            qkv_k[l, 2, all_rows(p)] = (projected[:, 256:] + shift[1:2]).astype(BF)
        query = qkv_k[l, 0]
        keys = qkv_k[l, 1]
        values = qkv_k[l, 2]
        mixed = []
        for h in range(2):
            scores = dot_last(only(h, query), keys) * HEAD_DIM ** -0.5
            raised = jnp.exp(scores - jnp.max(scores, axis=1, keepdims=True))
            probs = raised / jnp.sum(raised, axis=1, keepdims=True)
            prob_k[l, h] = probs
            mixed.append(dot(probs.astype(BF), values))
        mixed = pick(mixed).astype(BF)
        mixed_k[l] = mixed
        weight_wait(l, 1)
        for p in PARTS:
            part = mixed[all_rows(p)]
            scatter_start(l, 0, p, dot(part, out_half(l, 0)), dot(part, out_half(l, 1)))
        for p in PARTS:
            scatter_relay(l, 0, p)
        @pl.when(l == 0)
        def _():
            weights_in(1)
            qkv_in(1)

        for p in PARTS:
            middle = stream[own_rows(p)] + vec_row(l, 2) + scatter_wait(l, 0, p)
            stream[own_rows(p)] = middle
            gather_start(l, 1, p, norm_forward(l, 1, p, middle))
        for p in PARTS:
            gather_wait(l, 1, p)
            if p == 0:
                weight_wait(l, 2)
            else:
                scatter_relay(l, 1, p - 1)
            hidden_part(l, p)
        scatter_relay(l, 1, PARTS[-1])

        @pl.when(l == 0)
        def _():
            for m in (1, 2, 3):
                weights_relay(1, m)
            drain(in_r.at[1], in_rs.at[1])
            grad_k[...] = lanes(tiles_read(in_r, 1))
            for p in PARTS:
                gather_start(LAYERS - 1, 2, p, grad_k[own_rows(p)])

        before = before_k[...]
        slope_k[l] = slope_k[l] + before * INV_ROOT_TAU * jnp.exp(-0.5 * before * before)

        @pl.when(l == 0)
        def _():
            for p in PARTS:
                value = stream[own_rows(p)] + vec_row(0, 5) + scatter_wait(0, 1, p)
                stream[own_rows(p)] = value
                gather_start(1, 0, p, norm_forward(1, 0, p, value))

    def tiles_out(n, value):
        for r in range(GROUP):
            out_f[n, r, 0:TOK] = value[:, 128 * r : 128 * r + 128].astype(BF)
        fan(row, own_tile, lambda j: out_f.at[n, j], out_r.at[n, u], out_ss.at[n], out_rs.at[n], back_dev)

    vacc[...] = jnp.zeros_like(vacc)
    vcol[...] = jnp.zeros_like(vcol)

    grads = (
        (gq_s, gq_r, sq, tq, gqkv_o, gqkv_h), (go_s, go_r, so, to, gout_o, gout_h),
        (gu_s, gu_r, su, tu, gup_o, gup_h), (gd_s, gd_r, sd, td, gdown_o, gdown_h),
    )

    def grad_slot(m, r):
        return 4 * (r % 2) + r // 2 if m == 3 else r

    def pair_fan(src, dst, ssem, rsem):
        def dev(j):
            return plane_dev(2 * z + j)

        @pl.when(own_plane)
        def _():
            pltpu.make_async_copy(src(yl), dst, rsem).start()

        @pl.when(jnp.logical_not(own_plane))
        def _():
            push(src(yl), dst, ssem, rsem, dev(yl))

        push(src(1 - yl), dst, ssem, rsem, dev(1 - yl))

    def grads_out(l, m):
        src, dst = grads[m][:2]
        if m == 2:
            for k in (2, 1, 3):
                push(src.at[l, pl.ds(2 * z_at(k), 2)], dst.at[l, k], g_ss.at[l, m], g_rs.at[l, m], z_dev(k))
        elif m == 3:
            pair_fan(lambda j: src.at[l, pl.ds(4 * j, 4)], dst.at[l, yl], g_ss.at[l, m], g_rs.at[l, m])
        else:
            fan(row, own_plane, lambda j: src.at[l, j], dst.at[l, row], g_ss.at[l, m], g_rs.at[l, m], plane_dev)

    def up_relay(l):
        drain(gu_r.at[l, pl.ds(1, 3)], g_rs.at[l, 2])
        for j in range(2):
            total = gu_s[l, 2 * z + j].astype(F32)
            for k in (1, 2, 3):
                total += gu_r[l, k, j].astype(F32)
            gu_c[l, j] = total.astype(BF)
        pair_fan(lambda j: gu_c.at[l, j], gu_f.at[l, yl], gf_ss.at[l, 0], gf_rs.at[l, 0])

    keeper = lax.div(z, 2) == core

    def down_pair(l):
        drain(gd_r.at[l], g_rs.at[l, 3])
        for j in range(2):
            theirs = 2 * (1 - core) + j
            gd_p[l, j] = (gd_r[l, 0, theirs].astype(F32) + gd_r[l, 1, theirs].astype(F32)).astype(BF)
        push(gd_p.at[l], gd_q.at[l], gf_ss.at[l, 2], gf_rs.at[l, 2], sibling)

    def down_relay(l):
        drain(gd_q.at[l], gf_rs.at[l, 2])
        for j in range(2):
            ours = 2 * core + j
            total = gd_r[l, 0, ours].astype(F32) + gd_r[l, 1, ours].astype(F32) + gd_q[l, j].astype(F32)
            gd_c[l, j] = total.astype(BF)

            @pl.when(ours != z)
            def _():
                push(gd_c.at[l, j], gd_f.at[l, z], gf_ss.at[l, 1], gf_rs.at[l, 1], (core, 2 * ours + yl, col))

        @pl.when(keeper)
        def _():
            gd_f[l, z] = gd_c[l, lax.rem(z, 2)]

    def pair_sent(ref, ssem):
        @pl.when(own_plane)
        def _():
            drain(ref.at[0], ssem)

        @pl.when(jnp.logical_not(own_plane))
        def _():
            drain(ref, ssem)

    def grads_sent(l, m):
        src, dst = grads[m][:2]
        if m == 2:
            drain(dst.at[l, pl.ds(1, 3)], g_ss.at[l, m])
            pair_sent(gu_c.at[l], gf_ss.at[l, 0])
        elif m == 3:
            pair_sent(dst.at[l], g_ss.at[l, m])
            drain(gd_q.at[l], gf_ss.at[l, 2])

            @pl.when(keeper)
            def _():
                drain(gd_c.at[l, 0], gf_ss.at[l, 1])

            @pl.when(jnp.logical_not(keeper))
            def _():
                drain(gd_c.at[l], gf_ss.at[l, 1])
        else:
            fan_sent(own_plane, src.at[l], g_ss.at[l, m])

    def sum_terms(l, m):
        src, dst, part, other = grads[m][:4]
        if m == 2:
            drain(gu_f.at[l], gf_rs.at[l, 0])
            total = gu_f[l, 0].astype(F32) + gu_f[l, 1].astype(F32)
        elif m == 3:

            @pl.when(keeper)
            def _():
                drain(gd_f.at[l, pl.ds(0, 3)], gf_rs.at[l, 1])
                part[l] = jnp.sum(gd_f[l].astype(F32), axis=0)
                push(part.at[l], other.at[l], x_ss.at[l, m], x_rs.at[l, m], sibling)

            return
        elif m == 0:
            for j in (2, 0, 1):
                drain(dst.at[l, :, j], g_rs.at[l, 4 + j])
                total = dst[l, 0, j].astype(F32)
                for r in range(1, GROUP):
                    total += dst[l, r, j].astype(F32)
                part[l, j] = total
                push(part.at[l, j], other.at[l, j], x_ss.at[l, m], x_rs.at[l, m], sibling)
            return
        else:
            drain(dst.at[l], g_rs.at[l, m])
            total = dst[l, 0].astype(F32)
            for r in range(1, GROUP):
                total += dst[l, r].astype(F32)
        part[l] = total
        push(part.at[l], other.at[l], x_ss.at[l, m], x_rs.at[l, m], sibling)

    def hidden_back(l, p):
        left, right = gather_read(l, 2, p)
        hidden_grad = dot_last(left, down_half(l, 0)) + dot_last(right, down_half(l, 1))
        before_grad = (hidden_grad * slope_k[l, all_rows(p)]).astype(BF)
        before_grad_k[all_rows(p)] = before_grad
        scatter_start(l, 2, p, dot_last(before_grad, up_half(l, 0)), dot_last(before_grad, up_half(l, 1)))

    @pl.loop(0, LAYERS)
    def _(step):
        l = LAYERS - 1 - step
        add_row(l, 5, grad_k[...].astype(BF).astype(F32))
        for p in PARTS:
            gather_wait(l, 2, p)
            if p > 0:
                scatter_relay(l, 2, p - 1)
            hidden_back(l, p)
        scatter_relay(l, 2, PARTS[-1])
        before_grad = before_grad_k[...]
        for h, part in enumerate(gather_whole(l, 2)):
            product = dot_first(hidden_k[l], part).astype(BF)
            for r in range(4):
                gd_s[l, grad_slot(3, 4 * h + r)] = product[:, 128 * r : 128 * r + 128]
        grads_out(l, 3)
        for h, part in enumerate(gather_whole(l, 1)):
            gu_s[l, 4 * h : 4 * h + 4] = dot_first(part, before_grad).astype(BF).reshape(4, 128, 512)
        grads_out(l, 2)
        for p in PARTS:
            grad_mid = grad_k[own_rows(p)] + norm_backward(l, 1, p, scatter_wait(l, 2, p))
            grad_k[own_rows(p)] = grad_mid
            gather_start(l, 3, p, grad_mid)
        sums = jnp.sum(before_grad.astype(F32), axis=0, keepdims=True)
        for j in range(4):
            vcol[l, 2 + j : 3 + j, :] = sums[:, 128 * j : 128 * j + 128]
        add_row(l, 2, grad_k[...].astype(BF).astype(F32))

        @pl.when(step == 0)
        def _():
            for p in PARTS:
                stream[own_rows(p)] = stream[own_rows(p)] + vec_row(LAYERS - 1, 5) + scatter_wait(LAYERS - 1, 1, p)
            tiles_out(0, stream[...])

        mixed_grad = []
        for p in PARTS:
            gather_wait(l, 3, p)
            left, right = gather_read(l, 3, p)
            mixed_grad.append((dot_last(left, out_half(l, 0)) + dot_last(right, out_half(l, 1))).astype(BF))
        mixed_grad = jnp.concatenate(mixed_grad, axis=0)
        query = qkv_k[l, 0]
        keys = qkv_k[l, 1]
        values = qkv_k[l, 2]

        def out_terms():
            for h, part in enumerate(gather_whole(l, 3)):
                product = dot_first(mixed_k[l], part).astype(BF)
                for r in range(4):
                    go_s[l, 4 * h + r] = product[:, 128 * r : 128 * r + 128]
            grads_out(l, 1)

        def qkv_term(j, value):
            for h, part in enumerate(gather_whole(l, 0)):
                product = dot_first(part, value).astype(BF)
                for r in range(4):
                    gq_s[l, 4 * h + r, j] = product[128 * r : 128 * r + 128]
            fan(
                row, own_plane, lambda r: gq_s.at[l, r, j], gq_r.at[l, row, j], g_ss.at[l, 0], g_rs.at[l, 4 + j], plane_dev
            )

        values_grad = pick([dot_first(prob_k[l, h].astype(BF), mixed_grad) for h in range(2)]).astype(BF)

        @pl.when(l == 0)
        def _():
            out_terms()
            qkv_term(2, values_grad)

        query_grads, key_grads = [], []
        for h in range(2):
            probs = prob_k[l, h]
            probs_grad = dot_last(only(h, mixed_grad), values)
            inner = jnp.sum(probs * probs_grad, axis=1, keepdims=True)
            scores_grad = (probs * (probs_grad - inner)).astype(BF)
            query_grads.append(dot(scores_grad, keys))
            key_grads.append(dot_first(scores_grad, query))
        query_grad = (pick(query_grads) * HEAD_DIM ** -0.5).astype(BF)
        keys_grad = (pick(key_grads) * HEAD_DIM ** -0.5).astype(BF)

        @pl.when(l == 0)
        def _():
            qkv_term(0, query_grad)
            qkv_term(1, keys_grad)

        joined = lanes([query_grad, keys_grad, values_grad])
        for p in PARTS:
            part = joined[all_rows(p)]
            scatter_start(l, 3, p, dot_last(part, qkv_half(l, 0)), dot_last(part, qkv_half(l, 1)))
        for p in PARTS:
            scatter_relay(l, 3, p)
        down_pair(l)
        up_relay(l)
        down_relay(l)

        @pl.when(l != 0)
        def _():
            qkv_term(0, query_grad)
            qkv_term(1, keys_grad)
            qkv_term(2, values_grad)
            out_terms()

        vcol[l, 0:1, :] = jnp.sum(query_grad.astype(F32), axis=0, keepdims=True)
        vcol[l, 1:2, :] = jnp.sum(values_grad.astype(F32), axis=0, keepdims=True)

        @pl.when(l == 0)
        def _():
            fan(row, own_plane, lambda j: vcol, vb_r.at[row], v_ss.at[1], v_rs.at[1], plane_dev)
            for m in (3, 2, 0, 1):
                sum_terms(1, m)

        for p in PARTS:
            grad_k[own_rows(p)] = grad_k[own_rows(p)] + norm_backward(l, 0, p, scatter_wait(l, 3, p))

            @pl.when(l > 0)
            def _():
                gather_start(l - 1, 2, p, grad_k[own_rows(p)])

    tiles_out(1, grad_k[...])

    for j in range(GROUP):
        vs_s[j] = vacc[:, :, 128 * j : 128 * j + 128]
    fan(row, own_plane, lambda j: vs_s.at[j], vs_r.at[row], v_ss.at[0], v_rs.at[0], plane_dev)

    results = []

    def result(src, dst):
        copy = pltpu.make_async_copy(src, dst, res_sem.at[len(results)])
        copy.start()
        results.append(copy)

    drain(out_r.at[0], out_rs.at[0])
    enc_o[...] = out_r[0].astype(F32)[:, 0:TOK].reshape(SEQ, 128).astype(BF)
    result(enc_o, enc_h)

    drain(vb_r, v_rs.at[1])
    vt_s[...] = jnp.sum(vb_r[...], axis=0)
    push(vt_s, vt_r, v_ss.at[2], v_rs.at[2], sibling)

    for m in (3, 2):
        sum_terms(0, m)

    drain(vs_r, v_rs.at[0])
    vh_r[place] = jnp.sum(vs_r[...], axis=0)

    @pl.loop(1, 2 * GROUP)
    def _(k):
        push(vh_r.at[place], vh_r.at[place], v_ss.at[3], v_rs.at[3], row_dev(lax.rem(place + k, 2 * GROUP)))

    for m in (1, 0):
        sum_terms(0, m)

    drain(vt_r, v_rs.at[2])
    columns = vt_s[...] + vt_r[...]
    for l in range(LAYERS):
        gqv_o[l] = columns[l, 0:2]
        for j in range(4):
            gub_o[l : l + 1, 128 * j : 128 * j + 128] = columns[l, 2 + j : 3 + j]
    result(gqv_o, gqv_h)
    result(gub_o, gub_h)

    drain(out_r.at[1], out_rs.at[1])
    gin_o[...] = out_r[1].astype(F32)[:, 0:TOK].reshape(SEQ, 128)
    result(gin_o, gin_h)

    for m in (3, 2, 1, 0):
        part, other, out, out_hbm = grads[m][2:]
        for l in (1, 0):
            if m == 3:

                @pl.when(keeper)
                def _():
                    out[l] = part[l]

                @pl.when(jnp.logical_not(keeper))
                def _():
                    drain(other.at[l], x_rs.at[l, m])
                    out[l] = other[l]
            else:
                drain(other.at[l], x_rs.at[l, m])
                out[l] = part[l] + other[l]
        result(out, out_hbm)

    drain(vh_r.at[pl.ds(0, 2 * GROUP - 1)], v_rs.at[3])
    rows = jnp.sum(vh_r[...], axis=0)
    for i, (ref, out_hbm) in enumerate(
        ((gg1_o, gg1_h), (gb1_o, gb1_h), (gob_o, gob_h), (gg2_o, gg2_h), (gb2_o, gb2_h), (gdb_o, gdb_h))
    ):
        for l in range(LAYERS):
            ref[l : l + 1, :] = rows[l, i : i + 1, :]
        result(ref, out_hbm)

    for n in range(2):
        fan_sent(own_tile, in_f.at[n], in_ss.at[n])
        fan_sent(own_tile, out_f.at[n], out_ss.at[n])
    fan_sent(own_plane, vec_g, vec_sem.at[0])
    fan_sent(own_plane, vb_r, v_ss.at[1])
    fan_sent(own_plane, vs_s, v_ss.at[0])
    drain(vt_s, v_ss.at[2])
    drain(vh_r.at[pl.ds(0, 2 * GROUP - 1)], v_ss.at[3])

    @pl.loop(0, LAYERS)
    def _(l):
        for m in range(4):
            weights_sent(l, m)
            grads_sent(l, m)
            if m == 3:

                @pl.when(keeper)
                def _():
                    drain(grads[m][2].at[l], x_ss.at[l, m])
            else:
                drain(grads[m][2].at[l], x_ss.at[l, m])
        for s in range(4):
            for p in PARTS:
                drain(ag[p].at[l, s, 0, pl.ds(0, 3)], ag_ss.at[l, s, p])
                drain(ag[p].at[l, s, 0], ag_fs.at[l, s, p])
                drain(rs_b[p].at[l, s], rs_bs.at[l, s, p])
                drain(rs_c[p].at[l, s, pl.ds(1, 3)], rs_ss.at[l, s, p])

    for copy in results:
        copy.wait()


def finish(*refs):
    count = (len(refs) - 2) // 3
    ins, outs, held = refs[:count], refs[count : 2 * count], refs[2 * count : 3 * count]
    in_sem, out_sem = refs[3 * count :]
    loads = [pltpu.make_async_copy(ins[n], held[n], in_sem.at[n]) for n in range(count)]
    stores = [pltpu.make_async_copy(held[n], outs[n], out_sem.at[n]) for n in range(count)]
    for copy in loads:
        copy.start()
    for load, store in zip(loads, stores):
        load.wait()
        store.start()
    for copy in stores:
        copy.wait()


def on_device(images, gain1, bias1, wqkv, qvb, wout, outb, gain2, bias2, wup, upb, wdown, downb, cot):
    L = LAYERS
    N = len(PARTS)
    wqkv = wqkv.transpose(0, 2, 1, 3)
    hbm = pl.BlockSpec(memory_space=pl.ANY)
    shape = jax.ShapeDtypeStruct
    dma = pltpu.SemaphoreType.DMA
    V = pltpu.VMEM
    out_shape = (
        shape((SEQ, 128), BF),
        shape((SEQ, 128), F32),
        shape((L, 3, 128, 128), F32),
        shape((L, 128, 128), F32),
        shape((L, 128, 512), F32),
        shape((L, 512, 128), F32),
        shape((L, 128), F32),
        shape((L, 128), F32),
        shape((L, 2, 128), F32),
        shape((L, 128), F32),
        shape((L, 128), F32),
        shape((L, 128), F32),
        shape((L, 512), F32),
        shape((L, 128), F32),
    )
    operands = (images, gain1, bias1, wqkv, qvb, wout, outb, gain2, bias2, wup, upb, wdown, downb, cot)
    staged = [V(a.shape, a.dtype) for a in (images, gain1, bias1, qvb, outb, gain2, bias2, upb, downb, cot)]
    results = pl.pallas_call(
        kernel,
        out_shape=out_shape,
        in_specs=[hbm] * 14,
        out_specs=(hbm,) * 14,
        scratch_shapes=staged + [V(a.shape, a.dtype) for a in out_shape] + [
            V((2, 8, 48, 128), BF), V((2, 8, 48, 128), BF), V((2, 8, 48, 128), BF), V((2, 8, 48, 128), BF),
            V((4, 8, 128), F32), V((8, 4, 8, 128), F32),
            V((L, 8, 3, 128, 128), BF), V((L, 8, 128, 128), BF), V((L, 8, 128, 512), BF), V((L, 8, 512, 128), BF),
            *[tuple(V((L, 4, 2, 4, 2 * rows, HALF), BF) for rows in ROWS) for _ in range(2)],
            *[tuple(V((L, 4, 4, 2 * rows, HALF), BF) for rows in ROWS) for _ in range(3)],
            V((L, 8, 3, 128, 128), BF), V((L, 8, 128, 128), BF), V((L, 8, 128, 512), BF), V((L, 8, 512, 128), BF),
            V((L, 8, 3, 128, 128), BF), V((L, 8, 128, 128), BF), V((L, 4, 2, 128, 512), BF), V((L, 2, 4, 512, 128), BF),
            V((L, 2, 128, 512), BF), V((L, 2, 128, 512), BF), V((L, 2, 512, 128), BF), V((L, 2, 512, 128), BF),
            V((L, 2, 512, 128), BF), V((L, 4, 512, 128), BF),
            V((L, 3, 128, 128), F32), V((L, 128, 128), F32), V((L, 128, 512), F32), V((L, 512, 128), F32),
            V((L, 3, 128, 128), F32), V((L, 128, 128), F32), V((L, 128, 512), F32), V((L, 512, 128), F32),
            V((TOK, D), F32), V((L, 2, TOK, D), F32), V((L, 2, TOK, 128), F32), V((L, 2, SEQ, SEQ), F32),
            V((L, 3, SEQ, 128), BF), V((L, SEQ, 128), BF), V((L, SEQ, 512), BF), V((L, SEQ, 512), F32),
            V((SEQ, 512), F32), V((SEQ, 512), BF), V((TOK, D), F32),
            V((L, 8, D), F32), V((L, 8, 128), F32),
            V((8, L, 8, 128), F32), V((8, L, 8, 128), F32), V((16, L, 8, 128), F32),
            V((8, L, 8, 128), F32), V((L, 8, 128), F32), V((L, 8, 128), F32),
            dma((10,)), dma((14,)), dma((2,)), dma((2,)), dma((2,)), dma((2,)), dma((2,)), dma((L, 4)), dma((L, 4)), dma((L, 4)), dma((L, 4)),
            dma((L, 4, N)), dma((L, 4, N, 4)), dma((L, 4, N)), dma((L, 4, N)), dma((L, 4, N, 4)), dma((L, 4, N)),
            dma((L, 4, N, 4)),
            dma((L, 4)), dma((L, 7)), dma((L, 3)), dma((L, 3)), dma((L, 4)), dma((L, 4)), dma((4,)), dma((4,)),
        ],
        compiler_params=pltpu.CompilerParams(collective_id=0, has_side_effects=True, vmem_limit_bytes=60 * 1024 * 1024),
        cost_estimate=pl.CostEstimate(flops=6 * 10**9, bytes_accessed=5 * 10**6, transcendentals=10**6),
    )(*operands)
    results = pl.pallas_call(
        finish,
        out_shape=out_shape,
        in_specs=[hbm] * 14,
        out_specs=(hbm,) * 14,
        scratch_shapes=[V(a.shape, a.dtype) for a in out_shape] + [dma((14,)), dma((14,))],
    )(*results)
    results = list(results)
    results[2] = results[2].transpose(0, 2, 1, 3)
    return tuple(results)


def solution(mesh):
    return jax.shard_map(
        on_device,
        mesh=mesh,
        in_specs=(
            P(("dp", "col"), "row"),
            P(None, "row"),
            P(None, "row"),
            P(None, "row", None, "col"),
            P(None, None, "col"),
            P(None, "col", "row"),
            P(None, "row"),
            P(None, "row"),
            P(None, "row"),
            P(None, "row", "col"),
            P(None, "col"),
            P(None, "col", "row"),
            P(None, "row"),
            P(("dp", "col"), "row"),
        ),
        out_specs=(
            P(("dp", "col"), "row"),
            P(("dp", "col"), "row"),
            P(None, "row", None, "col"),
            P(None, "col", "row"),
            P(None, "row", "col"),
            P(None, "col", "row"),
            P(None, "row"),
            P(None, "row"),
            P(None, None, "col"),
            P(None, "row"),
            P(None, "row"),
            P(None, "row"),
            P(None, "col"),
            P(None, "row"),
        ),
        check_vma=False,
    )
```
